512 devices in a mesh: row: 16 (over z_lo, y), col: 32 (over x, z_hi, core).
Axes of the slice: x: 4, y: 4, z: 16 (z_hi: 4, z_lo: 4; z = z_hi * 4 + z_lo), core: 2. Of those that a mesh axis runs over, the one named last changes fastest.
Arguments:
- inputs: bfloat16 [256, 98304], P('row', 'col'), may hold values from -6 to 6
- first_weight: bfloat16 [9, 36864], replicated, may hold values from -0.15625 to 0.15625
- second_weight: bfloat16 [9, 36864], replicated, may hold values from -0.15625 to 0.15625
- cotangent: bfloat16 [256, 98304], P('row', 'col'), may hold values from -6 to 6
Outputs:
- output_field_grid: bfloat16 [256, 98304], P('row', 'col')
- input_grad: bfloat16 [256, 98304], P('row', 'col')
- first_weight_gradient: bfloat16 [9, 36864], replicated
- second_weight_gradient: bfloat16 [9, 36864], replicated
The draws below stay inside these ranges and needn't reach their ends.
All inputs are finite; a program needn't handle non-finite values.
Results may differ from the reference program's by a relative error of at most 0.015.
Values may be sent and summed in bfloat16 or wider, within the bound.
No kernel may reach another device: no remote copies, remote signals or barrier semaphores. Data moves between devices by JAX's collectives and lax.ppermute only.
A program may use at most 64 MiB of HBM per device.

```python
import jax
import jax.numpy as jnp
from jax import lax

C = 192
H = 256
W = 512
DILATION_FIRST = 32
DILATION_SECOND = 64


def shard_levels(key, extent, shards, least, high):
    def one(position, shards_of):
        heights = jax.random.uniform(jax.random.fold_in(jax.random.fold_in(key, 6), position), (shards_of,), jnp.float32, least / len(shards), high / len(shards))
        return jnp.repeat(jnp.exp(heights), extent[position] // shards_of).reshape((-1,) + (1,) * (len(extent) - position - 1))

    factor_of = one(*shards[0])
    for cut in shards[1:]:
        factor_of = factor_of * one(*cut)
    return factor_of


def noise(rng, dims, spread, bound, cuts=(), held_as=jnp.bfloat16):
    drawn = spread * jax.random.normal(rng, dims, jnp.float32)
    if cuts:
        drawn = drawn * shard_levels(rng, dims, cuts, -0.22, 0.18)
    return jnp.clip(drawn, -bound, bound).astype(held_as)


def setup_inputs(seed: int = 0) -> dict:
    arg_keys = jax.random.split(jax.random.key(seed), 5)
    return {
        "inputs": noise(arg_keys[0], (H, W * C), 1.0, 6.0, ((0, 16), (1, 32))),
        "first_weight": noise(arg_keys[1], (9, C * C), (9 * C) ** -0.5, 0.15625),
        "second_weight": noise(arg_keys[2], (9, C * C), (9 * C) ** -0.5, 0.15625),
        "cotangent": noise(arg_keys[3], (H, W * C), 1.0, 6.0, ((0, 16), (1, 32))),
    }


def gelu_parts(value):
    normal_cdf = 0.5 * (1.0 + lax.erf(value * 0.7071067811865476))
    density = jnp.exp(-0.5 * value * value) * 0.3989422804014327
    return value * normal_cdf, normal_cdf + value * density


def shifted(field, row_off, col_off):
    reach = max(abs(row_off), abs(col_off))
    grid_rows, grid_cols = field.shape[0], field.shape[1]
    padded = jnp.pad(field, ((reach, reach), (reach, reach), (0, 0)))
    return padded[reach + row_off:reach + row_off + grid_rows, reach + col_off:reach + col_off + grid_cols]


def apply_convolution(field, kernel, dilation, direction, transpose_kernel):
    channels = field.shape[2]
    total = jnp.zeros((field.shape[0] * field.shape[1], channels), jnp.float32)
    tap_index = 0
    for row_off in (-1, 0, 1):
        for col_off in (-1, 0, 1):
            moved = shifted(field, direction * row_off * dilation, direction * col_off * dilation)
            block = kernel[tap_index * channels:(tap_index + 1) * channels]
            if transpose_kernel:
                block = block.T
            total = total + jnp.dot(moved.reshape(-1, channels), block, preferred_element_type=jnp.float32)
            tap_index += 1
    return total.reshape(field.shape)


def kernel_gradient(field, grad_field, dilation):
    channels = field.shape[2]
    flat_grad = grad_field.reshape(-1, channels)
    pieces = []
    for row_off in (-1, 0, 1):
        for col_off in (-1, 0, 1):
            moved = shifted(field, row_off * dilation, col_off * dilation).reshape(-1, channels)
            pieces.append(lax.dot_general(moved, flat_grad, (((0,), (0,)), ((), ())), preferred_element_type=jnp.float32))
    return jnp.concatenate(pieces, axis=0)


def reference(inputs, first_weight, second_weight, cotangent):
    grid_shape = (H, W, C)
    flat_shape = (H, W * C)
    inputs = inputs.reshape(grid_shape)
    cotangent = cotangent.reshape(grid_shape)
    first_weight = first_weight.reshape(9 * C, C)
    second_weight = second_weight.reshape(9 * C, C)
    input_padded_field = inputs.astype(jnp.float32)
    gelu_one, slope_one = gelu_parts(input_padded_field)
    activation_first = gelu_one.astype(jnp.bfloat16)
    hidden_state = (input_padded_field + apply_convolution(activation_first, first_weight, DILATION_FIRST, 1, False)).astype(jnp.bfloat16)
    hidden_padded_state = hidden_state.astype(jnp.float32)
    gelu_two, slope_two = gelu_parts(hidden_padded_state)
    activation_second = gelu_two.astype(jnp.bfloat16)
    output_field_grid = (hidden_padded_state + apply_convolution(activation_second, second_weight, DILATION_SECOND, 1, False)).astype(jnp.bfloat16)
    backward_second = apply_convolution(cotangent, second_weight, DILATION_SECOND, -1, True)
    hidden_gradient = (cotangent.astype(jnp.float32) + backward_second * slope_two).astype(jnp.bfloat16)
    scale_factor = 1.0 / H
    second_weight_gradient = (kernel_gradient(activation_second, cotangent, DILATION_SECOND) * scale_factor).astype(jnp.bfloat16)
    backward_first = apply_convolution(hidden_gradient, first_weight, DILATION_FIRST, -1, True)
    input_grad = (hidden_gradient.astype(jnp.float32) + backward_first * slope_one).astype(jnp.bfloat16)
    first_weight_gradient = (kernel_gradient(activation_first, hidden_gradient, DILATION_FIRST) * scale_factor).astype(jnp.bfloat16)
    return output_field_grid.reshape(flat_shape), input_grad.reshape(flat_shape), first_weight_gradient.reshape(9, C * C), second_weight_gradient.reshape(9, C * C)
```

```python
import functools

import jax
import jax.numpy as jnp
from jax import lax
from jax.experimental import pallas as pl
from jax.experimental.pallas import tpu as pltpu
from jax.sharding import Mesh, PartitionSpec as P

C = 192
AXES = ("zl", "yh", "yl", "x", "zh", "core")
SIZES = (4, 2, 2, 4, 4, 2)
PEERS = ("x", "zh", "zl", "yh")
PLANE = ("x", "yh", "yl")
LINE = ("zh", "zl")
BF16 = jnp.bfloat16
F32 = jnp.float32
ROWS = 168
PAD = 32


def call(kernel, out_shape, scratch=(), mem=40, smem_first=False):
    out_specs = jax.tree.map(lambda _: pl.BlockSpec(memory_space=pltpu.VMEM), out_shape)

    def run(*args):
        in_specs = [pl.BlockSpec(memory_space=pltpu.VMEM) for _ in args]
        if smem_first:
            in_specs[0] = pl.BlockSpec(memory_space=pltpu.SMEM)
        return pl.pallas_call(
            kernel,
            out_shape=out_shape,
            in_specs=in_specs,
            out_specs=out_specs,
            scratch_shapes=list(scratch),
            compiler_params=pltpu.CompilerParams(vmem_limit_bytes=mem * 1024 * 1024),
        )(*args)

    return run


def gelu_parts(value):
    normal_cdf = 0.5 * (1.0 + lax.erf(value * 0.7071067811865476))
    density = jnp.exp(-0.5 * value * value) * 0.3989422804014327
    return value * normal_cdf, normal_cdf + value * density


def pack_kernel(x_ref, g_ref, o_ref):
    fields = [x_ref[...].astype(F32), g_ref[...].astype(F32)]
    for pair in range(8):
        blocks = []
        for j in (2 * pair, 2 * pair + 1):
            pieces = [f[k * 8 : k * 8 + 8, j * C : (j + 1) * C] for f in fields for k in (0, 1)]
            blocks.append(jnp.concatenate(pieces, axis=1))
        o_ref[pair * 16 : pair * 16 + 16, :] = jnp.concatenate(blocks, axis=0).astype(BF16)


def main_kernel(core_ref, r_ref, w1_ref, w2_ref, o_ref, keep_ref, send_ref, tap_ref, ft_ref, wg_ref):
    cells = 256

    def unpack(f):
        part = r_ref[:, f * 2 * C : (f + 1) * 2 * C].astype(F32)
        both = [part[:, k * C : (k + 1) * C].reshape(16, 1, 8, C) for k in (0, 1)]
        return jnp.concatenate(both, axis=1).reshape(cells, C)

    def pack(value):
        split = value.reshape(16, 2, 8, C)
        return jnp.concatenate([split[:, k].reshape(128, C) for k in (0, 1)], axis=1)

    within = lax.broadcasted_iota(jnp.int32, (cells, C), 0) % 8

    def put_taps(slot, field, step):
        for a in (-1, 0, 1):
            moved = field
            if a != 0:
                rolled = pltpu.roll(field, (-a * step) % cells, 0)
                seen = (within + a * step >= 0) & (within + a * step < 8)
                moved = jnp.where(seen, rolled, 0.0)
            tap_ref[slot, a + 1, PAD : PAD + cells, :] = moved.astype(BF16)

    def tap(slot, a, b, step):
        start = PAD + 16 * b * step
        return tap_ref[slot, a + 1, start : start + cells, :]

    zeros = jnp.zeros((PAD, C), BF16)
    for slot in range(4):
        for a in range(3):
            tap_ref[slot, a, 0:PAD, :] = zeros
            tap_ref[slot, a, PAD + cells : 2 * PAD + cells, :] = zeros

    offsets = [(a, b) for a in (-1, 0, 1) for b in (-1, 0, 1)]

    def forward(slot, w_ref, step):
        total = None
        for t, (a, b) in enumerate(offsets):
            term = jnp.dot(
                tap(slot, a, b, step), w_ref[t * C : (t + 1) * C, :], preferred_element_type=F32
            )
            total = term if total is None else total + term
        return total

    def backward(slot, w_ref, step):
        total = None
        for t, (a, b) in enumerate(offsets):
            term = lax.dot_general(
                tap(slot, -a, -b, step),
                w_ref[t * C : (t + 1) * C, :],
                (((1,), (1,)), ((), ())),
                preferred_element_type=F32,
            )
            total = term if total is None else total + term
        return total

    def weight_grad(index, field, slot, step):
        turned = field.T
        for h in (0, 1):
            ft_ref[h] = turned[:, h * 128 : h * 128 + 128]
        left = jnp.concatenate(
            [
                jnp.concatenate([ft_ref[h, pl.ds(odd, 96, stride=2), :] for h in (0, 1)], axis=1)
                for odd in (0, 1)
            ],
            axis=0,
        ).astype(BF16)
        for t, (a, b) in enumerate(offsets):
            full = jnp.dot(left, tap(slot, -a, -b, step), preferred_element_type=F32)
            even, odd = full[0:96], full[96:192]
            lanes = (
                even[:, 0:128],
                jnp.concatenate([even[:, 128:192], odd[:, 0:64]], axis=1),
                odd[:, 64:192],
            )
            for q in range(3):
                for u in range(6):
                    wg_ref[index, pl.ds(t * 18 + q * 6 + u, 16, stride=ROWS), :] = lanes[q][
                        u * 16 : u * 16 + 16
                    ]

    x = unpack(0)
    g = unpack(1)
    gelu_one, slope_one = gelu_parts(x)
    act_one = gelu_one.astype(BF16).astype(F32)
    put_taps(0, act_one, 1)
    put_taps(2, g, 2)
    hidden = (x + forward(0, w1_ref, 1)).astype(BF16).astype(F32)
    gelu_two, slope_two = gelu_parts(hidden)
    act_two = gelu_two.astype(BF16).astype(F32)
    put_taps(1, act_two, 2)
    hidden_grad = (g + backward(2, w2_ref, 2) * slope_two).astype(BF16).astype(F32)
    put_taps(3, hidden_grad, 1)
    output = hidden + forward(1, w2_ref, 2)
    input_grad = hidden_grad + backward(3, w1_ref, 1) * slope_one
    o_ref[...] = jnp.concatenate([pack(output), pack(input_grad)], axis=1).astype(BF16)
    for index in (0, 1):
        for c in range(16):
            wg_ref[index, c * ROWS + 162 : c * ROWS + 168, :] = jnp.zeros((6, 128), F32)
    weight_grad(0, act_two, 2, 2)
    weight_grad(1, act_one, 3, 1)
    core = core_ref[0]
    keep_ref[...] = wg_ref[core].astype(BF16)
    send_ref[...] = wg_ref[1 - core].astype(BF16)


def join_kernel(s_ref, o_ref, out_ref, sum_ref, row_ref):
    total = s_ref[0].astype(F32)
    for c in range(1, 16):
        total = total + s_ref[c].astype(F32)
    sum_ref[...] = total
    row_ref[...] = jnp.zeros((2, 128, 128), F32)
    for x in range(4):
        for yh in range(2):
            t = x * 2 + yh
            base = x * 32 + yh
            row_ref[0, pl.ds(base, 16, stride=2), :] = sum_ref[t * 18 : t * 18 + 16, :]
            row_ref[1, pl.ds(base, 2, stride=2), :] = sum_ref[t * 18 + 16 : t * 18 + 18, :]
            row_ref[1, pl.ds(base + 4, 3, stride=2), :] = sum_ref[144 + t * 3 : 147 + t * 3, :]
    out_ref[:, 0:768] = o_ref[...]
    for h in (0, 1):
        out_ref[:, 768 + h * 128 : 896 + h * 128] = row_ref[h].astype(BF16)


def split_kernel(r_ref, out_ref, ig_ref, z_ref):
    value = r_ref[...].astype(F32)
    for f, ref in enumerate((out_ref, ig_ref)):
        halves = []
        for k in (0, 1):
            lo = f * 2 * C + k * C
            halves.append(
                jnp.concatenate([value[j * 8 : j * 8 + 8, lo : lo + C] for j in range(16)], axis=1)
            )
        ref[...] = jnp.concatenate(halves, axis=0).astype(BF16)
    row = lax.broadcasted_iota(jnp.int32, (8, 256), 0)
    total = jnp.zeros((8, 256), F32)
    for x in range(4):
        part = value[x * 32 : x * 32 + 8, 768:1024]
        for zh in range(1, 4):
            part = part + value[x * 32 + zh * 8 : x * 32 + zh * 8 + 8, 768:1024]
        part = part + pltpu.roll(part, 4, 0)
        part = part + pltpu.roll(part, 2, 0)
        total = jnp.where(row // 2 == x, part, total)
    total = total * (1.0 / 256.0)
    mine = jnp.concatenate([total[:, 0:128], total[:, 128:256]], axis=0).astype(BF16)
    for z in range(16):
        z_ref[z] = mine


def spread_kernel(z_ref, out_ref):
    slots = [z_ref[z].astype(F32) for z in range(16)]
    rows = [s[0:8] for s in slots] + [s[8:16] for s in slots[:5]]
    mine = jnp.concatenate(rows, axis=0).astype(BF16)
    for c in range(16):
        out_ref[c] = mine


def final_kernel(core_ref, own_ref, other_ref, one_ref, two_ref, scr_ref):
    core = core_ref[0]
    for c in range(16):
        scr_ref[core, c * ROWS : (c + 1) * ROWS, :] = own_ref[c].astype(F32)
        scr_ref[1 - core, c * ROWS : (c + 1) * ROWS, :] = other_ref[c].astype(F32)
    for index, ref in enumerate((two_ref, one_ref)):
        for n in range(288):
            m, q = n // 3, n % 3
            u, c = m // 16, m % 16
            c8, yl = c // 2, c % 2
            v = q * 6 + u
            eight = scr_ref[index, pl.ds(yl * ROWS + v * 8 + c8, 8, stride=2 * ROWS), :]
            last = ((v // 3) * 2 + yl) * ROWS + (18 + v % 3) * 8 + c8
            nine = jnp.concatenate([eight, scr_ref[index, last : last + 1, :]], axis=0)
            ref[:, n * 128 : (n + 1) * 128] = nine.astype(BF16)


def exchange(value, axes):
    return lax.all_to_all(value, axes, split_axis=0, concat_axis=0, tiled=True)


def shape(*dims, dtype=BF16):
    return jax.ShapeDtypeStruct(dims, dtype)


def per_device(inputs, first_weight, second_weight, cotangent):
    core = lax.axis_index("core").astype(jnp.int32).reshape(1)
    swap = [(0, 1), (1, 0)]
    kernel_one = first_weight.reshape(9 * C, C)
    kernel_two = second_weight.reshape(9 * C, C)
    packed = call(pack_kernel, shape(128, 768))(inputs, cotangent)
    received = exchange(packed, PEERS)
    fields, keep, send = call(
        main_kernel,
        (shape(128, 768), shape(16 * ROWS, 128), shape(16 * ROWS, 128)),
        scratch=(
            pltpu.VMEM((4, 3, 256 + 2 * PAD, C), BF16),
            pltpu.VMEM((2, C, 128), F32),
            pltpu.VMEM((2, 16 * ROWS, 128), F32),
        ),
        smem_first=True,
    )(core, received, kernel_one, kernel_two)
    other = lax.ppermute(send, "core", swap)
    pair = (keep.astype(F32) + other.astype(F32)).astype(BF16).reshape(16, ROWS, 128)
    plane = exchange(pair, PLANE)
    joined = call(
        join_kernel,
        shape(128, 1024),
        scratch=(pltpu.VMEM((ROWS, 128), F32), pltpu.VMEM((2, 128, 128), F32)),
    )(plane, fields)
    back = exchange(joined, PEERS)
    output, input_grad, mine = call(
        split_kernel, (shape(16, 16 * C), shape(16, 16 * C), shape(16, 16, 128))
    )(back)
    line = exchange(mine, LINE)
    spread = call(spread_kernel, shape(16, ROWS, 128))(line)
    gathered = exchange(spread, PLANE)
    partner = lax.ppermute(gathered, "core", swap)
    one, two = call(
        final_kernel,
        (shape(9, C * C), shape(9, C * C)),
        scratch=(pltpu.VMEM((2, 16 * ROWS, 128), F32),),
        smem_first=True,
    )(core, gathered, partner)
    return output, input_grad, one, two


def solution(mesh):
    grid = Mesh(mesh.devices.reshape(SIZES), AXES)
    tile = P(("zl", "yh", "yl"), ("x", "zh", "core"))
    return jax.shard_map(
        per_device,
        mesh=grid,
        in_specs=(tile, P(), P(), tile),
        out_specs=(tile, tile, P(), P()),
        check_vma=False,
    )
```

```python
import jax
import jax.numpy as jnp
from jax import lax
from jax.experimental import pallas as pl
from jax.experimental.pallas import tpu as pltpu
from jax.sharding import Mesh, PartitionSpec as P

C = 192
AXES = ("zl", "yh", "yl", "x", "zh", "core")
SIZES = (4, 2, 2, 4, 4, 2)
LINE = ("zh", "zl")
BLOCK = ("x", "yh")
PLANE = ("yl", "x", "yh")
BF16 = jnp.bfloat16
F32 = jnp.float32
ROWS = 176
FIELD = 96
PAD = 32


def call(kernel, out_shape, scratch=(), mem=40, smem_first=False):
    out_specs = jax.tree.map(lambda _: pl.BlockSpec(memory_space=pltpu.VMEM), out_shape)

    def run(*args):
        in_specs = [pl.BlockSpec(memory_space=pltpu.VMEM) for _ in args]
        if smem_first:
            in_specs[0] = pl.BlockSpec(memory_space=pltpu.SMEM)
        return pl.pallas_call(
            kernel,
            out_shape=out_shape,
            in_specs=in_specs,
            out_specs=out_specs,
            scratch_shapes=list(scratch),
            compiler_params=pltpu.CompilerParams(vmem_limit_bytes=mem * 1024 * 1024),
        )(*args)

    return run


def gelu_parts(value):
    normal_cdf = 0.5 * (1.0 + lax.erf(value * 0.7071067811865476))
    density = jnp.exp(-0.5 * value * value) * 0.3989422804014327
    return value * normal_cdf, normal_cdf + value * density


def pack_kernel(x_ref, g_ref, o_ref):
    fields = [x_ref[...].astype(F32), g_ref[...].astype(F32)]
    for z in range(16):
        pieces = [f[k * 8 : k * 8 + 8, z * C : (z + 1) * C] for f in fields for k in (0, 1)]
        wide = jnp.concatenate(pieces, axis=1)
        tiles = [wide[:, t * 128 : t * 128 + 128] for t in range(6)]
        o_ref[z] = jnp.concatenate(tiles, axis=0).astype(BF16)


def relay_kernel(r_ref, o_ref, scr_ref):
    for z in range(16):
        scr_ref[z * 48 : z * 48 + 48, :] = r_ref[z].astype(F32)
    for e in range(8):
        tiles = [scr_ref[pl.ds(t * 8 + e, 16, stride=48), :] for t in range(6)]
        o_ref[e] = jnp.concatenate(tiles, axis=0).astype(BF16)


def main_kernel(core_ref, r_ref, w1_ref, w2_ref, o_ref, keep_ref, send_ref, tap_ref, ft_ref, wg_ref):
    cells = 256

    def unpack(f):
        tiles = []
        for t in range(3 * f, 3 * f + 3):
            pieces = []
            for x in range(4):
                pair = [r_ref[x * 2 + yh, t * 16 : t * 16 + 16, :].astype(F32) for yh in (0, 1)]
                for zh in range(4):
                    pieces += [p[zh * 4 : zh * 4 + 4] for p in pair]
            tiles.append(jnp.concatenate(pieces, axis=0))
        part = jnp.concatenate(tiles, axis=1)
        both = [part[:, k * C : (k + 1) * C].reshape(16, 1, 8, C) for k in (0, 1)]
        return jnp.concatenate(both, axis=1).reshape(cells, C)

    def pack(value):
        split = value.reshape(16, 2, 8, C)
        wide = jnp.concatenate([split[:, k].reshape(128, C) for k in (0, 1)], axis=1)
        return [wide[:, t * 128 : t * 128 + 128] for t in range(3)]

    within = lax.broadcasted_iota(jnp.int32, (cells, C), 0) % 8
    yh_of, zl_of = within // 4, within % 4

    def ahead(field, rows):
        return pltpu.roll(field, (-rows) % cells, 0)

    def put_taps(slot, field, step):
        for a in (-1, 0, 1):
            moved = field
            if a != 0 and step == 2:
                moved = jnp.where((zl_of + a >= 0) & (zl_of + a < 4), ahead(field, a), 0.0)
            elif a != 0:
                start = 0 if a == 1 else 1
                crossed = jnp.where((zl_of + a >= 0) & (zl_of + a < 4), ahead(field, -3 * a), 0.0)
                moved = jnp.where(yh_of == start, ahead(field, 4 * a), crossed)
            tap_ref[slot, a + 1, PAD : PAD + cells, :] = moved.astype(BF16)

    def tap(slot, a, b, step):
        start = PAD + 16 * b * step
        return tap_ref[slot, a + 1, start : start + cells, :]

    zeros = jnp.zeros((PAD, C), BF16)
    for slot in range(4):
        for a in range(3):
            tap_ref[slot, a, 0:PAD, :] = zeros
            tap_ref[slot, a, PAD + cells : 2 * PAD + cells, :] = zeros

    offsets = [(a, b) for a in (-1, 0, 1) for b in (-1, 0, 1)]

    def forward(slot, w_ref, step):
        total = None
        for t, (a, b) in enumerate(offsets):
            term = jnp.dot(
                tap(slot, a, b, step), w_ref[t * C : (t + 1) * C, :], preferred_element_type=F32
            )
            total = term if total is None else total + term
        return total

    def backward(slot, w_ref, step):
        total = None
        for t, (a, b) in enumerate(offsets):
            term = lax.dot_general(
                tap(slot, -a, -b, step),
                w_ref[t * C : (t + 1) * C, :],
                (((1,), (1,)), ((), ())),
                preferred_element_type=F32,
            )
            total = term if total is None else total + term
        return total

    def weight_grad(index, field, slot, step):
        turned = field.T
        for h in (0, 1):
            ft_ref[h] = turned[:, h * 128 : h * 128 + 128]
        left = jnp.concatenate(
            [
                jnp.concatenate([ft_ref[h, pl.ds(odd, 96, stride=2), :] for h in (0, 1)], axis=1)
                for odd in (0, 1)
            ],
            axis=0,
        ).astype(BF16)
        for t, (a, b) in enumerate(offsets):
            full = jnp.dot(left, tap(slot, -a, -b, step), preferred_element_type=F32)
            even, odd = full[0:96], full[96:192]
            lanes = (
                even[:, 0:128],
                jnp.concatenate([even[:, 128:192], odd[:, 0:64]], axis=1),
                odd[:, 64:192],
            )
            for q in range(3):
                for u in range(6):
                    wg_ref[index, pl.ds(t * 18 + q * 6 + u, 16, stride=ROWS), :] = lanes[q][
                        u * 16 : u * 16 + 16
                    ]

    x = unpack(0)
    g = unpack(1)
    gelu_one, slope_one = gelu_parts(x)
    act_one = gelu_one.astype(BF16).astype(F32)
    put_taps(0, act_one, 1)
    put_taps(2, g, 2)
    hidden = (x + forward(0, w1_ref, 1)).astype(BF16).astype(F32)
    gelu_two, slope_two = gelu_parts(hidden)
    act_two = gelu_two.astype(BF16).astype(F32)
    put_taps(1, act_two, 2)
    hidden_grad = (g + backward(2, w2_ref, 2) * slope_two).astype(BF16).astype(F32)
    put_taps(3, hidden_grad, 1)
    output = hidden + forward(1, w2_ref, 2)
    input_grad = hidden_grad + backward(3, w1_ref, 1) * slope_one
    tiles = pack(output) + pack(input_grad)
    for x in range(4):
        for yh in (0, 1):
            pieces = []
            for tile in tiles:
                for zh in range(4):
                    start = (x * 4 + zh) * 8 + yh * 4
                    pieces.append(tile[start : start + 4])
            o_ref[x * 2 + yh] = jnp.concatenate(pieces, axis=0).astype(BF16)
    for index in (0, 1):
        for c in range(16):
            wg_ref[index, c * ROWS + 162 : (c + 1) * ROWS, :] = jnp.zeros((ROWS - 162, 128), F32)
    weight_grad(0, act_two, 2, 2)
    weight_grad(1, act_one, 3, 1)
    core = core_ref[0]
    for c in range(16):
        keep_ref[c] = wg_ref[core, c * ROWS : (c + 1) * ROWS, :].astype(BF16)
        send_ref[c] = wg_ref[1 - core, c * ROWS : (c + 1) * ROWS, :].astype(BF16)


def join_kernel(f_ref, keep_ref, other_ref, o_ref):
    for c in range(16):
        o_ref[c, 0:FIELD, :] = f_ref[c % 8]
        pair = keep_ref[c].astype(F32) + other_ref[c].astype(F32)
        o_ref[c, FIELD : FIELD + ROWS, :] = pair.astype(BF16)


def line_kernel(yl_ref, s_ref, o_ref, sum_ref, scr_ref):
    yl = yl_ref[0]
    total = s_ref[0, FIELD : FIELD + ROWS, :].astype(F32)
    for c in range(1, 16):
        total = total + s_ref[c, FIELD : FIELD + ROWS, :].astype(F32)
    sum_ref[0:ROWS, :] = total
    sum_ref[ROWS : ROWS + 8, :] = jnp.zeros((8, 128), F32)
    for s in range(8):
        scr_ref[s * FIELD : (s + 1) * FIELD, :] = s_ref[yl * 8 + s, 0:FIELD, :].astype(F32)
    for z in range(16):
        tiles = [scr_ref[pl.ds(t * 16 + z, 8, stride=FIELD), :] for t in range(6)]
        tiles.append(sum_ref[z * 11 : z * 11 + 16, :])
        o_ref[z] = jnp.concatenate(tiles, axis=0).astype(BF16)


def split_kernel(r_ref, out_ref, ig_ref, z_ref):
    total = r_ref[0, 48:64, :].astype(F32)
    for z in range(1, 16):
        total = total + r_ref[z, 48:64, :].astype(F32)
    mine = (total * (1.0 / 256.0)).astype(BF16)
    for z in range(16):
        z_ref[z] = mine
    for z in range(16):
        value = r_ref[z, 0:48, :].astype(F32)
        wide = jnp.concatenate([value[t * 8 : t * 8 + 8] for t in range(6)], axis=1)
        for f, ref in enumerate((out_ref, ig_ref)):
            halves = [wide[:, (2 * f + k) * C : (2 * f + k + 1) * C] for k in (0, 1)]
            ref[:, z * C : (z + 1) * C] = jnp.concatenate(halves, axis=0).astype(BF16)


def spread_kernel(z_ref, out_ref, scr_ref):
    for z in range(16):
        scr_ref[z * 11 : z * 11 + 16, :] = z_ref[z].astype(F32)
    mine = scr_ref[0:ROWS, :].astype(BF16)
    for c in range(16):
        out_ref[c] = mine


def final_kernel(core_ref, own_ref, other_ref, one_ref, two_ref, scr_ref):
    core = core_ref[0]
    for c in range(16):
        scr_ref[core, c * ROWS : (c + 1) * ROWS, :] = own_ref[c].astype(F32)
        scr_ref[1 - core, c * ROWS : (c + 1) * ROWS, :] = other_ref[c].astype(F32)
    for index, ref in enumerate((two_ref, one_ref)):
        for n in range(288):
            m, q = n // 3, n % 3
            base = (m % 16) * ROWS + q * 6 + m // 16
            eight = scr_ref[index, pl.ds(base, 8, stride=18), :]
            nine = jnp.concatenate([eight, scr_ref[index, base + 144 : base + 145, :]], axis=0)
            ref[:, n * 128 : (n + 1) * 128] = nine.astype(BF16)


def exchange(value, axes):
    return lax.all_to_all(value, axes, split_axis=0, concat_axis=0, tiled=True)


def shape(*dims, dtype=BF16):
    return jax.ShapeDtypeStruct(dims, dtype)


def per_device(inputs, first_weight, second_weight, cotangent):
    core = lax.axis_index("core").astype(jnp.int32).reshape(1)
    half = lax.axis_index("yl").astype(jnp.int32).reshape(1)
    swap = [(0, 1), (1, 0)]
    kernel_one = first_weight.reshape(9 * C, C)
    kernel_two = second_weight.reshape(9 * C, C)
    packed = call(pack_kernel, shape(16, 48, 128))(inputs, cotangent)
    line_in = exchange(packed, LINE)
    relayed = call(relay_kernel, shape(8, FIELD, 128), scratch=(pltpu.VMEM((768, 128), F32),))(line_in)
    received = exchange(relayed, BLOCK)
    fields, keep, send = call(
        main_kernel,
        (shape(8, FIELD, 128), shape(16, ROWS, 128), shape(16, ROWS, 128)),
        scratch=(
            pltpu.VMEM((4, 3, 256 + 2 * PAD, C), BF16),
            pltpu.VMEM((2, C, 128), F32),
            pltpu.VMEM((2, 16 * ROWS, 128), F32),
        ),
        smem_first=True,
    )(core, received, kernel_one, kernel_two)
    other = lax.ppermute(send, "core", swap)
    joined = call(join_kernel, shape(16, FIELD + ROWS, 128))(fields, keep, other)
    plane = exchange(joined, PLANE)
    to_line = call(
        line_kernel,
        shape(16, 64, 128),
        scratch=(pltpu.VMEM((ROWS + 8, 128), F32), pltpu.VMEM((8 * FIELD, 128), F32)),
        smem_first=True,
    )(half, plane)
    back = exchange(to_line, LINE)
    output, input_grad, mine = call(
        split_kernel, (shape(16, 16 * C), shape(16, 16 * C), shape(16, 16, 128))
    )(back)
    line = exchange(mine, LINE)
    spread = call(
        spread_kernel, shape(16, ROWS, 128), scratch=(pltpu.VMEM((ROWS + 8, 128), F32),)
    )(line)
    gathered = exchange(spread, PLANE)
    partner = lax.ppermute(gathered, "core", swap)
    one, two = call(
        final_kernel,
        (shape(9, C * C), shape(9, C * C)),
        scratch=(pltpu.VMEM((2, 16 * ROWS, 128), F32),),
        smem_first=True,
    )(core, gathered, partner)
    return output, input_grad, one, two


def solution(mesh):
    grid = Mesh(mesh.devices.reshape(SIZES), AXES)
    tile = P(("zl", "yh", "yl"), ("x", "zh", "core"))
    return jax.shard_map(
        per_device,
        mesh=grid,
        in_specs=(tile, P(), P(), tile),
        out_specs=(tile, tile, P(), P()),
        check_vma=False,
    )
```

```python
import jax
import jax.numpy as jnp
from jax import lax
from jax.experimental import pallas as pl
from jax.experimental.pallas import tpu as pltpu
from jax.sharding import Mesh, PartitionSpec as P

C = 192
AXES = ("zl", "yh", "yl", "x", "zh", "core")
SIZES = (4, 2, 2, 4, 4, 2)
PEERS = ("x", "zh", "zl", "yh")
PLANE = ("core", "yl", "x", "yh")
LINE = ("zh", "zl")
BF16 = jnp.bfloat16
F32 = jnp.float32
ROWS = 168
PAD = 32


def call(kernel, out_shape, scratch=(), space=pltpu.VMEM):
    out_specs = jax.tree.map(lambda _: pl.BlockSpec(memory_space=pltpu.VMEM), out_shape)

    def run(*args):
        return pl.pallas_call(
            kernel,
            out_shape=out_shape,
            in_specs=[pl.BlockSpec(memory_space=space) for _ in args],
            out_specs=out_specs,
            scratch_shapes=list(scratch),
            compiler_params=pltpu.CompilerParams(vmem_limit_bytes=40 * 1024 * 1024),
        )(*args)

    return run


def gelu_parts(value):
    normal_cdf = 0.5 * (1.0 + lax.erf(value * 0.7071067811865476))
    density = jnp.exp(-0.5 * value * value) * 0.3989422804014327
    return value * normal_cdf, normal_cdf + value * density


def pack_kernel(x_hbm, g_hbm, o_ref, in_ref, row_ref, sems):
    copies = [pltpu.make_async_copy(h, in_ref.at[n], sems.at[n]) for n, h in enumerate((x_hbm, g_hbm))]
    for copy in copies:
        copy.start()
    row_ref[...] = jnp.zeros((1024, 128), F32)
    for copy in copies:
        copy.wait()
    fields = [in_ref[n].astype(F32) for n in (0, 1)]
    for j in range(16):
        pieces = [f[k * 8 : k * 8 + 8, j * C : (j + 1) * C] for f in fields for k in (0, 1)]
        wide = jnp.concatenate(pieces, axis=1)
        for t in range(6):
            row_ref[pl.ds(j * 64 + t, 8, stride=8), :] = wide[:, t * 128 : t * 128 + 128]
    for j in range(16):
        o_ref[j * 64 : j * 64 + 64, :] = row_ref[j * 64 : j * 64 + 64, :].astype(BF16)


def main_kernel(r_ref, w1_ref, w2_ref, o_ref, g_ref, row_ref, tap_ref, ft_ref, wg_ref):
    cells = 256

    row_ref[...] = r_ref[...].astype(F32)

    def unpack(f):
        tiles = [row_ref[pl.ds(3 * f + t, 128, stride=8), :] for t in range(3)]
        part = jnp.concatenate(tiles, axis=1)
        both = [part[:, k * C : (k + 1) * C].reshape(16, 1, 8, C) for k in (0, 1)]
        return jnp.concatenate(both, axis=1).reshape(cells, C)

    def pack(value):
        split = value.reshape(16, 2, 8, C)
        return jnp.concatenate([split[:, k].reshape(128, C) for k in (0, 1)], axis=1)

    within = lax.broadcasted_iota(jnp.int32, (cells, C), 0) % 8

    def put_taps(slot, field, step):
        for a in (-1, 0, 1):
            moved = field
            if a != 0:
                rolled = pltpu.roll(field, (-a * step) % cells, 0)
                seen = (within + a * step >= 0) & (within + a * step < 8)
                moved = jnp.where(seen, rolled, 0.0)
            tap_ref[slot, a + 1, PAD : PAD + cells, :] = moved.astype(BF16)

    def tap(slot, a, b, step):
        start = PAD + 16 * b * step
        return tap_ref[slot, a + 1, start : start + cells, :]

    zeros = jnp.zeros((PAD, C), BF16)
    for slot in range(4):
        for a in range(3):
            tap_ref[slot, a, 0:PAD, :] = zeros
            tap_ref[slot, a, PAD + cells : 2 * PAD + cells, :] = zeros

    offsets = [(a, b) for a in (-1, 0, 1) for b in (-1, 0, 1)]

    def forward(slot, w_ref, step):
        total = None
        for t, (a, b) in enumerate(offsets):
            term = jnp.dot(
                tap(slot, a, b, step), w_ref[t * C : (t + 1) * C, :], preferred_element_type=F32
            )
            total = term if total is None else total + term
        return total

    def backward(slot, w_ref, step):
        total = None
        for t, (a, b) in enumerate(offsets):
            term = lax.dot_general(
                tap(slot, -a, -b, step),
                w_ref[t * C : (t + 1) * C, :],
                (((1,), (1,)), ((), ())),
                preferred_element_type=F32,
            )
            total = term if total is None else total + term
        return total

    def weight_grad(index, field, slot, step):
        turned = field.T
        for h in (0, 1):
            ft_ref[h] = turned[:, h * 128 : h * 128 + 128]
        left = jnp.concatenate(
            [
                jnp.concatenate([ft_ref[h, pl.ds(odd, 96, stride=2), :] for h in (0, 1)], axis=1)
                for odd in (0, 1)
            ],
            axis=0,
        ).astype(BF16)
        for t, (a, b) in enumerate(offsets):
            full = jnp.dot(left, tap(slot, -a, -b, step), preferred_element_type=F32)
            even, odd = full[0:96], full[96:192]
            lanes = (
                even[:, 0:128],
                jnp.concatenate([even[:, 128:192], odd[:, 0:64]], axis=1),
                odd[:, 64:192],
            )
            for q in range(3):
                for u in range(6):
                    wg_ref[index, pl.ds(t * 18 + q * 6 + u, 16, stride=ROWS), :] = lanes[q][
                        u * 16 : u * 16 + 16
                    ]

    x = unpack(0)
    g = unpack(1)
    gelu_one, slope_one = gelu_parts(x)
    act_one = gelu_one.astype(BF16).astype(F32)
    put_taps(0, act_one, 1)
    put_taps(2, g, 2)
    hidden = (x + forward(0, w1_ref, 1)).astype(BF16).astype(F32)
    gelu_two, slope_two = gelu_parts(hidden)
    act_two = gelu_two.astype(BF16).astype(F32)
    put_taps(1, act_two, 2)
    hidden_grad = (g + backward(2, w2_ref, 2) * slope_two).astype(BF16).astype(F32)
    put_taps(3, hidden_grad, 1)
    output = hidden + forward(1, w2_ref, 2)
    input_grad = hidden_grad + backward(3, w1_ref, 1) * slope_one
    o_ref[...] = jnp.concatenate([pack(output), pack(input_grad)], axis=1).astype(BF16)
    for index in (0, 1):
        for c in range(16):
            wg_ref[index, c * ROWS + 162 : c * ROWS + 168, :] = jnp.zeros((6, 128), F32)
    weight_grad(0, act_two, 2, 2)
    weight_grad(1, act_one, 3, 1)
    for c in range(32):
        g_ref[c] = wg_ref[c // 16, (c % 16) * ROWS : (c % 16 + 1) * ROWS, :].astype(BF16)


def join_kernel(s_ref, f_ref, out_ref, sum_ref, row_ref):
    total = s_ref[0].astype(F32)
    for c in range(1, 32):
        total = total + s_ref[c].astype(F32)
    sum_ref[...] = total
    value = f_ref[...].astype(F32)
    for t in range(6):
        row_ref[pl.ds(t, 128, stride=8), :] = value[:, t * 128 : t * 128 + 128]
    for t in (6, 7):
        row_ref[pl.ds(t, 128, stride=8), :] = jnp.zeros((128, 128), F32)
    for x in range(4):
        for yh in range(2):
            t = x * 2 + yh
            base = (x * 32 + yh) * 8 + 6
            row_ref[pl.ds(base, 16, stride=16), :] = sum_ref[t * 18 : t * 18 + 16, :]
            row_ref[pl.ds(base + 1, 2, stride=16), :] = sum_ref[t * 18 + 16 : t * 18 + 18, :]
            row_ref[pl.ds(base + 33, 3, stride=16), :] = sum_ref[144 + t * 3 : 147 + t * 3, :]
    out_ref[...] = row_ref[...].astype(BF16)


def split_kernel(r_ref, out_ref, ig_ref, z_ref, row_ref):
    row_ref[...] = r_ref[...].astype(F32)
    tiles = [row_ref[pl.ds(t, 128, stride=8), :] for t in range(8)]
    for f, ref in enumerate((out_ref, ig_ref)):
        wide = jnp.concatenate(tiles[3 * f : 3 * f + 3], axis=1)
        halves = []
        for k in (0, 1):
            part = wide[:, k * C : (k + 1) * C]
            halves.append(jnp.concatenate([part[j * 8 : j * 8 + 8] for j in range(16)], axis=1))
        ref[...] = jnp.concatenate(halves, axis=0).astype(BF16)
    value = jnp.concatenate(tiles[6:8], axis=1)
    row = lax.broadcasted_iota(jnp.int32, (8, 256), 0)
    total = jnp.zeros((8, 256), F32)
    for x in range(4):
        part = value[x * 32 : x * 32 + 8]
        for zh in range(1, 4):
            part = part + value[x * 32 + zh * 8 : x * 32 + zh * 8 + 8]
        part = part + pltpu.roll(part, 4, 0)
        part = part + pltpu.roll(part, 2, 0)
        total = jnp.where(row // 2 == x, part, total)
    total = total * (1.0 / 256.0)
    mine = jnp.concatenate([total[:, 0:128], total[:, 128:256]], axis=0).astype(BF16)
    for z in range(16):
        z_ref[z] = mine


def spread_kernel(z_ref, out_ref):
    slots = [z_ref[z].astype(F32) for z in range(16)]
    rows = [s[0:8] for s in slots] + [s[8:16] for s in slots[:5]]
    mine = jnp.concatenate(rows, axis=0).astype(BF16)
    for c in range(32):
        out_ref[c] = mine


def final_kernel(r_ref, one_ref, two_ref, scr_ref):
    for c in range(32):
        scr_ref[c * ROWS : (c + 1) * ROWS, :] = r_ref[c].astype(F32)
    for index, ref in enumerate((two_ref, one_ref)):
        for n in range(288):
            m, q = n // 3, n % 3
            u, c = m // 16, m % 16
            v = q * 6 + u
            first = (index * 16 + (c // 8) * 8) * ROWS + c % 8
            eight = scr_ref[pl.ds(first + v * 8, 8, stride=ROWS), :]
            last = first + (v // 3) * ROWS + (18 + v % 3) * 8
            nine = jnp.concatenate([eight, scr_ref[last : last + 1, :]], axis=0)
            ref[:, n * 128 : (n + 1) * 128] = nine.astype(BF16)


def exchange(value, axes):
    return lax.all_to_all(value, axes, split_axis=0, concat_axis=0, tiled=True)


def shape(*dims, dtype=BF16):
    return jax.ShapeDtypeStruct(dims, dtype)


def per_device(inputs, first_weight, second_weight, cotangent):
    rows = pltpu.VMEM((1024, 128), F32)
    kernel_one = first_weight.reshape(9 * C, C)
    kernel_two = second_weight.reshape(9 * C, C)
    packed = call(
        pack_kernel,
        shape(1024, 128),
        scratch=(pltpu.VMEM((2, 16, 16 * C), BF16), rows, pltpu.SemaphoreType.DMA((2,))),
        space=pl.ANY,
    )(inputs, cotangent)
    received = exchange(packed.reshape(128, 8, 128), PEERS).reshape(1024, 128)
    fields, grads = call(
        main_kernel,
        (shape(128, 768), shape(32, ROWS, 128)),
        scratch=(
            rows,
            pltpu.VMEM((4, 3, 256 + 2 * PAD, C), BF16),
            pltpu.VMEM((2, C, 128), F32),
            pltpu.VMEM((2, 16 * ROWS, 128), F32),
        ),
    )(received, kernel_one, kernel_two)
    plane = exchange(grads, PLANE)
    joined = call(join_kernel, shape(1024, 128), scratch=(pltpu.VMEM((ROWS, 128), F32), rows))(
        plane, fields
    )
    back = exchange(joined.reshape(128, 8, 128), PEERS).reshape(1024, 128)
    output, input_grad, mine = call(
        split_kernel,
        (shape(16, 16 * C), shape(16, 16 * C), shape(16, 16, 128)),
        scratch=(rows,),
    )(back)
    line = exchange(mine, LINE)
    spread = call(spread_kernel, shape(32, ROWS, 128))(line)
    gathered = exchange(spread, PLANE)
    one, two = call(
        final_kernel,
        (shape(9, C * C), shape(9, C * C)),
        scratch=(pltpu.VMEM((32 * ROWS, 128), F32),),
    )(gathered)
    return output, input_grad, one, two


def solution(mesh):
    grid = Mesh(mesh.devices.reshape(SIZES), AXES)
    tile = P(("zl", "yh", "yl"), ("x", "zh", "core"))
    return jax.shard_map(
        per_device,
        mesh=grid,
        in_specs=(tile, P(), P(), tile),
        out_specs=(tile, tile, P(), P()),
        check_vma=False,
    )
```

```python
import jax
import jax.numpy as jnp
from jax import lax
from jax.experimental import pallas as pl
from jax.experimental.pallas import tpu as pltpu
from jax.sharding import Mesh, PartitionSpec as P

C = 192
AXES = ("zl", "yh", "yl", "x", "zh", "core")
SIZES = (4, 2, 2, 4, 4, 2)
LINE = ("zh", "zl")
PEERS = ("zh", "zl", "x", "yh")
PLANE = ("yl", "x", "yh")
BF16 = jnp.bfloat16
F32 = jnp.float32
ROWS = 176
FIELD = 96
PAD = 32


def call(kernel, out_shape, scratch=(), spaces={}, out_specs=None, limit=40 * 1024 * 1024):
    if out_specs is None:
        out_specs = jax.tree.map(lambda _: pl.BlockSpec(memory_space=pltpu.VMEM), out_shape)

    def run(*args):
        return pl.pallas_call(
            kernel,
            out_shape=out_shape,
            in_specs=[
                pl.BlockSpec(memory_space=spaces.get(n, pltpu.VMEM)) for n in range(len(args))
            ],
            out_specs=out_specs,
            scratch_shapes=list(scratch),
            compiler_params=pltpu.CompilerParams(vmem_limit_bytes=limit),
        )(*args)

    return run


def gelu_parts(value):
    normal_cdf = 0.5 * (1.0 + lax.erf(value * 0.7071067811865476))
    density = jnp.exp(-0.5 * value * value) * 0.3989422804014327
    return value * normal_cdf, normal_cdf + value * density


def pack_kernel(core_ref, half_ref, x_hbm, g_hbm, o_ref, where_ref, in_ref, row_ref, sems):
    copies = [pltpu.make_async_copy(h, in_ref.at[n], sems.at[n]) for n, h in enumerate((x_hbm, g_hbm))]
    for copy in copies:
        copy.start()
    where_ref[0] = core_ref[0]
    where_ref[1] = half_ref[0]
    row_ref[...] = jnp.zeros((1024, 128), F32)
    for copy in copies:
        copy.wait()
    fields = [in_ref[n].astype(F32) for n in (0, 1)]
    for z in range(16):
        pieces = [f[k * 8 : k * 8 + 8, z * C : (z + 1) * C] for f in fields for k in (0, 1)]
        wide = jnp.concatenate(pieces, axis=1)
        for t in range(6):
            row_ref[pl.ds(z * 64 + t, 8, stride=8), :] = wide[:, t * 128 : t * 128 + 128]
    for z in range(16):
        o_ref[z * 64 : z * 64 + 64, :] = row_ref[z * 64 : z * 64 + 64, :].astype(BF16)


def main_kernel(
    where_ref, r_ref, w1_ref, w2_ref, o_ref, keep_ref, send_ref, row_ref, tap_ref, ft_ref, wg_ref
):
    cells = 256

    row_ref[...] = r_ref[...].astype(F32)

    def unpack(f):
        tiles = []
        for t in range(3 * f, 3 * f + 3):
            pieces = []
            for x in range(4):
                for zh in range(4):
                    for yh in (0, 1):
                        first = (zh * 32 + x * 2 + yh) * 8 + t
                        pieces.append(row_ref[pl.ds(first, 4, stride=64), :])
            tiles.append(jnp.concatenate(pieces, axis=0))
        part = jnp.concatenate(tiles, axis=1)
        both = [part[:, k * C : (k + 1) * C].reshape(16, 1, 8, C) for k in (0, 1)]
        return jnp.concatenate(both, axis=1).reshape(cells, C)

    def pack(value):
        split = value.reshape(16, 2, 8, C)
        wide = jnp.concatenate([split[:, k].reshape(128, C) for k in (0, 1)], axis=1)
        return [wide[:, t * 128 : t * 128 + 128] for t in range(3)]

    within = lax.broadcasted_iota(jnp.int32, (cells, C), 0) % 8
    yh_of, zl_of = within // 4, within % 4

    def ahead(field, rows):
        return pltpu.roll(field, (-rows) % cells, 0)

    def put_taps(slot, field, step):
        for a in (-1, 0, 1):
            moved = field
            if a != 0 and step == 2:
                moved = jnp.where((zl_of + a >= 0) & (zl_of + a < 4), ahead(field, a), 0.0)
            elif a != 0:
                start = 0 if a == 1 else 1
                crossed = jnp.where((zl_of + a >= 0) & (zl_of + a < 4), ahead(field, -3 * a), 0.0)
                moved = jnp.where(yh_of == start, ahead(field, 4 * a), crossed)
            tap_ref[slot, a + 1, PAD : PAD + cells, :] = moved.astype(BF16)

    def tap(slot, a, b, step):
        start = PAD + 16 * b * step
        return tap_ref[slot, a + 1, start : start + cells, :]

    zeros = jnp.zeros((PAD, C), BF16)
    for slot in range(4):
        for a in range(3):
            tap_ref[slot, a, 0:PAD, :] = zeros
            tap_ref[slot, a, PAD + cells : 2 * PAD + cells, :] = zeros

    offsets = [(a, b) for a in (-1, 0, 1) for b in (-1, 0, 1)]

    def forward(slot, w_ref, step):
        total = None
        for t, (a, b) in enumerate(offsets):
            term = jnp.dot(
                tap(slot, a, b, step), w_ref[t * C : (t + 1) * C, :], preferred_element_type=F32
            )
            total = term if total is None else total + term
        return total

    def backward(slot, w_ref, step):
        total = None
        for t, (a, b) in enumerate(offsets):
            term = lax.dot_general(
                tap(slot, -a, -b, step),
                w_ref[t * C : (t + 1) * C, :],
                (((1,), (1,)), ((), ())),
                preferred_element_type=F32,
            )
            total = term if total is None else total + term
        return total

    def weight_grad(index, field, slot, step):
        turned = field.T
        for h in (0, 1):
            ft_ref[h] = turned[:, h * 128 : h * 128 + 128]
        left = jnp.concatenate(
            [
                jnp.concatenate([ft_ref[h, pl.ds(odd, 96, stride=2), :] for h in (0, 1)], axis=1)
                for odd in (0, 1)
            ],
            axis=0,
        ).astype(BF16)
        for t, (a, b) in enumerate(offsets):
            full = jnp.dot(left, tap(slot, -a, -b, step), preferred_element_type=F32)
            even, odd = full[0:96], full[96:192]
            lanes = (
                even[:, 0:128],
                jnp.concatenate([even[:, 128:192], odd[:, 0:64]], axis=1),
                odd[:, 64:192],
            )
            for q in range(3):
                for u in range(6):
                    wg_ref[index, pl.ds(t * 18 + q * 6 + u, 16, stride=ROWS), :] = lanes[q][
                        u * 16 : u * 16 + 16
                    ]

    x = unpack(0)
    g = unpack(1)
    gelu_one, slope_one = gelu_parts(x)
    act_one = gelu_one.astype(BF16).astype(F32)
    put_taps(0, act_one, 1)
    put_taps(2, g, 2)
    hidden = (x + forward(0, w1_ref, 1)).astype(BF16).astype(F32)
    gelu_two, slope_two = gelu_parts(hidden)
    act_two = gelu_two.astype(BF16).astype(F32)
    put_taps(1, act_two, 2)
    hidden_grad = (g + backward(2, w2_ref, 2) * slope_two).astype(BF16).astype(F32)
    put_taps(3, hidden_grad, 1)
    output = hidden + forward(1, w2_ref, 2)
    input_grad = hidden_grad + backward(3, w1_ref, 1) * slope_one
    tiles = pack(output) + pack(input_grad)
    for x in range(4):
        for yh in (0, 1):
            pieces = []
            for tile in tiles:
                for zh in range(4):
                    start = (x * 4 + zh) * 8 + yh * 4
                    pieces.append(tile[start : start + 4])
            o_ref[x * 2 + yh] = jnp.concatenate(pieces, axis=0).astype(BF16)
    for index in (0, 1):
        for c in range(16):
            wg_ref[index, c * ROWS + 162 : (c + 1) * ROWS, :] = jnp.zeros((ROWS - 162, 128), F32)
    weight_grad(0, act_two, 2, 2)
    weight_grad(1, act_one, 3, 1)
    core = where_ref[0]
    for c in range(16):
        keep_ref[c] = wg_ref[core, c * ROWS : (c + 1) * ROWS, :].astype(BF16)
        send_ref[c] = wg_ref[1 - core, c * ROWS : (c + 1) * ROWS, :].astype(BF16)


def join_kernel(f_ref, keep_ref, other_ref, o_ref):
    for c in range(16):
        o_ref[c, 0:FIELD, :] = f_ref[c % 8]
        pair = keep_ref[c].astype(F32) + other_ref[c].astype(F32)
        o_ref[c, FIELD : FIELD + ROWS, :] = pair.astype(BF16)


def line_kernel(where_ref, s_ref, o_ref, sum_ref, scr_ref):
    yl = where_ref[1]
    total = s_ref[0, FIELD : FIELD + ROWS, :].astype(F32)
    for c in range(1, 16):
        total = total + s_ref[c, FIELD : FIELD + ROWS, :].astype(F32)
    sum_ref[0:ROWS, :] = total
    sum_ref[ROWS : ROWS + 8, :] = jnp.zeros((8, 128), F32)
    for s in range(8):
        scr_ref[s * FIELD : (s + 1) * FIELD, :] = s_ref[yl * 8 + s, 0:FIELD, :].astype(F32)
    for z in range(16):
        tiles = [scr_ref[pl.ds(t * 16 + z, 8, stride=FIELD), :] for t in range(6)]
        tiles.append(sum_ref[z * 11 : z * 11 + 16, :])
        o_ref[z] = jnp.concatenate(tiles, axis=0).astype(BF16)


def split_kernel(r_ref, out_ref, ig_ref, z_ref):
    total = r_ref[0, 48:64, :].astype(F32)
    for z in range(1, 16):
        total = total + r_ref[z, 48:64, :].astype(F32)
    mine = (total * (1.0 / 256.0)).astype(BF16)
    for z in range(16):
        z_ref[z] = mine
    for z in range(16):
        value = r_ref[z, 0:48, :].astype(F32)
        wide = jnp.concatenate([value[t * 8 : t * 8 + 8] for t in range(6)], axis=1)
        for f, ref in enumerate((out_ref, ig_ref)):
            halves = [wide[:, (2 * f + k) * C : (2 * f + k + 1) * C] for k in (0, 1)]
            ref[:, z * C : (z + 1) * C] = jnp.concatenate(halves, axis=0).astype(BF16)


def spread_kernel(z_ref, out_ref, scr_ref):
    for z in range(16):
        scr_ref[z * 11 : z * 11 + 16, :] = z_ref[z].astype(F32)
    mine = scr_ref[0:ROWS, :].astype(BF16)
    for c in range(16):
        out_ref[c] = mine


def final_kernel(where_ref, own_ref, other_ref, one_ref, two_ref, scr_ref):
    core = where_ref[0]
    for c in range(16):
        scr_ref[core, c * ROWS : (c + 1) * ROWS, :] = own_ref[c].astype(F32)
        scr_ref[1 - core, c * ROWS : (c + 1) * ROWS, :] = other_ref[c].astype(F32)
    for index, ref in enumerate((two_ref, one_ref)):
        for n in range(288):
            m, q = n // 3, n % 3
            base = (m % 16) * ROWS + q * 6 + m // 16
            eight = scr_ref[index, pl.ds(base, 8, stride=18), :]
            nine = jnp.concatenate([eight, scr_ref[index, base + 144 : base + 145, :]], axis=0)
            ref[:, n * 128 : (n + 1) * 128] = nine.astype(BF16)


def exchange(value, axes):
    return lax.all_to_all(value, axes, split_axis=0, concat_axis=0, tiled=True)


def shape(*dims, dtype=BF16):
    return jax.ShapeDtypeStruct(dims, dtype)


def per_device(inputs, first_weight, second_weight, cotangent):
    smem, hbm, vmem = pltpu.SMEM, pltpu.HBM, pltpu.VMEM
    core = lax.axis_index("core").astype(jnp.int32).reshape(1)
    half = lax.axis_index("yl").astype(jnp.int32).reshape(1)
    swap = [(0, 1), (1, 0)]
    rows = vmem((1024, 128), F32)
    kernel_one = first_weight.reshape(9 * C, C)
    kernel_two = second_weight.reshape(9 * C, C)
    packed, where = call(
        pack_kernel,
        (shape(1024, 128), shape(2, dtype=jnp.int32)),
        scratch=(vmem((2, 16, 16 * C), BF16), rows, pltpu.SemaphoreType.DMA((2,))),
        spaces={0: smem, 1: smem, 2: hbm, 3: hbm},
        out_specs=(pl.BlockSpec(memory_space=vmem), pl.BlockSpec(memory_space=smem)),
        limit=63400000,
    )(core, half, inputs, cotangent)
    received = exchange(packed.reshape(128, 8, 128), PEERS).reshape(1024, 128)
    fields, keep, send = call(
        main_kernel,
        (shape(8, FIELD, 128), shape(16, ROWS, 128), shape(16, ROWS, 128)),
        scratch=(
            rows,
            vmem((4, 3, 256 + 2 * PAD, C), BF16),
            vmem((2, C, 128), F32),
            vmem((2, 16 * ROWS, 128), F32),
        ),
        spaces={0: smem},
    )(where, received, kernel_one, kernel_two)
    other = lax.ppermute(send, "core", swap)
    joined = call(join_kernel, shape(16, FIELD + ROWS, 128))(fields, keep, other)
    plane = exchange(joined, PLANE)
    to_line = call(
        line_kernel,
        shape(16, 64, 128),
        scratch=(vmem((ROWS + 8, 128), F32), vmem((8 * FIELD, 128), F32)),
        spaces={0: smem},
    )(where, plane)
    back = exchange(to_line, LINE)
    output, input_grad, mine = call(
        split_kernel, (shape(16, 16 * C), shape(16, 16 * C), shape(16, 16, 128))
    )(back)
    line = exchange(mine, LINE)
    spread = call(spread_kernel, shape(16, ROWS, 128), scratch=(vmem((ROWS + 8, 128), F32),))(line)
    gathered = exchange(spread, PLANE)
    partner = lax.ppermute(gathered, "core", swap)
    one, two = call(
        final_kernel,
        (shape(9, C * C), shape(9, C * C)),
        scratch=(vmem((2, 16 * ROWS, 128), F32),),
        spaces={0: smem},
    )(where, gathered, partner)
    return output, input_grad, one, two


def solution(mesh):
    grid = Mesh(mesh.devices.reshape(SIZES), AXES)
    tile = P(("zl", "yh", "yl"), ("x", "zh", "core"))
    return jax.shard_map(
        per_device,
        mesh=grid,
        in_specs=(tile, P(), P(), tile),
        out_specs=(tile, tile, P(), P()),
        check_vma=False,
    )
```

```python
import jax
import jax.numpy as jnp
from jax import lax
from jax.experimental import pallas as pl
from jax.experimental.pallas import tpu as pltpu
from jax.sharding import Mesh, PartitionSpec as P

C = 192
AXES = ("zl", "yh", "yl", "x", "zh", "core")
SIZES = (4, 2, 2, 4, 4, 2)
PEERS = ("x", "zh", "zl", "yh")
PLANE = ("yl", "x", "yh")
BF16 = jnp.bfloat16
F32 = jnp.float32
ROWS = 168
PITCH = 169
PAD = 32
CELLS = 256
OFFSETS = [(a, b) for a in (-1, 0, 1) for b in (-1, 0, 1)]


def call(kernel, out_shape, scratch=(), spaces={}, out_specs=None, limit=40 * 1024 * 1024):
    if out_specs is None:
        out_specs = jax.tree.map(lambda _: pl.BlockSpec(memory_space=pltpu.VMEM), out_shape)

    def run(*args):
        return pl.pallas_call(
            kernel,
            out_shape=out_shape,
            in_specs=[
                pl.BlockSpec(memory_space=spaces.get(n, pltpu.VMEM)) for n in range(len(args))
            ],
            out_specs=out_specs,
            scratch_shapes=list(scratch),
            compiler_params=pltpu.CompilerParams(vmem_limit_bytes=limit),
        )(*args)

    return run


def gelu_parts(value):
    normal_cdf = 0.5 * (1.0 + lax.erf(value * 0.7071067811865476))
    density = jnp.exp(-0.5 * value * value) * 0.3989422804014327
    return value * normal_cdf, normal_cdf + value * density


def pack_kernel(core_ref, x_hbm, g_hbm, o_ref, where_ref, in_ref, row_ref, sems):
    copies = [pltpu.make_async_copy(h, in_ref.at[n], sems.at[n]) for n, h in enumerate((x_hbm, g_hbm))]
    for copy in copies:
        copy.start()
    where_ref[0] = core_ref[0]
    for copy in copies:
        copy.wait()
    fields = [in_ref[n].astype(F32) for n in (0, 1)]
    for j in range(16):
        pieces = [f[k * 8 : k * 8 + 8, j * C : (j + 1) * C] for f in fields for k in (0, 1)]
        wide = jnp.concatenate(pieces, axis=1)
        for t in range(6):
            row_ref[pl.ds(j * 48 + t, 8, stride=6), :] = wide[:, t * 128 : t * 128 + 128]
    for j in range(16):
        o_ref[j * 48 : j * 48 + 48, :] = row_ref[j * 48 : j * 48 + 48, :].astype(BF16)


def put_taps(tap_ref, slot, field, step):
    within = lax.broadcasted_iota(jnp.int32, (CELLS, C), 0) % 8
    for a in (-1, 0, 1):
        moved = field
        if a != 0:
            rolled = pltpu.roll(field, (-a * step) % CELLS, 0)
            seen = (within + a * step >= 0) & (within + a * step < 8)
            moved = jnp.where(seen, rolled, 0.0)
        tap_ref[slot, a + 1, PAD : PAD + CELLS, :] = moved.astype(BF16)
    for a in range(3):
        tap_ref[slot, a, 0:PAD, :] = jnp.zeros((PAD, C), BF16)
        tap_ref[slot, a, PAD + CELLS : 2 * PAD + CELLS, :] = jnp.zeros((PAD, C), BF16)


def get_tap(tap_ref, slot, a, b, step):
    start = PAD + 16 * b * step
    return tap_ref[slot, a + 1, start : start + CELLS, :]


def main_kernel(where_ref, r_ref, w1_ref, w2_ref, o_ref, keep_ref, send_ref, row_ref, tap_ref, pair_ref):
    row_ref[...] = r_ref[...].astype(F32)

    def unpack(f):
        tiles = [row_ref[pl.ds(3 * f + t, 128, stride=6), :] for t in range(3)]
        part = jnp.concatenate(tiles, axis=1)
        both = [part[:, k * C : (k + 1) * C].reshape(16, 1, 8, C) for k in (0, 1)]
        return jnp.concatenate(both, axis=1).reshape(CELLS, C)

    def pack(value):
        split = value.reshape(16, 2, 8, C)
        return jnp.concatenate([split[:, k].reshape(128, C) for k in (0, 1)], axis=1)

    def forward(slot, w_ref, step):
        total = None
        for t, (a, b) in enumerate(OFFSETS):
            term = jnp.dot(
                get_tap(tap_ref, slot, a, b, step), w_ref[t * C : (t + 1) * C, :], preferred_element_type=F32
            )
            total = term if total is None else total + term
        return total

    def backward(slot, w_ref, step):
        total = None
        for t, (a, b) in enumerate(OFFSETS):
            term = lax.dot_general(
                get_tap(tap_ref, slot, -a, -b, step),
                w_ref[t * C : (t + 1) * C, :],
                (((1,), (1,)), ((), ())),
                preferred_element_type=F32,
            )
            total = term if total is None else total + term
        return total

    x = unpack(0)
    g = unpack(1)
    gelu_one, slope_one = gelu_parts(x)
    act_one = gelu_one.astype(BF16).astype(F32)
    put_taps(tap_ref, 0, act_one, 1)
    put_taps(tap_ref, 2, g, 2)
    hidden = (x + forward(0, w1_ref, 1)).astype(BF16).astype(F32)
    gelu_two, slope_two = gelu_parts(hidden)
    act_two = gelu_two.astype(BF16).astype(F32)
    put_taps(tap_ref, 1, act_two, 2)
    hidden_grad = (g + backward(2, w2_ref, 2) * slope_two).astype(BF16).astype(F32)
    put_taps(tap_ref, 3, hidden_grad, 1)
    output = hidden + forward(1, w2_ref, 2)
    input_grad = hidden_grad + backward(3, w1_ref, 1) * slope_one
    o_ref[...] = jnp.concatenate([pack(output), pack(input_grad)], axis=1).astype(BF16)
    for index, (act, grad) in enumerate(((act_two, g), (act_one, hidden_grad))):
        pair_ref[index, 0] = act[:, 0:128].astype(BF16)
        pair_ref[index, 1] = jnp.concatenate([act[:, 128:C], grad[:, 128:C]], axis=1).astype(BF16)
        pair_ref[index, 2] = grad[:, 0:128].astype(BF16)
    core = where_ref[0]
    keep_ref[...] = pair_ref[core]
    send_ref[...] = pair_ref[1 - core]


def weight_kernel(where_ref, own_ref, other_ref, o_ref, tap_ref, ft_ref, wg_ref):
    turned = []
    grads = []
    for ref in (own_ref, other_ref):
        first, mixed, last = [ref[n].astype(F32) for n in range(3)]
        turned.append(jnp.concatenate([first, mixed[:, 0:64]], axis=1).T)
        grads.append(jnp.concatenate([last, mixed[:, 64:128]], axis=1))
    for n in range(4):
        ft_ref[n] = turned[n // 2][:, (n % 2) * 128 : (n % 2) * 128 + 128]
    left = [
        jnp.concatenate(
            [
                jnp.concatenate(
                    [ft_ref[n, pl.ds(odd, 96, stride=2), :] for n in (2 * half, 2 * half + 1)], axis=1
                )
                for odd in (0, 1)
            ],
            axis=0,
        ).astype(BF16)
        for half in (0, 1)
    ]
    for c in range(16):
        wg_ref[c * ROWS + 162 : c * ROWS + 168, :] = jnp.zeros((6, 128), F32)

    def weight_grad(step):
        for half in (0, 1):
            put_taps(tap_ref, half, grads[half], step)
        for t, (a, b) in enumerate(OFFSETS):
            full = jnp.dot(left[0], get_tap(tap_ref, 0, -a, -b, step), preferred_element_type=F32)
            full = full + jnp.dot(
                left[1], get_tap(tap_ref, 1, -a, -b, step), preferred_element_type=F32
            )
            even, odd = full[0:96], full[96:192]
            lanes = (
                even[:, 0:128],
                jnp.concatenate([even[:, 128:192], odd[:, 0:64]], axis=1),
                odd[:, 64:192],
            )
            for q in range(3):
                for u in range(6):
                    wg_ref[pl.ds(t * 18 + q * 6 + u, 16, stride=ROWS), :] = lanes[q][
                        u * 16 : u * 16 + 16
                    ]

    for core, step in ((0, 2), (1, 1)):
        pl.when(where_ref[0] == core)(lambda step=step: weight_grad(step))
    for c in range(16):
        o_ref[c] = wg_ref[c * ROWS : (c + 1) * ROWS, :].astype(BF16)


def join_kernel(s_ref, f_ref, out_ref, sum_ref, row_ref):
    total = s_ref[0].astype(F32)
    for c in range(1, 16):
        total = total + s_ref[c].astype(F32)
    sum_ref[0:ROWS, :] = total
    sum_ref[ROWS : ROWS + 8, :] = jnp.zeros((8, 128), F32)
    value = f_ref[...].astype(F32)
    for t in range(6):
        row_ref[pl.ds(t, 128, stride=12), :] = value[:, t * 128 : t * 128 + 128]
    for x in range(4):
        for yh in range(2):
            t = x * 2 + yh
            for zl in range(4):
                first = t * 18 + zl * 6 if zl < 3 else 144 + t * 3
                piece = sum_ref[first : first + 6, :]
                for zh in range(4):
                    start = (x * 32 + zh * 8 + zl * 2 + yh) * 12 + 6
                    row_ref[start : start + 6, :] = piece
    out_ref[...] = row_ref[...].astype(BF16)


def split_kernel(r_ref, out_ref, ig_ref, z_ref, row_ref):
    row_ref[...] = r_ref[...].astype(F32)
    tiles = [row_ref[pl.ds(t, 128, stride=12), :] for t in range(12)]
    for f, ref in enumerate((out_ref, ig_ref)):
        wide = jnp.concatenate(tiles[3 * f : 3 * f + 3], axis=1)
        halves = []
        for k in (0, 1):
            part = wide[:, k * C : (k + 1) * C]
            halves.append(jnp.concatenate([part[j * 8 : j * 8 + 8] for j in range(16)], axis=1))
        ref[...] = jnp.concatenate(halves, axis=0).astype(BF16)
    row = lax.broadcasted_iota(jnp.int32, (8, 128), 0)
    slots = []
    for value in tiles[6:12]:
        total = jnp.zeros((8, 128), F32)
        for x in range(4):
            part = value[x * 32 : x * 32 + 8]
            for zh in range(1, 4):
                part = part + value[x * 32 + zh * 8 : x * 32 + zh * 8 + 8]
            part = part + pltpu.roll(part, 4, 0)
            part = part + pltpu.roll(part, 2, 0)
            total = jnp.where(row // 2 == x, part, total)
        slots.append(total * (1.0 / 256.0))
    mine = jnp.concatenate(slots, axis=0).astype(BF16)
    for z in range(4):
        z_ref[z] = mine


def spread_kernel(z_ref, out_ref):
    mine = jnp.concatenate([z_ref[0], z_ref[1], z_ref[2], z_ref[3, 0:32, :]], axis=0)
    for c in range(16):
        out_ref[c, 0:160, :] = mine[0:160]
        out_ref[c, 160:168, :] = z_ref[3, 16:32, :][0:8]


def final_kernel(where_ref, own_ref, other_ref, one_ref, two_ref, scr_ref):
    core = where_ref[0]
    for c in range(16):
        scr_ref[core, c * PITCH : c * PITCH + ROWS, :] = own_ref[c].astype(F32)
        scr_ref[1 - core, c * PITCH : c * PITCH + ROWS, :] = other_ref[c].astype(F32)
    for index, ref in enumerate((two_ref, one_ref)):
        for n in range(288):
            m, q = n // 3, n % 3
            u, c = m // 16, m % 16
            v = q * 6 + u
            first = (c // 8) * 8 * PITCH + c % 8
            eight = scr_ref[index, pl.ds(first + v * 8, 8, stride=PITCH), :]
            last = first + (v // 3) * PITCH + (18 + v % 3) * 8
            nine = jnp.concatenate([eight, scr_ref[index, last : last + 1, :]], axis=0)
            ref[:, n * 128 : (n + 1) * 128] = nine.astype(BF16)


def exchange(value, axes):
    return lax.all_to_all(value, axes, split_axis=0, concat_axis=0, tiled=True)


def shape(*dims, dtype=BF16):
    return jax.ShapeDtypeStruct(dims, dtype)


def per_device(inputs, first_weight, second_weight, cotangent):
    smem, hbm, vmem = pltpu.SMEM, pltpu.HBM, pltpu.VMEM
    core = lax.axis_index("core").astype(jnp.int32).reshape(1)
    swap = [(0, 1), (1, 0)]
    kernel_one = first_weight.reshape(9 * C, C)
    kernel_two = second_weight.reshape(9 * C, C)
    packed, where = call(
        pack_kernel,
        (shape(768, 128), shape(1, dtype=jnp.int32)),
        scratch=(
            vmem((2, 16, 16 * C), BF16),
            vmem((768, 128), F32),
            pltpu.SemaphoreType.DMA((2,)),
        ),
        spaces={0: smem, 1: hbm, 2: hbm},
        out_specs=(pl.BlockSpec(memory_space=vmem), pl.BlockSpec(memory_space=smem)),
        limit=63400000,
    )(core, inputs, cotangent)
    received = exchange(packed.reshape(384, 2, 128), PEERS).reshape(768, 128)
    fields, keep, send = call(
        main_kernel,
        (shape(128, 768), shape(3, CELLS, 128), shape(3, CELLS, 128)),
        scratch=(
            vmem((768, 128), F32),
            vmem((4, 3, CELLS + 2 * PAD, C), BF16),
            vmem((2, 3, CELLS, 128), BF16),
        ),
        spaces={0: smem},
    )(where, received, kernel_one, kernel_two)
    other = lax.ppermute(send, "core", swap)
    terms = call(
        weight_kernel,
        shape(16, ROWS, 128),
        scratch=(
            vmem((2, 3, CELLS + 2 * PAD, C), BF16),
            vmem((4, C, 128), F32),
            vmem((16 * ROWS, 128), F32),
        ),
        spaces={0: smem},
    )(where, keep, other)
    plane = exchange(terms, PLANE)
    joined = call(
        join_kernel, shape(1536, 128), scratch=(vmem((ROWS + 8, 128), F32), vmem((1536, 128), F32))
    )(plane, fields)
    back = exchange(joined.reshape(384, 4, 128), PEERS).reshape(1536, 128)
    output, input_grad, mine = call(
        split_kernel,
        (shape(16, 16 * C), shape(16, 16 * C), shape(4, 48, 128)),
        scratch=(vmem((1536, 128), F32),),
    )(back)
    line = exchange(mine, "zl")
    spread = call(spread_kernel, shape(16, ROWS, 128))(line)
    gathered = exchange(spread, PLANE)
    partner = lax.ppermute(gathered, "core", swap)
    one, two = call(
        final_kernel,
        (shape(9, C * C), shape(9, C * C)),
        scratch=(vmem((2, 16 * PITCH, 128), F32),),
        spaces={0: smem},
    )(where, gathered, partner)
    return output, input_grad, one, two


def solution(mesh):
    grid = Mesh(mesh.devices.reshape(SIZES), AXES)
    tile = P(("zl", "yh", "yl"), ("x", "zh", "core"))
    return jax.shard_map(
        per_device,
        mesh=grid,
        in_specs=(tile, P(), P(), tile),
        out_specs=(tile, tile, P(), P()),
        check_vma=False,
    )
```

```python
import functools

import jax
import jax.numpy as jnp
from jax import lax
from jax.experimental import pallas as pl
from jax.experimental.pallas import tpu as pltpu
from jax.sharding import Mesh, PartitionSpec as P

C = 192
AXES = ("zl", "yh", "yl", "x", "zh", "core")
SIZES = (4, 2, 2, 4, 4, 2)
PEERS = ("zh", "zl", "x", "yh")
PLANE = ("yl", "x", "yh")
BF16 = jnp.bfloat16
F32 = jnp.float32
ROWS = 168
TERMS = 162
PITCH = 169
ZH = 64
PAD = 2 * ZH
CELLS = 256
OFFSETS = [(a, b) for a in (-1, 0, 1) for b in (-1, 0, 1)]


def call(kernel, out_shape, scratch=(), spaces={}, out_specs=None, limit=40 * 1024 * 1024, **extra):
    if out_specs is None:
        out_specs = jax.tree.map(lambda _: pl.BlockSpec(memory_space=pltpu.VMEM), out_shape)

    def run(*args):
        return pl.pallas_call(
            kernel,
            out_shape=out_shape,
            in_specs=[
                pl.BlockSpec(memory_space=spaces.get(n, pltpu.VMEM)) for n in range(len(args))
            ],
            out_specs=out_specs,
            scratch_shapes=list(scratch),
            compiler_params=pltpu.CompilerParams(vmem_limit_bytes=limit),
            **extra,
        )(*args)

    return run


def gelu_parts(value):
    normal_cdf = 0.5 * (1.0 + lax.erf(value * 0.7071067811865476))
    density = jnp.exp(-0.5 * value * value) * 0.3989422804014327
    return value * normal_cdf, normal_cdf + value * density


def pack_kernel(core_ref, x_hbm, g_hbm, o_ref, where_ref, in_ref, row_ref, sems):
    copies = [pltpu.make_async_copy(h, in_ref.at[n], sems.at[n]) for n, h in enumerate((x_hbm, g_hbm))]
    for copy in copies:
        copy.start()
    where_ref[0] = core_ref[0]
    for copy in copies:
        copy.wait()
    fields = [in_ref[n].astype(F32) for n in (0, 1)]
    for j in range(16):
        pieces = [f[k * 8 : k * 8 + 8, j * C : (j + 1) * C] for f in fields for k in (0, 1)]
        wide = jnp.concatenate(pieces, axis=1)
        for t in range(6):
            row_ref[pl.ds(j * 48 + t, 8, stride=6), :] = wide[:, t * 128 : t * 128 + 128]
    for j in range(16):
        o_ref[j * 48 : j * 48 + 48, :] = row_ref[j * 48 : j * 48 + 48, :].astype(BF16)


def put_taps(tap_ref, slot, field, step):
    row = lax.broadcasted_iota(jnp.int32, (CELLS, C), 0)
    zl_of, x_of, yh_of = (row // 16) % 4, (row % 8) // 2, row % 2

    def ahead(value, rows):
        return pltpu.roll(value, (-rows) % CELLS, 0)

    more = step * ZH
    for a in (-1, 0, 1):
        moved = field
        if a != 0:
            inside = (zl_of + a >= 0) & (zl_of + a < 4)
            if step == 2:
                moved = jnp.where(inside, ahead(field, 16 * a), 0.0)
            else:
                crossed = jnp.where(inside, ahead(field, 15 * a), 0.0)
                moved = jnp.where(yh_of == (0 if a == 1 else 1), ahead(field, a), crossed)
        before = jnp.where(x_of > 0, ahead(moved, -2), 0.0)[CELLS - more :]
        after = jnp.where(x_of < 3, ahead(moved, 2), 0.0)[:more]
        tap_ref[slot, a + 1, PAD - more : PAD, :] = before.astype(BF16)
        tap_ref[slot, a + 1, PAD : PAD + CELLS, :] = moved.astype(BF16)
        tap_ref[slot, a + 1, PAD + CELLS : PAD + CELLS + more, :] = after.astype(BF16)


def get_tap(tap_ref, slot, a, b, step):
    start = PAD + ZH * b * step
    return tap_ref[slot, a + 1, start : start + CELLS, :]


def main_kernel(where_ref, r_ref, w1_ref, w2_ref, o_ref, keep_ref, send_ref, row_ref, tap_ref, pair_ref):
    row_ref[...] = r_ref[...].astype(F32)

    def unpack(f):
        tiles = [row_ref[pl.ds(3 * f + t, 128, stride=6), :] for t in range(3)]
        part = jnp.concatenate(tiles, axis=1)
        both = [part[:, k * C : (k + 1) * C].reshape(16, 1, 8, C) for k in (0, 1)]
        return jnp.concatenate(both, axis=1).reshape(CELLS, C)

    def pack(value):
        split = value.reshape(16, 2, 8, C)
        return jnp.concatenate([split[:, k].reshape(128, C) for k in (0, 1)], axis=1)

    def forward(slot, w_ref, step):
        total = None
        for t, (a, b) in enumerate(OFFSETS):
            term = jnp.dot(
                get_tap(tap_ref, slot, a, b, step), w_ref[t * C : (t + 1) * C, :], preferred_element_type=F32
            )
            total = term if total is None else total + term
        return total

    def backward(slot, w_ref, step):
        total = None
        for t, (a, b) in enumerate(OFFSETS):
            term = lax.dot_general(
                get_tap(tap_ref, slot, -a, -b, step),
                w_ref[t * C : (t + 1) * C, :],
                (((1,), (1,)), ((), ())),
                preferred_element_type=F32,
            )
            total = term if total is None else total + term
        return total

    x = unpack(0)
    g = unpack(1)
    gelu_one, slope_one = gelu_parts(x)
    act_one = gelu_one.astype(BF16).astype(F32)
    put_taps(tap_ref, 0, act_one, 1)
    put_taps(tap_ref, 2, g, 2)
    hidden = (x + forward(0, w1_ref, 1)).astype(BF16).astype(F32)
    gelu_two, slope_two = gelu_parts(hidden)
    act_two = gelu_two.astype(BF16).astype(F32)
    put_taps(tap_ref, 1, act_two, 2)
    hidden_grad = (g + backward(2, w2_ref, 2) * slope_two).astype(BF16).astype(F32)
    put_taps(tap_ref, 3, hidden_grad, 1)
    output = hidden + forward(1, w2_ref, 2)
    input_grad = hidden_grad + backward(3, w1_ref, 1) * slope_one
    o_ref[...] = jnp.concatenate([pack(output), pack(input_grad)], axis=1).astype(BF16)
    for index, (act, grad) in enumerate(((act_two, g), (act_one, hidden_grad))):
        pair_ref[index, 0] = act[:, 0:128].astype(BF16)
        pair_ref[index, 1] = jnp.concatenate([act[:, 128:C], grad[:, 128:C]], axis=1).astype(BF16)
        pair_ref[index, 2] = grad[:, 0:128].astype(BF16)
    core = where_ref[0]
    keep_ref[...] = pair_ref[core]
    send_ref[...] = pair_ref[1 - core]


def half_kernel(own, where_ref, pair_ref, *refs):
    o_ref, tap_ref, ft_ref = refs[-4:-1] if not own else refs[-3:]
    first, mixed, last = [pair_ref[n].astype(F32) for n in range(3)]
    turned = jnp.concatenate([first, mixed[:, 0:64]], axis=1).T
    grad = jnp.concatenate([last, mixed[:, 64:128]], axis=1)
    for n in (0, 1):
        ft_ref[n] = turned[:, n * 128 : n * 128 + 128]
    left = jnp.concatenate(
        [
            jnp.concatenate([ft_ref[n, pl.ds(odd, 96, stride=2), :] for n in (0, 1)], axis=1)
            for odd in (0, 1)
        ],
        axis=0,
    ).astype(BF16)

    def weight_grad(step):
        put_taps(tap_ref, 0, grad, step)
        for t, (a, b) in enumerate(OFFSETS):
            full = jnp.dot(left, get_tap(tap_ref, 0, -a, -b, step), preferred_element_type=F32)
            if own:
                o_ref[t] = full
                continue
            full = full + refs[0][t]
            even, odd = full[0:96], full[96:192]
            lanes = (
                even[:, 0:128],
                jnp.concatenate([even[:, 128:192], odd[:, 0:64]], axis=1),
                odd[:, 64:192],
            )
            wg_ref = refs[-1]
            for q in range(3):
                for u in range(6):
                    wg_ref[pl.ds(t * 18 + q * 6 + u, 16, stride=TERMS), :] = lanes[q][
                        u * 16 : u * 16 + 16
                    ]

    for core, step in ((0, 2), (1, 1)):
        pl.when(where_ref[0] == core)(lambda step=step: weight_grad(step))
    if not own:
        o_ref[...] = refs[-1][...].astype(BF16)


def join_kernel(s_ref, f_ref, out_ref, sum_ref, row_ref, part_ref):
    part_ref[0 : 16 * TERMS, :] = s_ref[...].astype(F32)
    part_ref[16 * TERMS : 16 * TERMS + 8, :] = jnp.zeros((8, 128), F32)
    total = part_ref[0:ROWS, :]
    for c in range(1, 16):
        total = total + part_ref[c * TERMS : c * TERMS + ROWS, :]
    sum_ref[0:ROWS, :] = total
    sum_ref[ROWS : ROWS + 8, :] = jnp.zeros((8, 128), F32)
    value = f_ref[...].astype(F32)
    for t in range(6):
        row_ref[pl.ds(t, 128, stride=12), :] = value[:, t * 128 : t * 128 + 128]
    for x in range(4):
        for yh in range(2):
            t = x * 2 + yh
            for zl in range(4):
                first = t * 18 + zl * 6 if zl < 3 else 144 + t * 3
                piece = sum_ref[first : first + 6, :]
                for zh in range(4):
                    start = ((zh * 4 + zl) * 8 + t) * 12 + 6
                    row_ref[start : start + 6, :] = piece
    out_ref[...] = row_ref[...].astype(BF16)


def line_kernel(r_ref, z_ref, row_ref):
    row_ref[...] = r_ref[...].astype(F32)
    slots = []
    for t in range(6, 12):
        value = row_ref[pl.ds(t, 128, stride=12), :]
        total = value[0:8]
        for z in range(1, 16):
            total = total + value[z * 8 : z * 8 + 8]
        slots.append(total * (1.0 / 256.0))
    mine = jnp.concatenate(slots, axis=0).astype(BF16)
    for z in range(4):
        z_ref[z] = mine


def tile_kernel(r_ref, out_ref, ig_ref, row_ref):
    row_ref[...] = r_ref[...].astype(F32)
    for f, ref in enumerate((out_ref, ig_ref)):
        tiles = [row_ref[pl.ds(3 * f + t, 128, stride=12), :] for t in range(3)]
        wide = jnp.concatenate(tiles, axis=1)
        halves = []
        for k in (0, 1):
            part = wide[:, k * C : (k + 1) * C]
            halves.append(jnp.concatenate([part[j * 8 : j * 8 + 8] for j in range(16)], axis=1))
        ref[...] = jnp.concatenate(halves, axis=0).astype(BF16)


def spread_kernel(z_ref, out_ref):
    mine = jnp.concatenate([z_ref[0], z_ref[1], z_ref[2], z_ref[3, 0:32, :]], axis=0)
    for c in range(16):
        out_ref[c, 0:160, :] = mine[0:160]
        out_ref[c, 160:168, :] = z_ref[3, 16:32, :][0:8]


def final_kernel(own, where_ref, r_ref, *refs):
    one_ref, two_ref, out_ref, scr_ref, sems = refs[-5:]
    for c in range(16):
        scr_ref[c * PITCH : c * PITCH + ROWS, :] = r_ref[c].astype(F32)
    def each_copy(part, act):
        lanes = pl.ds(part * 9216, 9216)
        for core in (0, 1):
            target = two_ref if (core == 0) == own else one_ref

            @pl.when(where_ref[0] == core)
            def _(target=target):
                act(
                    pltpu.make_async_copy(
                        out_ref.at[:, lanes], target.at[:, lanes], sems.at[part]
                    )
                )

    for n in range(288):
        m, q = n // 3, n % 3
        u, c = m // 16, m % 16
        v = q * 6 + u
        first = (c // 8) * 8 * PITCH + c % 8
        eight = scr_ref[pl.ds(first + v * 8, 8, stride=PITCH), :]
        last = first + (v // 3) * PITCH + (18 + v % 3) * 8
        nine = jnp.concatenate([eight, scr_ref[last : last + 1, :]], axis=0)
        out_ref[:, n * 128 : (n + 1) * 128] = nine.astype(BF16)
        if n % 72 == 71:
            each_copy(n // 72, lambda copy: copy.start())
    for part in range(4):
        each_copy(part, lambda copy: copy.wait())


def exchange(value, axes):
    return lax.all_to_all(value, axes, split_axis=0, concat_axis=0, tiled=True)


def shape(*dims, dtype=BF16):
    return jax.ShapeDtypeStruct(dims, dtype)


def per_device(inputs, first_weight, second_weight, cotangent):
    smem, hbm, vmem = pltpu.SMEM, pltpu.HBM, pltpu.VMEM
    core = lax.axis_index("core").astype(jnp.int32).reshape(1)
    swap = [(0, 1), (1, 0)]
    short = pl.CostEstimate(flops=10**9, bytes_accessed=3 * 10**6, transcendentals=0)
    kernel_one = first_weight.reshape(9 * C, C)
    kernel_two = second_weight.reshape(9 * C, C)
    packed, where = call(
        pack_kernel,
        (shape(768, 128), shape(1, dtype=jnp.int32)),
        scratch=(
            vmem((2, 16, 16 * C), BF16),
            vmem((768, 128), F32),
            pltpu.SemaphoreType.DMA((2,)),
        ),
        spaces={0: smem, 1: hbm, 2: hbm},
        out_specs=(pl.BlockSpec(memory_space=vmem), pl.BlockSpec(memory_space=smem)),
        limit=63400000,
    )(core, inputs, cotangent)
    received = exchange(packed.reshape(384, 2, 128), PEERS).reshape(768, 128)
    fields, keep, send = call(
        main_kernel,
        (shape(128, 768), shape(3, CELLS, 128), shape(3, CELLS, 128)),
        scratch=(
            vmem((768, 128), F32),
            vmem((4, 3, CELLS + 2 * PAD, C), BF16),
            vmem((2, 3, CELLS, 128), BF16),
        ),
        spaces={0: smem},
    )(where, received, kernel_one, kernel_two)
    other = lax.ppermute(send, "core", swap)
    scratch = (vmem((1, 3, CELLS + 2 * PAD, C), BF16), vmem((2, C, 128), F32))
    begun = call(
        functools.partial(half_kernel, True),
        shape(9, C, C, dtype=F32),
        scratch=scratch,
        spaces={0: smem},
        cost_estimate=short,
    )(where, keep)
    terms = call(
        functools.partial(half_kernel, False),
        shape(16 * TERMS, 128),
        scratch=(*scratch, vmem((16 * TERMS, 128), F32)),
        spaces={0: smem},
    )(where, other, begun)
    plane = exchange(terms.reshape(8 * TERMS, 2, 128), PLANE).reshape(16 * TERMS, 128)
    joined = call(
        join_kernel,
        shape(1536, 128),
        scratch=(
            vmem((ROWS + 8, 128), F32),
            vmem((1536, 128), F32),
            vmem((16 * TERMS + 8, 128), F32),
        ),
    )(plane, fields)
    back = exchange(joined.reshape(384, 4, 128), PEERS).reshape(1536, 128)
    mine = call(line_kernel, shape(4, 48, 128), scratch=(vmem((1536, 128), F32),))(back)
    line = exchange(mine, "zl")
    spread = call(spread_kernel, shape(16, ROWS, 128))(line)
    gathered = exchange(spread, PLANE)
    partner = lax.ppermute(gathered, "core", swap)
    output, input_grad = call(
        tile_kernel,
        (shape(16, 16 * C), shape(16, 16 * C)),
        scratch=(vmem((1536, 128), F32),),
        cost_estimate=short,
    )(back)
    weight = shape(9, C * C)
    anywhere = pl.BlockSpec(memory_space=pl.ANY)
    scratch = (vmem((9, C * C), BF16), vmem((16 * PITCH, 128), F32), pltpu.SemaphoreType.DMA((4,)))
    one, two = call(
        functools.partial(final_kernel, True),
        (weight, weight),
        scratch=scratch,
        spaces={0: smem},
        out_specs=(anywhere, anywhere),
        cost_estimate=short,
    )(where, gathered)
    one, two = call(
        functools.partial(final_kernel, False),
        (weight, weight),
        scratch=scratch,
        spaces={0: smem, 2: pl.ANY, 3: pl.ANY},
        out_specs=(anywhere, anywhere),
        input_output_aliases={2: 0, 3: 1},
    )(where, partner, one, two)
    return output, input_grad, one, two


def solution(mesh):
    grid = Mesh(mesh.devices.reshape(SIZES), AXES)
    tile = P(("zl", "yh", "yl"), ("x", "zh", "core"))
    return jax.shard_map(
        per_device,
        mesh=grid,
        in_specs=(tile, P(), P(), tile),
        out_specs=(tile, tile, P(), P()),
        check_vma=False,
    )
```

```python
import functools

import jax
import jax.numpy as jnp
from jax import lax
from jax.experimental import pallas as pl
from jax.experimental.pallas import tpu as pltpu
from jax.sharding import Mesh, PartitionSpec as P

C = 192
AXES = ("zl", "yh", "yl", "x", "zh", "core")
SIZES = (4, 2, 2, 4, 4, 2)
PEERS = ("zh", "zl", "x", "yh")
PLANE = ("yl", "x", "yh")
LINE = ("zh", "zl")
BF16 = jnp.bfloat16
F32 = jnp.float32
ROWS = 168
TERMS = 162
FIELD = 96
BOTH = TERMS + FIELD
PIECE = 41
LINE_ROWS = 48 + PIECE + 1
ZH = 64
PAD = 2 * ZH
CELLS = 256
OFFSETS = [(a, b) for a in (-1, 0, 1) for b in (-1, 0, 1)]


def call(kernel, out_shape, scratch=(), spaces={}, out_specs=None, limit=40 * 1024 * 1024, **extra):
    if out_specs is None:
        out_specs = jax.tree.map(lambda _: pl.BlockSpec(memory_space=pltpu.VMEM), out_shape)

    def run(*args):
        return pl.pallas_call(
            kernel,
            out_shape=out_shape,
            in_specs=[
                pl.BlockSpec(memory_space=spaces.get(n, pltpu.VMEM)) for n in range(len(args))
            ],
            out_specs=out_specs,
            scratch_shapes=list(scratch),
            compiler_params=pltpu.CompilerParams(vmem_limit_bytes=limit),
            **extra,
        )(*args)

    return run


def gelu_parts(value):
    normal_cdf = 0.5 * (1.0 + lax.erf(value * 0.7071067811865476))
    density = jnp.exp(-0.5 * value * value) * 0.3989422804014327
    return value * normal_cdf, normal_cdf + value * density


def pack_kernel(core_ref, half_ref, x_hbm, g_hbm, o_ref, where_ref, in_ref, row_ref, sems):
    copies = [pltpu.make_async_copy(h, in_ref.at[n], sems.at[n]) for n, h in enumerate((x_hbm, g_hbm))]
    for copy in copies:
        copy.start()
    where_ref[0] = core_ref[0]
    where_ref[1] = half_ref[0]
    for copy in copies:
        copy.wait()
    fields = [in_ref[n].astype(F32) for n in (0, 1)]
    for j in range(16):
        pieces = [f[k * 8 : k * 8 + 8, j * C : (j + 1) * C] for f in fields for k in (0, 1)]
        wide = jnp.concatenate(pieces, axis=1)
        for t in range(6):
            row_ref[pl.ds(j * 48 + t, 8, stride=6), :] = wide[:, t * 128 : t * 128 + 128]
    for j in range(16):
        o_ref[j * 48 : j * 48 + 48, :] = row_ref[j * 48 : j * 48 + 48, :].astype(BF16)


def put_taps(tap_ref, slot, field, step):
    row = lax.broadcasted_iota(jnp.int32, (CELLS, C), 0)
    zl_of, x_of, yh_of = (row // 16) % 4, (row % 8) // 2, row % 2

    def ahead(value, rows):
        return pltpu.roll(value, (-rows) % CELLS, 0)

    more = step * ZH
    for a in (-1, 0, 1):
        moved = field
        if a != 0:
            inside = (zl_of + a >= 0) & (zl_of + a < 4)
            if step == 2:
                moved = jnp.where(inside, ahead(field, 16 * a), 0.0)
            else:
                crossed = jnp.where(inside, ahead(field, 15 * a), 0.0)
                moved = jnp.where(yh_of == (0 if a == 1 else 1), ahead(field, a), crossed)
        before = jnp.where(x_of > 0, ahead(moved, -2), 0.0)[CELLS - more :]
        after = jnp.where(x_of < 3, ahead(moved, 2), 0.0)[:more]
        tap_ref[slot, a + 1, PAD - more : PAD, :] = before.astype(BF16)
        tap_ref[slot, a + 1, PAD : PAD + CELLS, :] = moved.astype(BF16)
        tap_ref[slot, a + 1, PAD + CELLS : PAD + CELLS + more, :] = after.astype(BF16)


def get_tap(tap_ref, slot, a, b, step):
    start = PAD + ZH * b * step
    return tap_ref[slot, a + 1, start : start + CELLS, :]


def main_kernel(where_ref, r_ref, w1_ref, w2_ref, o_ref, keep_ref, send_ref, row_ref, tap_ref, pair_ref):
    row_ref[...] = r_ref[...].astype(F32)

    def unpack(f):
        tiles = [row_ref[pl.ds(3 * f + t, 128, stride=6), :] for t in range(3)]
        part = jnp.concatenate(tiles, axis=1)
        both = [part[:, k * C : (k + 1) * C].reshape(16, 1, 8, C) for k in (0, 1)]
        return jnp.concatenate(both, axis=1).reshape(CELLS, C)

    def pack(value):
        split = value.reshape(16, 2, 8, C)
        return jnp.concatenate([split[:, k].reshape(128, C) for k in (0, 1)], axis=1)

    def forward(slot, w_ref, step):
        total = None
        for t, (a, b) in enumerate(OFFSETS):
            term = jnp.dot(
                get_tap(tap_ref, slot, a, b, step), w_ref[t * C : (t + 1) * C, :], preferred_element_type=F32
            )
            total = term if total is None else total + term
        return total

    def backward(slot, w_ref, step):
        total = None
        for t, (a, b) in enumerate(OFFSETS):
            term = lax.dot_general(
                get_tap(tap_ref, slot, -a, -b, step),
                w_ref[t * C : (t + 1) * C, :],
                (((1,), (1,)), ((), ())),
                preferred_element_type=F32,
            )
            total = term if total is None else total + term
        return total

    x = unpack(0)
    g = unpack(1)
    gelu_one, slope_one = gelu_parts(x)
    act_one = gelu_one.astype(BF16).astype(F32)
    put_taps(tap_ref, 0, act_one, 1)
    put_taps(tap_ref, 2, g, 2)
    hidden = (x + forward(0, w1_ref, 1)).astype(BF16).astype(F32)
    gelu_two, slope_two = gelu_parts(hidden)
    act_two = gelu_two.astype(BF16).astype(F32)
    put_taps(tap_ref, 1, act_two, 2)
    hidden_grad = (g + backward(2, w2_ref, 2) * slope_two).astype(BF16).astype(F32)
    put_taps(tap_ref, 3, hidden_grad, 1)
    output = hidden + forward(1, w2_ref, 2)
    input_grad = hidden_grad + backward(3, w1_ref, 1) * slope_one
    wide = jnp.concatenate([pack(output), pack(input_grad)], axis=1)
    for t in range(6):
        row_ref[t * 128 : t * 128 + 128, :] = wide[:, t * 128 : t * 128 + 128]
    for e in range(8):
        tiles = [row_ref[pl.ds(t * 128 + e, 16, stride=8), :] for t in range(6)]
        o_ref[e * FIELD : (e + 1) * FIELD, :] = jnp.concatenate(tiles, axis=0).astype(BF16)
    for index, (act, grad) in enumerate(((act_two, g), (act_one, hidden_grad))):
        pair_ref[index, 0] = act[:, 0:128].astype(BF16)
        pair_ref[index, 1] = jnp.concatenate([act[:, 128:C], grad[:, 128:C]], axis=1).astype(BF16)
        pair_ref[index, 2] = grad[:, 0:128].astype(BF16)
    core = where_ref[0]
    keep_ref[...] = pair_ref[core]
    send_ref[...] = pair_ref[1 - core]


def half_kernel(own, where_ref, pair_ref, *refs):
    o_ref, tap_ref, ft_ref = refs[-4:-1] if not own else refs[-3:]
    if not own:
        for c in range(16):
            piece = refs[1][(c % 8) * FIELD : (c % 8 + 1) * FIELD, :].astype(F32)
            refs[-1][c * BOTH + TERMS : (c + 1) * BOTH, :] = piece
    first, mixed, last = [pair_ref[n].astype(F32) for n in range(3)]
    turned = jnp.concatenate([first, mixed[:, 0:64]], axis=1).T
    grad = jnp.concatenate([last, mixed[:, 64:128]], axis=1)
    for n in (0, 1):
        ft_ref[n] = turned[:, n * 128 : n * 128 + 128]
    left = jnp.concatenate(
        [
            jnp.concatenate([ft_ref[n, pl.ds(odd, 96, stride=2), :] for n in (0, 1)], axis=1)
            for odd in (0, 1)
        ],
        axis=0,
    ).astype(BF16)

    def weight_grad(step):
        put_taps(tap_ref, 0, grad, step)
        for t, (a, b) in enumerate(OFFSETS):
            full = jnp.dot(left, get_tap(tap_ref, 0, -a, -b, step), preferred_element_type=F32)
            if own:
                o_ref[t] = full
                continue
            full = full + refs[0][t]
            even, odd = full[0:96], full[96:192]
            lanes = (
                even[:, 0:128],
                jnp.concatenate([even[:, 128:192], odd[:, 0:64]], axis=1),
                odd[:, 64:192],
            )
            wg_ref = refs[-1]
            for q in range(3):
                for u in range(6):
                    wg_ref[pl.ds(t * 18 + q * 6 + u, 16, stride=BOTH), :] = lanes[q][
                        u * 16 : u * 16 + 16
                    ]

    for core, step in ((0, 2), (1, 1)):
        pl.when(where_ref[0] == core)(lambda step=step: weight_grad(step))
    if not own:
        o_ref[...] = refs[-1][...].astype(BF16)


def line_kernel(where_ref, s_ref, out_ref, part_ref, sum_ref, row_ref):
    part_ref[0 : 16 * BOTH, :] = s_ref[...].astype(F32)
    total = part_ref[0:ROWS, :]
    for c in range(1, 16):
        total = total + part_ref[c * BOTH : c * BOTH + ROWS, :]
    sum_ref[...] = total
    for zl in range(4):
        piece = sum_ref[zl * PIECE : zl * PIECE + PIECE + 1, :]
        for zh in range(4):
            start = (zh * 4 + zl) * LINE_ROWS + 48
            row_ref[start : start + PIECE + 1, :] = piece
    for half in (0, 1):

        @pl.when(where_ref[1] == half)
        def _():
            for z in range(16):
                for t in range(6):
                    first = half * 8 * BOTH + TERMS + t * 16 + z
                    row_ref[z * LINE_ROWS + t * 8 : z * LINE_ROWS + t * 8 + 8, :] = part_ref[
                        pl.ds(first, 8, stride=BOTH), :
                    ]

    out_ref[...] = row_ref[...].astype(BF16)


def sum_kernel(r_ref, z_ref, row_ref):
    row_ref[0 : 16 * LINE_ROWS, :] = r_ref[...].astype(F32)
    row_ref[16 * LINE_ROWS :, :] = jnp.zeros((8, 128), F32)
    total = row_ref[48:96, :]
    for z in range(1, 16):
        total = total + row_ref[z * LINE_ROWS + 48 : z * LINE_ROWS + 96, :]
    mine = (total * (1.0 / 256.0)).astype(BF16)
    for z in range(4):
        z_ref[z] = mine


def tile_kernel(r_ref, out_ref, ig_ref, row_ref):
    row_ref[...] = r_ref[...].astype(F32)
    for f, ref in enumerate((out_ref, ig_ref)):
        halves = []
        for k in (0, 1):
            parts = []
            for z in range(16):
                tiles = [
                    row_ref[z * LINE_ROWS + (3 * f + t) * 8 : z * LINE_ROWS + (3 * f + t) * 8 + 8, :]
                    for t in (k, k + 1)
                ]
                both = jnp.concatenate(tiles, axis=1)
                parts.append(both[:, k * 64 : k * 64 + C])
            halves.append(jnp.concatenate(parts, axis=1))
        ref[...] = jnp.concatenate(halves, axis=0).astype(BF16)


def spread_kernel(z_ref, out_ref, row_ref):
    for z in range(4):
        row_ref[z * PIECE : z * PIECE + 48, :] = z_ref[z].astype(F32)
    mine = row_ref[0:ROWS, :].astype(BF16)
    for c in range(16):
        out_ref[c] = mine


def final_kernel(own, where_ref, r_ref, *refs):
    one_ref, two_ref, out_ref, scr_ref, sems = refs[-5:]
    for c in range(16):
        scr_ref[c * ROWS : (c + 1) * ROWS, :] = r_ref[c].astype(F32)
    def each_copy(part, act):
        lanes = pl.ds(part * 9216, 9216)
        for core in (0, 1):
            target = two_ref if (core == 0) == own else one_ref

            @pl.when(where_ref[0] == core)
            def _(target=target):
                act(
                    pltpu.make_async_copy(
                        out_ref.at[:, lanes], target.at[:, lanes], sems.at[part]
                    )
                )

    for n in range(288):
        m, q = n // 3, n % 3
        first = (m % 16) * ROWS + q * 6 + m // 16
        eight = scr_ref[pl.ds(first, 8, stride=18), :]
        last = first + 144
        nine = jnp.concatenate([eight, scr_ref[last : last + 1, :]], axis=0)
        out_ref[:, n * 128 : (n + 1) * 128] = nine.astype(BF16)
        if n % 72 == 71:
            each_copy(n // 72, lambda copy: copy.start())
    for part in range(4):
        each_copy(part, lambda copy: copy.wait())


def exchange(value, axes):
    return lax.all_to_all(value, axes, split_axis=0, concat_axis=0, tiled=True)


def shape(*dims, dtype=BF16):
    return jax.ShapeDtypeStruct(dims, dtype)


def per_device(inputs, first_weight, second_weight, cotangent):
    smem, hbm, vmem = pltpu.SMEM, pltpu.HBM, pltpu.VMEM
    core = lax.axis_index("core").astype(jnp.int32).reshape(1)
    half = lax.axis_index("yl").astype(jnp.int32).reshape(1)
    swap = [(0, 1), (1, 0)]
    short = pl.CostEstimate(flops=10**9, bytes_accessed=3 * 10**6, transcendentals=0)
    kernel_one = first_weight.reshape(9 * C, C)
    kernel_two = second_weight.reshape(9 * C, C)
    packed, where = call(
        pack_kernel,
        (shape(768, 128), shape(2, dtype=jnp.int32)),
        scratch=(
            vmem((2, 16, 16 * C), BF16),
            vmem((768, 128), F32),
            pltpu.SemaphoreType.DMA((2,)),
        ),
        spaces={0: smem, 1: smem, 2: hbm, 3: hbm},
        out_specs=(pl.BlockSpec(memory_space=vmem), pl.BlockSpec(memory_space=smem)),
        limit=63400000,
    )(core, half, inputs, cotangent)
    received = exchange(packed.reshape(384, 2, 128), PEERS).reshape(768, 128)
    fields, keep, send = call(
        main_kernel,
        (shape(8 * FIELD, 128), shape(3, CELLS, 128), shape(3, CELLS, 128)),
        scratch=(
            vmem((768, 128), F32),
            vmem((4, 3, CELLS + 2 * PAD, C), BF16),
            vmem((2, 3, CELLS, 128), BF16),
        ),
        spaces={0: smem},
    )(where, received, kernel_one, kernel_two)
    other = lax.ppermute(send, "core", swap)
    scratch = (vmem((1, 3, CELLS + 2 * PAD, C), BF16), vmem((2, C, 128), F32))
    begun = call(
        functools.partial(half_kernel, True),
        shape(9, C, C, dtype=F32),
        scratch=scratch,
        spaces={0: smem},
        cost_estimate=short,
    )(where, keep)
    terms = call(
        functools.partial(half_kernel, False),
        shape(16 * BOTH, 128),
        scratch=(*scratch, vmem((16 * BOTH, 128), F32)),
        spaces={0: smem},
    )(where, other, begun, fields)
    plane = exchange(terms.reshape(8 * BOTH, 2, 128), PLANE).reshape(16 * BOTH, 128)
    lines = call(
        line_kernel,
        shape(16 * LINE_ROWS, 128),
        scratch=(
            vmem((16 * BOTH, 128), F32),
            vmem((ROWS, 128), F32),
            vmem((16 * LINE_ROWS, 128), F32),
        ),
        spaces={0: smem},
    )(where, plane)
    back = exchange(lines.reshape(8 * LINE_ROWS, 2, 128), LINE).reshape(16 * LINE_ROWS, 128)
    mine = call(sum_kernel, shape(4, 48, 128), scratch=(vmem((16 * LINE_ROWS + 8, 128), F32),))(back)
    line = exchange(mine, "zl")
    spread = call(
        spread_kernel, shape(16, ROWS, 128), scratch=(vmem((3 * PIECE + 53, 128), F32),)
    )(line)
    gathered = exchange(spread, PLANE)
    partner = lax.ppermute(gathered, "core", swap)
    output, input_grad = call(
        tile_kernel,
        (shape(16, 16 * C), shape(16, 16 * C)),
        scratch=(vmem((16 * LINE_ROWS, 128), F32),),
        cost_estimate=short,
    )(back)
    weight = shape(9, C * C)
    anywhere = pl.BlockSpec(memory_space=pl.ANY)
    scratch = (vmem((9, C * C), BF16), vmem((16 * ROWS, 128), F32), pltpu.SemaphoreType.DMA((4,)))
    one, two = call(
        functools.partial(final_kernel, True),
        (weight, weight),
        scratch=scratch,
        spaces={0: smem},
        out_specs=(anywhere, anywhere),
        cost_estimate=short,
    )(where, gathered)
    one, two = call(
        functools.partial(final_kernel, False),
        (weight, weight),
        scratch=scratch,
        spaces={0: smem, 2: pl.ANY, 3: pl.ANY},
        out_specs=(anywhere, anywhere),
        input_output_aliases={2: 0, 3: 1},
    )(where, partner, one, two)
    return output, input_grad, one, two


def solution(mesh):
    grid = Mesh(mesh.devices.reshape(SIZES), AXES)
    tile = P(("zl", "yh", "yl"), ("x", "zh", "core"))
    return jax.shard_map(
        per_device,
        mesh=grid,
        in_specs=(tile, P(), P(), tile),
        out_specs=(tile, tile, P(), P()),
        check_vma=False,
    )
```

```python
import functools

import jax
import jax.numpy as jnp
from jax import lax
from jax.experimental import pallas as pl
from jax.experimental.pallas import tpu as pltpu
from jax.sharding import Mesh, PartitionSpec as P

C = 192
AXES = ("zl", "yh", "yl", "x", "zh", "core")
SIZES = (4, 2, 2, 4, 4, 2)
PEERS = ("zh", "zl", "x", "yh")
PLANE = ("yl", "x", "yh")
LINE = ("zh", "zl")
BF16 = jnp.bfloat16
F32 = jnp.float32
ROWS = 168
TERMS = 162
FIELD = 96
BOTH = TERMS + FIELD
PIECE = 41
WIDE = 21 * 128
LINE_ROWS = 48 + PIECE + 1
ZH = 64
PAD = 2 * ZH
CELLS = 256
OFFSETS = [(a, b) for a in (-1, 0, 1) for b in (-1, 0, 1)]


def call(kernel, out_shape, scratch=(), spaces={}, out_specs=None, limit=40 * 1024 * 1024, **extra):
    if out_specs is None:
        out_specs = jax.tree.map(lambda _: pl.BlockSpec(memory_space=pltpu.VMEM), out_shape)

    def run(*args):
        return pl.pallas_call(
            kernel,
            out_shape=out_shape,
            in_specs=[
                pl.BlockSpec(memory_space=spaces.get(n, pltpu.VMEM)) for n in range(len(args))
            ],
            out_specs=out_specs,
            scratch_shapes=list(scratch),
            compiler_params=pltpu.CompilerParams(vmem_limit_bytes=limit),
            **extra,
        )(*args)

    return run


def gelu_parts(value):
    normal_cdf = 0.5 * (1.0 + lax.erf(value * 0.7071067811865476))
    density = jnp.exp(-0.5 * value * value) * 0.3989422804014327
    return value * normal_cdf, normal_cdf + value * density


def pack_kernel(core_ref, half_ref, x_hbm, g_hbm, o_ref, where_ref, in_ref, row_ref, sems):
    copies = [pltpu.make_async_copy(h, in_ref.at[n], sems.at[n]) for n, h in enumerate((x_hbm, g_hbm))]
    for copy in copies:
        copy.start()
    where_ref[0] = core_ref[0]
    where_ref[1] = half_ref[0]
    for copy in copies:
        copy.wait()
    fields = [in_ref[n].astype(F32) for n in (0, 1)]
    for j in range(16):
        pieces = [f[k * 8 : k * 8 + 8, j * C : (j + 1) * C] for f in fields for k in (0, 1)]
        wide = jnp.concatenate(pieces, axis=1)
        for t in range(6):
            row_ref[pl.ds(j * 48 + t, 8, stride=6), :] = wide[:, t * 128 : t * 128 + 128]
    for j in range(16):
        o_ref[j * 48 : j * 48 + 48, :] = row_ref[j * 48 : j * 48 + 48, :].astype(BF16)


def put_taps(tap_ref, slot, field, step):
    row = lax.broadcasted_iota(jnp.int32, (CELLS, C), 0)
    zl_of, x_of, yh_of = (row // 16) % 4, (row % 8) // 2, row % 2

    def ahead(value, rows):
        return pltpu.roll(value, (-rows) % CELLS, 0)

    more = step * ZH
    for a in (-1, 0, 1):
        moved = field
        if a != 0:
            inside = (zl_of + a >= 0) & (zl_of + a < 4)
            if step == 2:
                moved = jnp.where(inside, ahead(field, 16 * a), 0.0)
            else:
                crossed = jnp.where(inside, ahead(field, 15 * a), 0.0)
                moved = jnp.where(yh_of == (0 if a == 1 else 1), ahead(field, a), crossed)
        before = jnp.where(x_of > 0, ahead(moved, -2), 0.0)[CELLS - more :]
        after = jnp.where(x_of < 3, ahead(moved, 2), 0.0)[:more]
        tap_ref[slot, a + 1, PAD - more : PAD, :] = before.astype(BF16)
        tap_ref[slot, a + 1, PAD : PAD + CELLS, :] = moved.astype(BF16)
        tap_ref[slot, a + 1, PAD + CELLS : PAD + CELLS + more, :] = after.astype(BF16)


def get_tap(tap_ref, slot, a, b, step):
    start = PAD + ZH * b * step
    return tap_ref[slot, a + 1, start : start + CELLS, :]


def main_kernel(where_ref, r_ref, w1_ref, w2_ref, o_ref, keep_ref, send_ref, row_ref, tap_ref, pair_ref):
    row_ref[...] = r_ref[...].astype(F32)

    def unpack(f):
        tiles = [row_ref[pl.ds(3 * f + t, 128, stride=6), :] for t in range(3)]
        part = jnp.concatenate(tiles, axis=1)
        both = [part[:, k * C : (k + 1) * C].reshape(16, 1, 8, C) for k in (0, 1)]
        return jnp.concatenate(both, axis=1).reshape(CELLS, C)

    def pack(value):
        split = value.reshape(16, 2, 8, C)
        return jnp.concatenate([split[:, k].reshape(128, C) for k in (0, 1)], axis=1)

    def forward(slot, w_ref, step):
        total = None
        for t, (a, b) in enumerate(OFFSETS):
            term = jnp.dot(
                get_tap(tap_ref, slot, a, b, step), w_ref[t * C : (t + 1) * C, :], preferred_element_type=F32
            )
            total = term if total is None else total + term
        return total

    def backward(slot, w_ref, step):
        total = None
        for t, (a, b) in enumerate(OFFSETS):
            term = lax.dot_general(
                get_tap(tap_ref, slot, -a, -b, step),
                w_ref[t * C : (t + 1) * C, :],
                (((1,), (1,)), ((), ())),
                preferred_element_type=F32,
            )
            total = term if total is None else total + term
        return total

    x = unpack(0)
    g = unpack(1)
    gelu_one, slope_one = gelu_parts(x)
    act_one = gelu_one.astype(BF16).astype(F32)
    put_taps(tap_ref, 0, act_one, 1)
    put_taps(tap_ref, 2, g, 2)
    hidden = (x + forward(0, w1_ref, 1)).astype(BF16).astype(F32)
    gelu_two, slope_two = gelu_parts(hidden)
    act_two = gelu_two.astype(BF16).astype(F32)
    put_taps(tap_ref, 1, act_two, 2)
    hidden_grad = (g + backward(2, w2_ref, 2) * slope_two).astype(BF16).astype(F32)
    put_taps(tap_ref, 3, hidden_grad, 1)
    output = hidden + forward(1, w2_ref, 2)
    input_grad = hidden_grad + backward(3, w1_ref, 1) * slope_one
    wide = jnp.concatenate([pack(output), pack(input_grad)], axis=1)
    for t in range(6):
        row_ref[t * 128 : t * 128 + 128, :] = wide[:, t * 128 : t * 128 + 128]
    for e in range(8):
        tiles = [row_ref[pl.ds(t * 128 + e, 16, stride=8), :] for t in range(6)]
        o_ref[e * FIELD : (e + 1) * FIELD, :] = jnp.concatenate(tiles, axis=0).astype(BF16)
    for index, (act, grad) in enumerate(((act_two, g), (act_one, hidden_grad))):
        pair_ref[index, 0] = act[:, 0:128].astype(BF16)
        pair_ref[index, 1] = jnp.concatenate([act[:, 128:C], grad[:, 128:C]], axis=1).astype(BF16)
        pair_ref[index, 2] = grad[:, 0:128].astype(BF16)
    core = where_ref[0]
    keep_ref[...] = pair_ref[core]
    send_ref[...] = pair_ref[1 - core]


def half_kernel(own, where_ref, pair_ref, *refs):
    o_ref, tap_ref, ft_ref = refs[-4:-1] if not own else refs[-3:]
    if not own:
        for c in range(16):
            piece = refs[1][(c % 8) * FIELD : (c % 8 + 1) * FIELD, :].astype(F32)
            refs[-1][c * BOTH + TERMS : (c + 1) * BOTH, :] = piece
    first, mixed, last = [pair_ref[n].astype(F32) for n in range(3)]
    turned = jnp.concatenate([first, mixed[:, 0:64]], axis=1).T
    grad = jnp.concatenate([last, mixed[:, 64:128]], axis=1)
    for n in (0, 1):
        ft_ref[n] = turned[:, n * 128 : n * 128 + 128]
    left = jnp.concatenate(
        [
            jnp.concatenate([ft_ref[n, pl.ds(2 * u + odd, 16, stride=12), :] for n in (0, 1)], axis=1)
            for odd in (0, 1)
            for u in range(6)
        ],
        axis=0,
    ).astype(BF16)

    def weight_grad(step):
        put_taps(tap_ref, 0, grad, step)
        for t, (a, b) in enumerate(OFFSETS):
            full = jnp.dot(left, get_tap(tap_ref, 0, -a, -b, step), preferred_element_type=F32)
            if own:
                o_ref[t] = full
                continue
            full = full + refs[0][t]
            even, odd = full[0:96], full[96:192]
            lanes = (
                even[:, 0:128],
                jnp.concatenate([even[:, 128:192], odd[:, 0:64]], axis=1),
                odd[:, 64:192],
            )
            wg_ref = refs[-1]
            for q in range(3):
                for u in range(6):
                    wg_ref[pl.ds(t * 18 + u * 3 + q, 16, stride=BOTH), :] = lanes[q][
                        u * 16 : u * 16 + 16
                    ]

    for core, step in ((0, 2), (1, 1)):
        pl.when(where_ref[0] == core)(lambda step=step: weight_grad(step))
    if not own:
        o_ref[...] = refs[-1][...].astype(BF16)


def line_kernel(where_ref, s_ref, out_ref, part_ref, sum_ref, row_ref):
    part_ref[0 : 16 * BOTH, :] = s_ref[...].astype(F32)
    total = part_ref[0:ROWS, :]
    for c in range(1, 16):
        total = total + part_ref[c * BOTH : c * BOTH + ROWS, :]
    sum_ref[...] = total
    for zl in range(4):
        piece = sum_ref[zl * PIECE : zl * PIECE + PIECE + 1, :]
        for zh in range(4):
            start = (zh * 4 + zl) * LINE_ROWS + 48
            row_ref[start : start + PIECE + 1, :] = piece
    for half in (0, 1):

        @pl.when(where_ref[1] == half)
        def _():
            for z in range(16):
                for t in range(6):
                    first = half * 8 * BOTH + TERMS + t * 16 + z
                    row_ref[z * LINE_ROWS + t * 8 : z * LINE_ROWS + t * 8 + 8, :] = part_ref[
                        pl.ds(first, 8, stride=BOTH), :
                    ]

    out_ref[...] = row_ref[...].astype(BF16)


def sum_kernel(r_ref, z_ref, row_ref):
    row_ref[0 : 16 * LINE_ROWS, :] = r_ref[...].astype(F32)
    row_ref[16 * LINE_ROWS :, :] = jnp.zeros((8, 128), F32)
    total = row_ref[48:96, :]
    for z in range(1, 16):
        total = total + row_ref[z * LINE_ROWS + 48 : z * LINE_ROWS + 96, :]
    mine = (total * (1.0 / 256.0)).astype(BF16)
    for z in range(4):
        z_ref[z] = mine


def tile_kernel(r_ref, out_ref, ig_ref, row_ref):
    row_ref[...] = r_ref[...].astype(F32)
    for f, ref in enumerate((out_ref, ig_ref)):
        halves = []
        for k in (0, 1):
            parts = []
            for z in range(16):
                tiles = [
                    row_ref[z * LINE_ROWS + (3 * f + t) * 8 : z * LINE_ROWS + (3 * f + t) * 8 + 8, :]
                    for t in (k, k + 1)
                ]
                both = jnp.concatenate(tiles, axis=1)
                parts.append(both[:, k * 64 : k * 64 + C])
            halves.append(jnp.concatenate(parts, axis=1))
        ref[...] = jnp.concatenate(halves, axis=0).astype(BF16)


def spread_kernel(z_ref, out_ref, row_ref):
    for z in range(4):
        row_ref[z * PIECE : z * PIECE + 48, :] = z_ref[z].astype(F32)
    tiles = [row_ref[pl.ds(v, 8, stride=18), :] for v in range(18)]
    tiles += [row_ref[v : v + 8, :] for v in (144, 152, 160)]
    mine = jnp.concatenate(tiles, axis=1).astype(BF16)
    for c in range(16):
        out_ref[c] = mine


def final_kernel(own, where_ref, r_ref, *refs):
    one_ref, two_ref, out_ref, sems = refs[-4:]

    def each_copy(part, act):
        lanes = pl.ds(part * 9216, 9216)
        for core in (0, 1):
            target = two_ref if (core == 0) == own else one_ref

            @pl.when(where_ref[0] == core)
            def _(target=target):
                act(
                    pltpu.make_async_copy(
                        out_ref.at[:, lanes], target.at[:, lanes], sems.at[part]
                    )
                )

    for c in range(16):
        lanes = c * 2304
        out_ref[0:8, lanes : lanes + 2304] = r_ref[c, :, 0:2304]
        last = r_ref[c, :, 2304:WIDE].astype(F32)
        for v in range(18):
            row = last[v % 8 : v % 8 + 1, v // 8 * 128 : v // 8 * 128 + 128]
            out_ref[8:9, lanes + v * 128 : lanes + v * 128 + 128] = row.astype(BF16)
        if c % 4 == 3:
            each_copy(c // 4, lambda copy: copy.start())
    for part in range(4):
        each_copy(part, lambda copy: copy.wait())


def exchange(value, axes):
    return lax.all_to_all(value, axes, split_axis=0, concat_axis=0, tiled=True)


def shape(*dims, dtype=BF16):
    return jax.ShapeDtypeStruct(dims, dtype)


def per_device(inputs, first_weight, second_weight, cotangent):
    smem, hbm, vmem = pltpu.SMEM, pltpu.HBM, pltpu.VMEM
    core = lax.axis_index("core").astype(jnp.int32).reshape(1)
    half = lax.axis_index("yl").astype(jnp.int32).reshape(1)
    swap = [(0, 1), (1, 0)]
    short = pl.CostEstimate(flops=10**9, bytes_accessed=3 * 10**6, transcendentals=0)
    kernel_one = first_weight.reshape(9 * C, C)
    kernel_two = second_weight.reshape(9 * C, C)
    packed, where = call(
        pack_kernel,
        (shape(768, 128), shape(2, dtype=jnp.int32)),
        scratch=(
            vmem((2, 16, 16 * C), BF16),
            vmem((768, 128), F32),
            pltpu.SemaphoreType.DMA((2,)),
        ),
        spaces={0: smem, 1: smem, 2: hbm, 3: hbm},
        out_specs=(pl.BlockSpec(memory_space=vmem), pl.BlockSpec(memory_space=smem)),
        limit=63400000,
    )(core, half, inputs, cotangent)
    received = exchange(packed.reshape(384, 2, 128), PEERS).reshape(768, 128)
    fields, keep, send = call(
        main_kernel,
        (shape(8 * FIELD, 128), shape(3, CELLS, 128), shape(3, CELLS, 128)),
        scratch=(
            vmem((768, 128), F32),
            vmem((4, 3, CELLS + 2 * PAD, C), BF16),
            vmem((2, 3, CELLS, 128), BF16),
        ),
        spaces={0: smem},
    )(where, received, kernel_one, kernel_two)
    other = lax.ppermute(send, "core", swap)
    scratch = (vmem((1, 3, CELLS + 2 * PAD, C), BF16), vmem((2, C, 128), F32))
    begun = call(
        functools.partial(half_kernel, True),
        shape(9, C, C, dtype=F32),
        scratch=scratch,
        spaces={0: smem},
        cost_estimate=short,
    )(where, keep)
    terms = call(
        functools.partial(half_kernel, False),
        shape(16 * BOTH, 128),
        scratch=(*scratch, vmem((16 * BOTH, 128), F32)),
        spaces={0: smem},
    )(where, other, begun, fields)
    plane = exchange(terms.reshape(8 * BOTH, 2, 128), PLANE).reshape(16 * BOTH, 128)
    lines = call(
        line_kernel,
        shape(16 * LINE_ROWS, 128),
        scratch=(
            vmem((16 * BOTH, 128), F32),
            vmem((ROWS, 128), F32),
            vmem((16 * LINE_ROWS, 128), F32),
        ),
        spaces={0: smem},
    )(where, plane)
    back = exchange(lines.reshape(8 * LINE_ROWS, 2, 128), LINE).reshape(16 * LINE_ROWS, 128)
    mine = call(sum_kernel, shape(4, 48, 128), scratch=(vmem((16 * LINE_ROWS + 8, 128), F32),))(back)
    line = exchange(mine, "zl")
    spread = call(
        spread_kernel, shape(16, 8, WIDE), scratch=(vmem((3 * PIECE + 53, 128), F32),)
    )(line)
    gathered = exchange(spread, PLANE)
    partner = lax.ppermute(gathered, "core", swap)
    output, input_grad = call(
        tile_kernel,
        (shape(16, 16 * C), shape(16, 16 * C)),
        scratch=(vmem((16 * LINE_ROWS, 128), F32),),
        cost_estimate=short,
    )(back)
    weight = shape(9, C * C)
    anywhere = pl.BlockSpec(memory_space=pl.ANY)
    scratch = (vmem((9, C * C), BF16), pltpu.SemaphoreType.DMA((4,)))
    one, two = call(
        functools.partial(final_kernel, True),
        (weight, weight),
        scratch=scratch,
        spaces={0: smem},
        out_specs=(anywhere, anywhere),
        cost_estimate=short,
    )(where, gathered)
    one, two = call(
        functools.partial(final_kernel, False),
        (weight, weight),
        scratch=scratch,
        spaces={0: smem, 2: pl.ANY, 3: pl.ANY},
        out_specs=(anywhere, anywhere),
        input_output_aliases={2: 0, 3: 1},
    )(where, partner, one, two)
    return output, input_grad, one, two


def solution(mesh):
    grid = Mesh(mesh.devices.reshape(SIZES), AXES)
    tile = P(("zl", "yh", "yl"), ("x", "zh", "core"))
    return jax.shard_map(
        per_device,
        mesh=grid,
        in_specs=(tile, P(), P(), tile),
        out_specs=(tile, tile, P(), P()),
        check_vma=False,
    )
```

```python
import functools

import jax
import jax.numpy as jnp
from jax import lax
from jax.experimental import pallas as pl
from jax.experimental.pallas import tpu as pltpu
from jax.sharding import Mesh, PartitionSpec as P

C = 192
AXES = ("zl", "yh", "yl", "x", "zh", "core")
SIZES = (4, 2, 2, 4, 4, 2)
PEERS = ("zh", "zl", "x", "yh")
PLANE = ("yl", "x", "yh")
LINE = ("zh", "zl")
BF16 = jnp.bfloat16
F32 = jnp.float32
ROWS = 168
TERMS = 162
FIELD = 96
BOTH = TERMS + FIELD
PIECE = 41
WIDE = 21 * 128
LINE_ROWS = 48 + PIECE + 1
ZH = 64
PAD = 2 * ZH
CELLS = 256
OFFSETS = [(a, b) for a in (-1, 0, 1) for b in (-1, 0, 1)]


def call(kernel, out_shape, scratch=(), spaces={}, out_specs=None, limit=40 * 1024 * 1024, **extra):
    if out_specs is None:
        out_specs = jax.tree.map(lambda _: pl.BlockSpec(memory_space=pltpu.VMEM), out_shape)

    def run(*args):
        return pl.pallas_call(
            kernel,
            out_shape=out_shape,
            in_specs=[
                pl.BlockSpec(memory_space=spaces.get(n, pltpu.VMEM)) for n in range(len(args))
            ],
            out_specs=out_specs,
            scratch_shapes=list(scratch),
            compiler_params=pltpu.CompilerParams(vmem_limit_bytes=limit),
            **extra,
        )(*args)

    return run


def gelu_parts(value):
    normal_cdf = 0.5 * (1.0 + lax.erf(value * 0.7071067811865476))
    density = jnp.exp(-0.5 * value * value) * 0.3989422804014327
    return value * normal_cdf, normal_cdf + value * density


def pack_kernel(x_hbm, g_hbm, o_ref, in_ref, row_ref, sems):
    copies = [pltpu.make_async_copy(h, in_ref.at[n], sems.at[n]) for n, h in enumerate((x_hbm, g_hbm))]
    for copy in copies:
        copy.start()
    for copy in copies:
        copy.wait()
    fields = [in_ref[n].astype(F32) for n in (0, 1)]
    for j in range(16):
        pieces = [f[k * 8 : k * 8 + 8, j * C : (j + 1) * C] for f in fields for k in (0, 1)]
        wide = jnp.concatenate(pieces, axis=1)
        for t in range(6):
            row_ref[pl.ds(j * 48 + t, 8, stride=6), :] = wide[:, t * 128 : t * 128 + 128]
    for j in range(16):
        o_ref[j * 48 : j * 48 + 48, :] = row_ref[j * 48 : j * 48 + 48, :].astype(BF16)


def put_taps(tap_ref, slot, field, step):
    row = lax.broadcasted_iota(jnp.int32, (CELLS, C), 0)
    zl_of, x_of, yh_of = (row // 16) % 4, (row % 8) // 2, row % 2

    def ahead(value, rows):
        return pltpu.roll(value, (-rows) % CELLS, 0)

    more = step * ZH
    for a in (-1, 0, 1):
        moved = field
        if a != 0:
            inside = (zl_of + a >= 0) & (zl_of + a < 4)
            if step == 2:
                moved = jnp.where(inside, ahead(field, 16 * a), 0.0)
            else:
                crossed = jnp.where(inside, ahead(field, 15 * a), 0.0)
                moved = jnp.where(yh_of == (0 if a == 1 else 1), ahead(field, a), crossed)
        before = jnp.where(x_of > 0, ahead(moved, -2), 0.0)[CELLS - more :]
        after = jnp.where(x_of < 3, ahead(moved, 2), 0.0)[:more]
        tap_ref[slot, a + 1, PAD - more : PAD, :] = before.astype(BF16)
        tap_ref[slot, a + 1, PAD : PAD + CELLS, :] = moved.astype(BF16)
        tap_ref[slot, a + 1, PAD + CELLS : PAD + CELLS + more, :] = after.astype(BF16)


def get_tap(tap_ref, slot, a, b, step):
    start = PAD + ZH * b * step
    return tap_ref[slot, a + 1, start : start + CELLS, :]


def main_kernel(r_ref, w1_ref, w2_ref, o_ref, keep_ref, send_ref, row_ref, tap_ref, pair_ref):
    row_ref[...] = r_ref[...].astype(F32)

    def unpack(f):
        tiles = [row_ref[pl.ds(3 * f + t, 128, stride=6), :] for t in range(3)]
        part = jnp.concatenate(tiles, axis=1)
        both = [part[:, k * C : (k + 1) * C].reshape(16, 1, 8, C) for k in (0, 1)]
        return jnp.concatenate(both, axis=1).reshape(CELLS, C)

    def pack(value):
        split = value.reshape(16, 2, 8, C)
        return jnp.concatenate([split[:, k].reshape(128, C) for k in (0, 1)], axis=1)

    def forward(slot, w_ref, step):
        total = None
        for t, (a, b) in enumerate(OFFSETS):
            term = jnp.dot(
                get_tap(tap_ref, slot, a, b, step), w_ref[t * C : (t + 1) * C, :], preferred_element_type=F32
            )
            total = term if total is None else total + term
        return total

    def backward(slot, w_ref, step):
        total = None
        for t, (a, b) in enumerate(OFFSETS):
            term = lax.dot_general(
                get_tap(tap_ref, slot, -a, -b, step),
                w_ref[t * C : (t + 1) * C, :],
                (((1,), (1,)), ((), ())),
                preferred_element_type=F32,
            )
            total = term if total is None else total + term
        return total

    x = unpack(0)
    g = unpack(1)
    gelu_one, slope_one = gelu_parts(x)
    act_one = gelu_one.astype(BF16).astype(F32)
    put_taps(tap_ref, 0, act_one, 1)
    put_taps(tap_ref, 2, g, 2)
    hidden = (x + forward(0, w1_ref, 1)).astype(BF16).astype(F32)
    gelu_two, slope_two = gelu_parts(hidden)
    act_two = gelu_two.astype(BF16).astype(F32)
    put_taps(tap_ref, 1, act_two, 2)
    hidden_grad = (g + backward(2, w2_ref, 2) * slope_two).astype(BF16).astype(F32)
    put_taps(tap_ref, 3, hidden_grad, 1)
    output = hidden + forward(1, w2_ref, 2)
    input_grad = hidden_grad + backward(3, w1_ref, 1) * slope_one
    wide = jnp.concatenate([pack(output), pack(input_grad)], axis=1)
    for t in range(6):
        row_ref[t * 128 : t * 128 + 128, :] = wide[:, t * 128 : t * 128 + 128]
    for e in range(8):
        tiles = [row_ref[pl.ds(t * 128 + e, 16, stride=8), :] for t in range(6)]
        o_ref[e * FIELD : (e + 1) * FIELD, :] = jnp.concatenate(tiles, axis=0).astype(BF16)
    for index, (act, grad) in enumerate(((act_two, g), (act_one, hidden_grad))):
        pair_ref[index, 0] = act[:, 0:128].astype(BF16)
        pair_ref[index, 1] = jnp.concatenate([act[:, 128:C], grad[:, 128:C]], axis=1).astype(BF16)
        pair_ref[index, 2] = grad[:, 0:128].astype(BF16)
    core = lax.axis_index("core")
    keep_ref[...] = pair_ref[core]
    send_ref[...] = pair_ref[1 - core]


def half_kernel(own, pair_ref, *refs):
    o_ref, tap_ref, ft_ref = refs[-4:-1] if not own else refs[-3:]
    if not own:
        for c in range(16):
            piece = refs[1][(c % 8) * FIELD : (c % 8 + 1) * FIELD, :].astype(F32)
            refs[-1][c * BOTH + TERMS : (c + 1) * BOTH, :] = piece
    first, mixed, last = [pair_ref[n].astype(F32) for n in range(3)]
    turned = jnp.concatenate([first, mixed[:, 0:64]], axis=1).T
    grad = jnp.concatenate([last, mixed[:, 64:128]], axis=1)
    for n in (0, 1):
        ft_ref[n] = turned[:, n * 128 : n * 128 + 128]
    left = jnp.concatenate(
        [
            jnp.concatenate([ft_ref[n, pl.ds(2 * u + odd, 16, stride=12), :] for n in (0, 1)], axis=1)
            for odd in (0, 1)
            for u in range(6)
        ],
        axis=0,
    ).astype(BF16)

    def weight_grad(step):
        put_taps(tap_ref, 0, grad, step)
        for t, (a, b) in enumerate(OFFSETS):
            full = jnp.dot(left, get_tap(tap_ref, 0, -a, -b, step), preferred_element_type=F32)
            if own:
                o_ref[t] = full
                continue
            full = full + refs[0][t]
            even, odd = full[0:96], full[96:192]
            lanes = (
                even[:, 0:128],
                jnp.concatenate([even[:, 128:192], odd[:, 0:64]], axis=1),
                odd[:, 64:192],
            )
            wg_ref = refs[-1]
            for q in range(3):
                for u in range(6):
                    wg_ref[pl.ds(t * 18 + u * 3 + q, 16, stride=BOTH), :] = lanes[q][
                        u * 16 : u * 16 + 16
                    ]

    for core, step in ((0, 2), (1, 1)):
        pl.when(lax.axis_index("core") == core)(lambda step=step: weight_grad(step))
    if not own:
        o_ref[...] = refs[-1][...].astype(BF16)


def line_kernel(s_ref, out_ref, part_ref, sum_ref, row_ref):
    part_ref[0 : 16 * BOTH, :] = s_ref[...].astype(F32)
    total = part_ref[0:ROWS, :]
    for c in range(1, 16):
        total = total + part_ref[c * BOTH : c * BOTH + ROWS, :]
    sum_ref[...] = total
    for zl in range(4):
        piece = sum_ref[zl * PIECE : zl * PIECE + PIECE + 1, :]
        for zh in range(4):
            start = (zh * 4 + zl) * LINE_ROWS + 48
            row_ref[start : start + PIECE + 1, :] = piece
    for half in (0, 1):

        @pl.when(lax.axis_index("yl") == half)
        def _():
            for z in range(16):
                for t in range(6):
                    first = half * 8 * BOTH + TERMS + t * 16 + z
                    row_ref[z * LINE_ROWS + t * 8 : z * LINE_ROWS + t * 8 + 8, :] = part_ref[
                        pl.ds(first, 8, stride=BOTH), :
                    ]

    out_ref[...] = row_ref[...].astype(BF16)


def sum_kernel(r_ref, z_ref, row_ref):
    row_ref[0 : 16 * LINE_ROWS, :] = r_ref[...].astype(F32)
    row_ref[16 * LINE_ROWS :, :] = jnp.zeros((8, 128), F32)
    total = row_ref[48:96, :]
    for z in range(1, 16):
        total = total + row_ref[z * LINE_ROWS + 48 : z * LINE_ROWS + 96, :]
    mine = (total * (1.0 / 256.0)).astype(BF16)
    for z in range(4):
        z_ref[z] = mine


def tile_kernel(r_ref, out_ref, ig_ref, row_ref):
    row_ref[...] = r_ref[...].astype(F32)
    for f, ref in enumerate((out_ref, ig_ref)):
        halves = []
        for k in (0, 1):
            parts = []
            for z in range(16):
                tiles = [
                    row_ref[z * LINE_ROWS + (3 * f + t) * 8 : z * LINE_ROWS + (3 * f + t) * 8 + 8, :]
                    for t in (k, k + 1)
                ]
                both = jnp.concatenate(tiles, axis=1)
                parts.append(both[:, k * 64 : k * 64 + C])
            halves.append(jnp.concatenate(parts, axis=1))
        ref[...] = jnp.concatenate(halves, axis=0).astype(BF16)


def spread_kernel(z_ref, out_ref, row_ref):
    for z in range(4):
        row_ref[z * PIECE : z * PIECE + 48, :] = z_ref[z].astype(F32)
    tiles = [row_ref[pl.ds(v, 8, stride=18), :] for v in range(18)]
    tiles += [row_ref[v : v + 8, :] for v in (144, 152, 160)]
    mine = jnp.concatenate(tiles, axis=1).astype(BF16)
    for c in range(16):
        out_ref[c] = mine


def final_kernel(own, r_ref, *refs):
    one_ref, two_ref, out_ref, sems = refs[-4:]

    def each_copy(part, act):
        lanes = pl.ds(part * 9216, 9216)
        for core in (0, 1):
            target = two_ref if (core == 0) == own else one_ref

            @pl.when(lax.axis_index("core") == core)
            def _(target=target):
                act(
                    pltpu.make_async_copy(
                        out_ref.at[:, lanes], target.at[:, lanes], sems.at[part]
                    )
                )

    for c in range(16):
        lanes = c * 2304
        out_ref[0:8, lanes : lanes + 2304] = r_ref[c, :, 0:2304]
        last = r_ref[c, :, 2304:WIDE].astype(F32)
        for v in range(18):
            row = last[v % 8 : v % 8 + 1, v // 8 * 128 : v // 8 * 128 + 128]
            out_ref[8:9, lanes + v * 128 : lanes + v * 128 + 128] = row.astype(BF16)
        if c % 4 == 3:
            each_copy(c // 4, lambda copy: copy.start())
    for part in range(4):
        each_copy(part, lambda copy: copy.wait())


def exchange(value, axes):
    return lax.all_to_all(value, axes, split_axis=0, concat_axis=0, tiled=True)


def shape(*dims, dtype=BF16):
    return jax.ShapeDtypeStruct(dims, dtype)


def per_device(inputs, first_weight, second_weight, cotangent):
    hbm, vmem = pltpu.HBM, pltpu.VMEM
    swap = [(0, 1), (1, 0)]
    short = pl.CostEstimate(flops=10**9, bytes_accessed=3 * 10**6, transcendentals=0)
    kernel_one = first_weight.reshape(9 * C, C)
    kernel_two = second_weight.reshape(9 * C, C)
    packed = call(
        pack_kernel,
        shape(768, 128),
        scratch=(
            vmem((2, 16, 16 * C), BF16),
            vmem((768, 128), F32),
            pltpu.SemaphoreType.DMA((2,)),
        ),
        spaces={0: hbm, 1: hbm},
        limit=63400000,
    )(inputs, cotangent)
    received = exchange(packed.reshape(384, 2, 128), PEERS).reshape(768, 128)
    fields, keep, send = call(
        main_kernel,
        (shape(8 * FIELD, 128), shape(3, CELLS, 128), shape(3, CELLS, 128)),
        scratch=(
            vmem((768, 128), F32),
            vmem((4, 3, CELLS + 2 * PAD, C), BF16),
            vmem((2, 3, CELLS, 128), BF16),
        ),
    )(received, kernel_one, kernel_two)
    other = lax.ppermute(send, "core", swap)
    scratch = (vmem((1, 3, CELLS + 2 * PAD, C), BF16), vmem((2, C, 128), F32))
    begun = call(
        functools.partial(half_kernel, True),
        shape(9, C, C, dtype=F32),
        scratch=scratch,
        cost_estimate=short,
    )(keep)
    terms = call(
        functools.partial(half_kernel, False),
        shape(16 * BOTH, 128),
        scratch=(*scratch, vmem((16 * BOTH, 128), F32)),
    )(other, begun, fields)
    plane = exchange(terms.reshape(8 * BOTH, 2, 128), PLANE).reshape(16 * BOTH, 128)
    lines = call(
        line_kernel,
        shape(16 * LINE_ROWS, 128),
        scratch=(
            vmem((16 * BOTH, 128), F32),
            vmem((ROWS, 128), F32),
            vmem((16 * LINE_ROWS, 128), F32),
        ),
    )(plane)
    back = exchange(lines.reshape(8 * LINE_ROWS, 2, 128), LINE).reshape(16 * LINE_ROWS, 128)
    mine = call(sum_kernel, shape(4, 48, 128), scratch=(vmem((16 * LINE_ROWS + 8, 128), F32),))(back)
    line = exchange(mine, "zl")
    spread = call(
        spread_kernel, shape(16, 8, WIDE), scratch=(vmem((3 * PIECE + 53, 128), F32),)
    )(line)
    gathered = exchange(spread, PLANE)
    partner = lax.ppermute(gathered, "core", swap)
    output, input_grad = call(
        tile_kernel,
        (shape(16, 16 * C), shape(16, 16 * C)),
        scratch=(vmem((16 * LINE_ROWS, 128), F32),),
        cost_estimate=short,
    )(back)
    weight = shape(9, C * C)
    anywhere = pl.BlockSpec(memory_space=pl.ANY)
    scratch = (vmem((9, C * C), BF16), pltpu.SemaphoreType.DMA((4,)))
    one, two = call(
        functools.partial(final_kernel, True),
        (weight, weight),
        scratch=scratch,
        out_specs=(anywhere, anywhere),
        cost_estimate=short,
    )(gathered)
    one, two = call(
        functools.partial(final_kernel, False),
        (weight, weight),
        scratch=scratch,
        spaces={1: pl.ANY, 2: pl.ANY},
        out_specs=(anywhere, anywhere),
        input_output_aliases={1: 0, 2: 1},
    )(partner, one, two)
    return output, input_grad, one, two


def solution(mesh):
    grid = Mesh(mesh.devices.reshape(SIZES), AXES)
    tile = P(("zl", "yh", "yl"), ("x", "zh", "core"))
    return jax.shard_map(
        per_device,
        mesh=grid,
        in_specs=(tile, P(), P(), tile),
        out_specs=(tile, tile, P(), P()),
        check_vma=False,
    )
```

```python
import functools

import jax
import jax.numpy as jnp
from jax import lax
from jax.experimental import pallas as pl
from jax.experimental.pallas import tpu as pltpu
from jax.sharding import Mesh, PartitionSpec as P

C = 192
AXES = ("zl", "yh", "yl", "x", "zh", "core")
SIZES = (4, 2, 2, 4, 4, 2)
PEERS = ("zh", "zl", "x", "yh")
PLANE = ("yl", "x", "yh")
LINE = ("zh", "zl")
BF16 = jnp.bfloat16
F32 = jnp.float32
ROWS = 168
TERMS = 162
FIELD = 96
BOTH = TERMS + FIELD
PIECE = 41
WIDE = 21 * 128
LINE_ROWS = 48 + PIECE + 1
ZH = 64
PAD = 2 * ZH
CELLS = 256
OFFSETS = [(a, b) for a in (-1, 0, 1) for b in (-1, 0, 1)]


def call(kernel, out_shape, scratch=(), spaces={}, out_specs=None, limit=40 * 1024 * 1024, **extra):
    if out_specs is None:
        out_specs = jax.tree.map(lambda _: pl.BlockSpec(memory_space=pltpu.VMEM), out_shape)

    def run(*args):
        return pl.pallas_call(
            kernel,
            out_shape=out_shape,
            in_specs=[
                pl.BlockSpec(memory_space=spaces.get(n, pltpu.VMEM)) for n in range(len(args))
            ],
            out_specs=out_specs,
            scratch_shapes=list(scratch),
            compiler_params=pltpu.CompilerParams(vmem_limit_bytes=limit),
            **extra,
        )(*args)

    return run


def gelu_parts(value):
    normal_cdf = 0.5 * (1.0 + lax.erf(value * 0.7071067811865476))
    density = jnp.exp(-0.5 * value * value) * 0.3989422804014327
    return value * normal_cdf, normal_cdf + value * density


def pack_kernel(x_hbm, g_hbm, o_ref, in_ref, row_ref, sems):
    copies = [pltpu.make_async_copy(h, in_ref.at[n], sems.at[n]) for n, h in enumerate((x_hbm, g_hbm))]
    for copy in copies:
        copy.start()
    for copy in copies:
        copy.wait()
    fields = [in_ref[n].astype(F32) for n in (0, 1)]
    for j in range(16):
        pieces = [f[k * 8 : k * 8 + 8, j * C : (j + 1) * C] for f in fields for k in (0, 1)]
        wide = jnp.concatenate(pieces, axis=1)
        for t in range(6):
            row_ref[pl.ds(j * 48 + t, 8, stride=6), :] = wide[:, t * 128 : t * 128 + 128]
    for j in range(16):
        o_ref[j * 48 : j * 48 + 48, :] = row_ref[j * 48 : j * 48 + 48, :].astype(BF16)


def put_taps(tap_ref, slot, field, step):
    row = lax.broadcasted_iota(jnp.int32, (CELLS, C), 0)
    zl_of, x_of, yh_of = (row // 16) % 4, (row % 8) // 2, row % 2

    def ahead(value, rows):
        return pltpu.roll(value, (-rows) % CELLS, 0)

    more = step * ZH
    for a in (-1, 0, 1):
        moved = field
        if a != 0:
            inside = (zl_of + a >= 0) & (zl_of + a < 4)
            if step == 2:
                moved = jnp.where(inside, ahead(field, 16 * a), 0.0)
            else:
                crossed = jnp.where(inside, ahead(field, 15 * a), 0.0)
                moved = jnp.where(yh_of == (0 if a == 1 else 1), ahead(field, a), crossed)
        before = jnp.where(x_of > 0, ahead(moved, -2), 0.0)[CELLS - more :]
        after = jnp.where(x_of < 3, ahead(moved, 2), 0.0)[:more]
        tap_ref[slot, a + 1, PAD - more : PAD, :] = before.astype(BF16)
        tap_ref[slot, a + 1, PAD : PAD + CELLS, :] = moved.astype(BF16)
        tap_ref[slot, a + 1, PAD + CELLS : PAD + CELLS + more, :] = after.astype(BF16)


def get_tap(tap_ref, slot, a, b, step):
    start = PAD + ZH * b * step
    return tap_ref[slot, a + 1, start : start + CELLS, :]


def main_kernel(r_ref, w1_ref, w2_ref, o_ref, keep_ref, send_ref, row_ref, tap_ref, pair_ref):
    row_ref[...] = r_ref[...].astype(F32)

    def unpack(f):
        tiles = [row_ref[pl.ds(3 * f + t, 128, stride=6), :] for t in range(3)]
        part = jnp.concatenate(tiles, axis=1)
        both = [part[:, k * C : (k + 1) * C].reshape(16, 1, 8, C) for k in (0, 1)]
        return jnp.concatenate(both, axis=1).reshape(CELLS, C)

    def pack(value):
        split = value.reshape(16, 2, 8, C)
        return jnp.concatenate([split[:, k].reshape(128, C) for k in (0, 1)], axis=1)

    def forward(slot, w_ref, step):
        total = None
        for t, (a, b) in enumerate(OFFSETS):
            term = jnp.dot(
                get_tap(tap_ref, slot, a, b, step), w_ref[t * C : (t + 1) * C, :], preferred_element_type=F32
            )
            total = term if total is None else total + term
        return total

    def backward(slot, w_ref, step):
        total = None
        for t, (a, b) in enumerate(OFFSETS):
            term = lax.dot_general(
                get_tap(tap_ref, slot, -a, -b, step),
                w_ref[t * C : (t + 1) * C, :],
                (((1,), (1,)), ((), ())),
                preferred_element_type=F32,
            )
            total = term if total is None else total + term
        return total

    x = unpack(0)
    g = unpack(1)
    gelu_one, slope_one = gelu_parts(x)
    act_one = gelu_one.astype(BF16).astype(F32)
    put_taps(tap_ref, 0, act_one, 1)
    put_taps(tap_ref, 2, g, 2)
    hidden = (x + forward(0, w1_ref, 1)).astype(BF16).astype(F32)
    gelu_two, slope_two = gelu_parts(hidden)
    act_two = gelu_two.astype(BF16).astype(F32)
    put_taps(tap_ref, 1, act_two, 2)
    hidden_grad = (g + backward(2, w2_ref, 2) * slope_two).astype(BF16).astype(F32)
    put_taps(tap_ref, 3, hidden_grad, 1)
    output = hidden + forward(1, w2_ref, 2)
    input_grad = hidden_grad + backward(3, w1_ref, 1) * slope_one
    wide = jnp.concatenate([pack(output), pack(input_grad)], axis=1)
    for t in range(6):
        row_ref[t * 128 : t * 128 + 128, :] = wide[:, t * 128 : t * 128 + 128]
    for e in range(8):
        tiles = [row_ref[pl.ds(t * 128 + e, 16, stride=8), :] for t in range(6)]
        o_ref[e * FIELD : (e + 1) * FIELD, :] = jnp.concatenate(tiles, axis=0).astype(BF16)
    for index, (act, grad) in enumerate(((act_two, g), (act_one, hidden_grad))):
        pair_ref[index, 0] = act[:, 0:128].astype(BF16)
        pair_ref[index, 1] = jnp.concatenate([act[:, 128:C], grad[:, 128:C]], axis=1).astype(BF16)
        pair_ref[index, 2] = grad[:, 0:128].astype(BF16)
    core = lax.axis_index("core")
    keep_ref[...] = pair_ref[core]
    send_ref[...] = pair_ref[1 - core]


def half_kernel(own, pair_ref, *refs):
    o_ref, tap_ref, ft_ref = refs[-4:-1] if not own else refs[-3:]
    if not own:
        for c in range(16):
            piece = refs[1][(c % 8) * FIELD : (c % 8 + 1) * FIELD, :].astype(F32)
            refs[-1][c * BOTH + TERMS : (c + 1) * BOTH, :] = piece
    first, mixed, last = [pair_ref[n].astype(F32) for n in range(3)]
    turned = jnp.concatenate([first, mixed[:, 0:64]], axis=1).T
    grad = jnp.concatenate([last, mixed[:, 64:128]], axis=1)
    for n in (0, 1):
        ft_ref[n] = turned[:, n * 128 : n * 128 + 128]
    left = jnp.concatenate(
        [
            jnp.concatenate([ft_ref[n, pl.ds(2 * u + odd, 16, stride=12), :] for n in (0, 1)], axis=1)
            for odd in (0, 1)
            for u in range(6)
        ],
        axis=0,
    ).astype(BF16)

    def weight_grad(step):
        put_taps(tap_ref, 0, grad, step)
        for t, (a, b) in enumerate(OFFSETS):
            full = jnp.dot(left, get_tap(tap_ref, 0, -a, -b, step), preferred_element_type=F32)
            if own:
                o_ref[t] = full
                continue
            full = full + refs[0][t]
            even, odd = full[0:96], full[96:192]
            lanes = (
                even[:, 0:128],
                jnp.concatenate([even[:, 128:192], odd[:, 0:64]], axis=1),
                odd[:, 64:192],
            )
            wg_ref = refs[-1]
            for q in range(3):
                for u in range(6):
                    wg_ref[pl.ds(t * 18 + u * 3 + q, 16, stride=BOTH), :] = lanes[q][
                        u * 16 : u * 16 + 16
                    ]

    for core, step in ((0, 2), (1, 1)):
        pl.when(lax.axis_index("core") == core)(lambda step=step: weight_grad(step))
    if not own:
        o_ref[...] = refs[-1][0 : 16 * BOTH, :].astype(BF16)


def line_kernel(s_ref, out_ref, part_ref, sum_ref, row_ref):
    part_ref[0 : 16 * BOTH, :] = s_ref[...].astype(F32)
    total = part_ref[0:ROWS, :]
    for c in range(1, 16):
        total = total + part_ref[c * BOTH : c * BOTH + ROWS, :]
    sum_ref[0:ROWS, :] = total
    sum_ref[ROWS : ROWS + 16, :] = jnp.zeros((16, 128), F32)
    for zl in range(4):
        piece = sum_ref[zl * PIECE : zl * PIECE + PIECE + 1, :]
        for zh in range(4):
            start = (zh * 4 + zl) * LINE_ROWS + 48
            row_ref[start : start + PIECE + 1, :] = piece
    for half in (0, 1):

        @pl.when(lax.axis_index("yl") == half)
        def _():
            for z in range(16):
                for t in range(6):
                    first = half * 8 * BOTH + TERMS + t * 16 + z
                    row_ref[z * LINE_ROWS + t * 8 : z * LINE_ROWS + t * 8 + 8, :] = part_ref[
                        pl.ds(first, 8, stride=BOTH), :
                    ]

    out_ref[...] = row_ref[0 : 16 * LINE_ROWS, :].astype(BF16)


def sum_kernel(r_ref, z_ref, row_ref):
    row_ref[0 : 16 * LINE_ROWS, :] = r_ref[...].astype(F32)
    row_ref[16 * LINE_ROWS :, :] = jnp.zeros((16, 128), F32)
    total = row_ref[48:96, :]
    for z in range(1, 16):
        total = total + row_ref[z * LINE_ROWS + 48 : z * LINE_ROWS + 96, :]
    mine = (total * (1.0 / 256.0)).astype(BF16)
    for z in range(4):
        z_ref[z] = mine


def tile_kernel(r_ref, out_ref, ig_ref, row_ref):
    row_ref[...] = r_ref[...].astype(F32)
    for f, ref in enumerate((out_ref, ig_ref)):
        halves = []
        for k in (0, 1):
            parts = []
            for z in range(16):
                tiles = [
                    row_ref[z * LINE_ROWS + (3 * f + t) * 8 : z * LINE_ROWS + (3 * f + t) * 8 + 8, :]
                    for t in (k, k + 1)
                ]
                both = jnp.concatenate(tiles, axis=1)
                parts.append(both[:, k * 64 : k * 64 + C])
            halves.append(jnp.concatenate(parts, axis=1))
        ref[...] = jnp.concatenate(halves, axis=0).astype(BF16)


def spread_kernel(z_ref, out_ref, row_ref):
    for z in range(4):
        row_ref[z * PIECE : z * PIECE + 48, :] = z_ref[z].astype(F32)
    tiles = [row_ref[pl.ds(v, 8, stride=18), :] for v in range(18)]
    tiles += [row_ref[v : v + 8, :] for v in (144, 152, 160)]
    mine = jnp.concatenate(tiles, axis=1).astype(BF16)
    for c in range(16):
        out_ref[c] = mine


def final_kernel(own, r_ref, *refs):
    one_ref, two_ref, out_ref, sems = refs[-4:]

    def each_copy(part, act):
        lanes = pl.ds(part * 9216, 9216)
        for core in (0, 1):
            target = two_ref if (core == 0) == own else one_ref

            @pl.when(lax.axis_index("core") == core)
            def _(target=target):
                act(
                    pltpu.make_async_copy(
                        out_ref.at[:, lanes], target.at[:, lanes], sems.at[part]
                    )
                )

    for c in range(16):
        lanes = c * 2304
        out_ref[0:8, lanes : lanes + 2304] = r_ref[c, :, 0:2304]
        last = r_ref[c, :, 2304:WIDE].astype(F32)
        for v in range(18):
            row = last[v % 8 : v % 8 + 1, v // 8 * 128 : v // 8 * 128 + 128]
            out_ref[8:9, lanes + v * 128 : lanes + v * 128 + 128] = row.astype(BF16)
        if c % 4 == 3:
            each_copy(c // 4, lambda copy: copy.start())
    for part in range(4):
        each_copy(part, lambda copy: copy.wait())


def exchange(value, axes):
    return lax.all_to_all(value, axes, split_axis=0, concat_axis=0, tiled=True)


def shape(*dims, dtype=BF16):
    return jax.ShapeDtypeStruct(dims, dtype)


def per_device(inputs, first_weight, second_weight, cotangent):
    hbm, vmem = pltpu.HBM, pltpu.VMEM
    swap = [(0, 1), (1, 0)]
    short = pl.CostEstimate(flops=10**9, bytes_accessed=3 * 10**6, transcendentals=0)
    kernel_one = first_weight.reshape(9 * C, C)
    kernel_two = second_weight.reshape(9 * C, C)
    packed = call(
        pack_kernel,
        shape(768, 128),
        scratch=(
            vmem((2, 16, 16 * C), BF16),
            vmem((768, 128), F32),
            pltpu.SemaphoreType.DMA((2,)),
        ),
        spaces={0: hbm, 1: hbm},
        limit=63400000,
    )(inputs, cotangent)
    received = exchange(packed.reshape(384, 2, 128), PEERS).reshape(768, 128)
    fields, keep, send = call(
        main_kernel,
        (shape(8 * FIELD, 128), shape(3, CELLS, 128), shape(3, CELLS, 128)),
        scratch=(
            vmem((768, 128), F32),
            vmem((4, 3, CELLS + 2 * PAD, C), BF16),
            vmem((2, 3, CELLS, 128), BF16),
        ),
    )(received, kernel_one, kernel_two)
    other = lax.ppermute(send, "core", swap)
    scratch = (vmem((1, 3, CELLS + 2 * PAD, C), BF16), vmem((2, C, 128), F32))
    begun = call(
        functools.partial(half_kernel, True),
        shape(9, C, C, dtype=F32),
        scratch=scratch,
        cost_estimate=short,
    )(keep)
    terms = call(
        functools.partial(half_kernel, False),
        shape(16 * BOTH, 128),
        scratch=(*scratch, vmem((16 * BOTH + 8, 128), F32)),
    )(other, begun, fields)
    plane = exchange(terms.reshape(8 * BOTH, 2, 128), PLANE).reshape(16 * BOTH, 128)
    lines = call(
        line_kernel,
        shape(16 * LINE_ROWS, 128),
        scratch=(
            vmem((16 * BOTH + 8, 128), F32),
            vmem((ROWS + 16, 128), F32),
            vmem((16 * LINE_ROWS + 8, 128), F32),
        ),
    )(plane)
    back = exchange(lines.reshape(8 * LINE_ROWS, 2, 128), LINE).reshape(16 * LINE_ROWS, 128)
    mine = call(sum_kernel, shape(4, 48, 128), scratch=(vmem((16 * LINE_ROWS + 16, 128), F32),))(back)
    line = exchange(mine, "zl")
    spread = call(
        spread_kernel, shape(16, 8, WIDE), scratch=(vmem((3 * PIECE + 61, 128), F32),)
    )(line)
    gathered = exchange(spread, PLANE)
    partner = lax.ppermute(gathered, "core", swap)
    output, input_grad = call(
        tile_kernel,
        (shape(16, 16 * C), shape(16, 16 * C)),
        scratch=(vmem((16 * LINE_ROWS, 128), F32),),
        cost_estimate=short,
    )(back)
    weight = shape(9, C * C)
    anywhere = pl.BlockSpec(memory_space=pl.ANY)
    scratch = (vmem((9, C * C), BF16), pltpu.SemaphoreType.DMA((4,)))
    one, two = call(
        functools.partial(final_kernel, True),
        (weight, weight),
        scratch=scratch,
        out_specs=(anywhere, anywhere),
        cost_estimate=short,
    )(gathered)
    one, two = call(
        functools.partial(final_kernel, False),
        (weight, weight),
        scratch=scratch,
        spaces={1: pl.ANY, 2: pl.ANY},
        out_specs=(anywhere, anywhere),
        input_output_aliases={1: 0, 2: 1},
    )(partner, one, two)
    return output, input_grad, one, two


def solution(mesh):
    grid = Mesh(mesh.devices.reshape(SIZES), AXES)
    tile = P(("zl", "yh", "yl"), ("x", "zh", "core"))
    return jax.shard_map(
        per_device,
        mesh=grid,
        in_specs=(tile, P(), P(), tile),
        out_specs=(tile, tile, P(), P()),
        check_vma=False,
    )
```

```python
import functools

import jax
import jax.numpy as jnp
from jax import lax
from jax.experimental import pallas as pl
from jax.experimental.pallas import tpu as pltpu
from jax.sharding import Mesh, PartitionSpec as P

C = 192
AXES = ("zl", "yh", "yl", "x", "zh", "core")
SIZES = (4, 2, 2, 4, 4, 2)
PEERS = ("zh", "zl", "x", "yh")
PLANE = ("x", "yh", "yl")
LINE = ("zh", "zl")
BF16 = jnp.bfloat16
F32 = jnp.float32
ROWS = 168
TERMS = 162
FIELD = 96
BOTH = TERMS + FIELD
PIECE = 41
WIDE = 21 * 128
LINE_ROWS = 48 + PIECE + 1
ZH = 64
PAD = 2 * ZH
CELLS = 256
OFFSETS = [(a, b) for a in (-1, 0, 1) for b in (-1, 0, 1)]


def call(kernel, out_shape, scratch=(), spaces={}, out_specs=None, limit=40 * 1024 * 1024, **extra):
    if out_specs is None:
        out_specs = jax.tree.map(lambda _: pl.BlockSpec(memory_space=pltpu.VMEM), out_shape)

    def run(*args):
        return pl.pallas_call(
            kernel,
            out_shape=out_shape,
            in_specs=[
                pl.BlockSpec(memory_space=spaces.get(n, pltpu.VMEM)) for n in range(len(args))
            ],
            out_specs=out_specs,
            scratch_shapes=list(scratch),
            compiler_params=pltpu.CompilerParams(vmem_limit_bytes=limit),
            **extra,
        )(*args)

    return run


def gelu_parts(value):
    normal_cdf = 0.5 * (1.0 + lax.erf(value * 0.7071067811865476))
    density = jnp.exp(-0.5 * value * value) * 0.3989422804014327
    return value * normal_cdf, normal_cdf + value * density


def pack_kernel(x_hbm, g_hbm, o_ref, in_ref, row_ref, sems):
    copies = [pltpu.make_async_copy(h, in_ref.at[n], sems.at[n]) for n, h in enumerate((x_hbm, g_hbm))]
    for copy in copies:
        copy.start()
    for copy in copies:
        copy.wait()
    fields = [in_ref[n].astype(F32) for n in (0, 1)]
    for j in range(16):
        pieces = [f[k * 8 : k * 8 + 8, j * C : (j + 1) * C] for f in fields for k in (0, 1)]
        wide = jnp.concatenate(pieces, axis=1)
        for t in range(6):
            row_ref[pl.ds(j * 48 + t, 8, stride=6), :] = wide[:, t * 128 : t * 128 + 128]
    for j in range(16):
        o_ref[j * 48 : j * 48 + 48, :] = row_ref[j * 48 : j * 48 + 48, :].astype(BF16)


def put_taps(tap_ref, slot, field, step):
    row = lax.broadcasted_iota(jnp.int32, (CELLS, C), 0)
    zl_of, x_of, yh_of = (row // 16) % 4, (row % 8) // 2, row % 2

    def ahead(value, rows):
        return pltpu.roll(value, (-rows) % CELLS, 0)

    more = step * ZH
    for a in (-1, 0, 1):
        moved = field
        if a != 0:
            inside = (zl_of + a >= 0) & (zl_of + a < 4)
            if step == 2:
                moved = jnp.where(inside, ahead(field, 16 * a), 0.0)
            else:
                crossed = jnp.where(inside, ahead(field, 15 * a), 0.0)
                moved = jnp.where(yh_of == (0 if a == 1 else 1), ahead(field, a), crossed)
        before = jnp.where(x_of > 0, ahead(moved, -2), 0.0)[CELLS - more :]
        after = jnp.where(x_of < 3, ahead(moved, 2), 0.0)[:more]
        tap_ref[slot, a + 1, PAD - more : PAD, :] = before.astype(BF16)
        tap_ref[slot, a + 1, PAD : PAD + CELLS, :] = moved.astype(BF16)
        tap_ref[slot, a + 1, PAD + CELLS : PAD + CELLS + more, :] = after.astype(BF16)


def get_tap(tap_ref, slot, a, b, step):
    start = PAD + ZH * b * step
    return tap_ref[slot, a + 1, start : start + CELLS, :]


def main_kernel(r_ref, w1_ref, w2_ref, o_ref, keep_ref, send_ref, row_ref, tap_ref, pair_ref):
    row_ref[...] = r_ref[...].astype(F32)

    def unpack(f):
        tiles = [row_ref[pl.ds(3 * f + t, 128, stride=6), :] for t in range(3)]
        part = jnp.concatenate(tiles, axis=1)
        both = [part[:, k * C : (k + 1) * C].reshape(16, 1, 8, C) for k in (0, 1)]
        return jnp.concatenate(both, axis=1).reshape(CELLS, C)

    def pack(value):
        split = value.reshape(16, 2, 8, C)
        return jnp.concatenate([split[:, k].reshape(128, C) for k in (0, 1)], axis=1)

    def forward(slot, w_ref, step):
        total = None
        for t, (a, b) in enumerate(OFFSETS):
            term = jnp.dot(
                get_tap(tap_ref, slot, a, b, step), w_ref[t * C : (t + 1) * C, :], preferred_element_type=F32
            )
            total = term if total is None else total + term
        return total

    def backward(slot, w_ref, step):
        total = None
        for t, (a, b) in enumerate(OFFSETS):
            term = lax.dot_general(
                get_tap(tap_ref, slot, -a, -b, step),
                w_ref[t * C : (t + 1) * C, :],
                (((1,), (1,)), ((), ())),
                preferred_element_type=F32,
            )
            total = term if total is None else total + term
        return total

    x = unpack(0)
    g = unpack(1)
    gelu_one, slope_one = gelu_parts(x)
    act_one = gelu_one.astype(BF16).astype(F32)
    put_taps(tap_ref, 0, act_one, 1)
    put_taps(tap_ref, 2, g, 2)
    hidden = (x + forward(0, w1_ref, 1)).astype(BF16).astype(F32)
    gelu_two, slope_two = gelu_parts(hidden)
    act_two = gelu_two.astype(BF16).astype(F32)
    put_taps(tap_ref, 1, act_two, 2)
    hidden_grad = (g + backward(2, w2_ref, 2) * slope_two).astype(BF16).astype(F32)
    put_taps(tap_ref, 3, hidden_grad, 1)
    output = hidden + forward(1, w2_ref, 2)
    input_grad = hidden_grad + backward(3, w1_ref, 1) * slope_one
    wide = jnp.concatenate([pack(output), pack(input_grad)], axis=1)
    for t in range(6):
        row_ref[t * 128 : t * 128 + 128, :] = wide[:, t * 128 : t * 128 + 128]
    for e in range(8):
        tiles = [row_ref[pl.ds(t * 128 + e, 16, stride=8), :] for t in range(6)]
        o_ref[e * FIELD : (e + 1) * FIELD, :] = jnp.concatenate(tiles, axis=0).astype(BF16)
    for index, (act, grad) in enumerate(((act_two, g), (act_one, hidden_grad))):
        pair_ref[index, 0] = act[:, 0:128].astype(BF16)
        pair_ref[index, 1] = jnp.concatenate([act[:, 128:C], grad[:, 128:C]], axis=1).astype(BF16)
        pair_ref[index, 2] = grad[:, 0:128].astype(BF16)
    core = lax.axis_index("core")
    keep_ref[...] = pair_ref[core]
    send_ref[...] = pair_ref[1 - core]


def half_kernel(own, pair_ref, *refs):
    o_ref, tap_ref, ft_ref = refs[-4:-1] if not own else refs[-3:]
    if not own:
        for c in range(16):
            piece = refs[1][(c // 2) * FIELD : (c // 2 + 1) * FIELD, :].astype(F32)
            refs[-1][c * BOTH + TERMS : (c + 1) * BOTH, :] = piece
    first, mixed, last = [pair_ref[n].astype(F32) for n in range(3)]
    turned = jnp.concatenate([first, mixed[:, 0:64]], axis=1).T
    grad = jnp.concatenate([last, mixed[:, 64:128]], axis=1)
    for n in (0, 1):
        ft_ref[n] = turned[:, n * 128 : n * 128 + 128]
    left = jnp.concatenate(
        [
            jnp.concatenate([ft_ref[n, pl.ds(2 * u + odd, 16, stride=12), :] for n in (0, 1)], axis=1)
            for odd in (0, 1)
            for u in range(6)
        ],
        axis=0,
    ).astype(BF16)

    def weight_grad(step):
        put_taps(tap_ref, 0, grad, step)
        for t, (a, b) in enumerate(OFFSETS):
            full = jnp.dot(left, get_tap(tap_ref, 0, -a, -b, step), preferred_element_type=F32)
            if own:
                o_ref[t] = full
                continue
            full = full + refs[0][t]
            even, odd = full[0:96], full[96:192]
            lanes = (
                even[:, 0:128],
                jnp.concatenate([even[:, 128:192], odd[:, 0:64]], axis=1),
                odd[:, 64:192],
            )
            wg_ref = refs[-1]
            for q in range(3):
                for u in range(6):
                    wg_ref[pl.ds(t * 18 + u * 3 + q, 16, stride=BOTH), :] = lanes[q][
                        u * 16 : u * 16 + 16
                    ]

    for core, step in ((0, 2), (1, 1)):
        pl.when(lax.axis_index("core") == core)(lambda step=step: weight_grad(step))
    if not own:
        o_ref[...] = refs[-1][0 : 16 * BOTH, :].astype(BF16)


def line_kernel(s_ref, out_ref, part_ref, sum_ref, row_ref):
    part_ref[0 : 16 * BOTH, :] = s_ref[...].astype(F32)
    total = part_ref[0:ROWS, :]
    for c in range(1, 16):
        total = total + part_ref[c * BOTH : c * BOTH + ROWS, :]
    sum_ref[0:ROWS, :] = total
    sum_ref[ROWS : ROWS + 16, :] = jnp.zeros((16, 128), F32)
    for zl in range(4):
        piece = sum_ref[zl * PIECE : zl * PIECE + PIECE + 1, :]
        for zh in range(4):
            start = (zh * 4 + zl) * LINE_ROWS + 48
            row_ref[start : start + PIECE + 1, :] = piece
    for half in (0, 1):

        @pl.when(lax.axis_index("yl") == half)
        def _():
            for z in range(16):
                for t in range(6):
                    first = half * BOTH + TERMS + t * 16 + z
                    row_ref[z * LINE_ROWS + t * 8 : z * LINE_ROWS + t * 8 + 8, :] = part_ref[
                        pl.ds(first, 8, stride=2 * BOTH), :
                    ]

    out_ref[...] = row_ref[0 : 16 * LINE_ROWS, :].astype(BF16)


def sum_kernel(r_ref, z_ref, row_ref):
    row_ref[0 : 16 * LINE_ROWS, :] = r_ref[...].astype(F32)
    row_ref[16 * LINE_ROWS :, :] = jnp.zeros((16, 128), F32)
    total = row_ref[48:96, :]
    for z in range(1, 16):
        total = total + row_ref[z * LINE_ROWS + 48 : z * LINE_ROWS + 96, :]
    mine = (total * (1.0 / 256.0)).astype(BF16)
    for z in range(4):
        z_ref[z] = mine


def tile_kernel(r_ref, out_ref, ig_ref, row_ref):
    row_ref[...] = r_ref[...].astype(F32)
    for f, ref in enumerate((out_ref, ig_ref)):
        halves = []
        for k in (0, 1):
            parts = []
            for z in range(16):
                tiles = [
                    row_ref[z * LINE_ROWS + (3 * f + t) * 8 : z * LINE_ROWS + (3 * f + t) * 8 + 8, :]
                    for t in (k, k + 1)
                ]
                both = jnp.concatenate(tiles, axis=1)
                parts.append(both[:, k * 64 : k * 64 + C])
            halves.append(jnp.concatenate(parts, axis=1))
        ref[...] = jnp.concatenate(halves, axis=0).astype(BF16)


def spread_kernel(z_ref, out_ref, row_ref):
    for z in range(4):
        row_ref[z * PIECE : z * PIECE + 48, :] = z_ref[z].astype(F32)
    tiles = [row_ref[pl.ds(v, 8, stride=18), :] for v in range(18)]
    tiles += [row_ref[v : v + 8, :] for v in (144, 152, 160)]
    mine = jnp.concatenate(tiles, axis=1).astype(BF16)
    for c in range(16):
        out_ref[c] = mine


def final_kernel(own, r_ref, *refs):
    one_ref, two_ref, out_ref, sems = refs[-4:]

    def each_copy(part, act):
        lanes = pl.ds(part * 9216, 9216)
        for core in (0, 1):
            target = two_ref if (core == 0) == own else one_ref

            @pl.when(lax.axis_index("core") == core)
            def _(target=target):
                act(
                    pltpu.make_async_copy(
                        out_ref.at[:, lanes], target.at[:, lanes], sems.at[part]
                    )
                )

    for c in range(16):
        lanes = c * 2304
        out_ref[0:8, lanes : lanes + 2304] = r_ref[c, :, 0:2304]
        last = r_ref[c, :, 2304:WIDE].astype(F32)
        for v in range(18):
            row = last[v % 8 : v % 8 + 1, v // 8 * 128 : v // 8 * 128 + 128]
            out_ref[8:9, lanes + v * 128 : lanes + v * 128 + 128] = row.astype(BF16)
        if c % 4 == 3:
            each_copy(c // 4, lambda copy: copy.start())
    for part in range(4):
        each_copy(part, lambda copy: copy.wait())


def exchange(value, axes):
    return lax.all_to_all(value, axes, split_axis=0, concat_axis=0, tiled=True)


def shape(*dims, dtype=BF16):
    return jax.ShapeDtypeStruct(dims, dtype)


def per_device(inputs, first_weight, second_weight, cotangent):
    hbm, vmem = pltpu.HBM, pltpu.VMEM
    swap = [(0, 1), (1, 0)]
    short = pl.CostEstimate(flops=10**9, bytes_accessed=3 * 10**6, transcendentals=0)
    kernel_one = first_weight.reshape(9 * C, C)
    kernel_two = second_weight.reshape(9 * C, C)
    packed = call(
        pack_kernel,
        shape(768, 128),
        scratch=(
            vmem((2, 16, 16 * C), BF16),
            vmem((768, 128), F32),
            pltpu.SemaphoreType.DMA((2,)),
        ),
        spaces={0: hbm, 1: hbm},
        limit=63400000,
    )(inputs, cotangent)
    received = exchange(packed.reshape(384, 2, 128), PEERS).reshape(768, 128)
    fields, keep, send = call(
        main_kernel,
        (shape(8 * FIELD, 128), shape(3, CELLS, 128), shape(3, CELLS, 128)),
        scratch=(
            vmem((768, 128), F32),
            vmem((4, 3, CELLS + 2 * PAD, C), BF16),
            vmem((2, 3, CELLS, 128), BF16),
        ),
    )(received, kernel_one, kernel_two)
    other = lax.ppermute(send, "core", swap)
    scratch = (vmem((1, 3, CELLS + 2 * PAD, C), BF16), vmem((2, C, 128), F32))
    begun = call(
        functools.partial(half_kernel, True),
        shape(9, C, C, dtype=F32),
        scratch=scratch,
        cost_estimate=short,
    )(keep)
    terms = call(
        functools.partial(half_kernel, False),
        shape(16 * BOTH, 128),
        scratch=(*scratch, vmem((16 * BOTH + 8, 128), F32)),
    )(other, begun, fields)
    plane = exchange(terms.reshape(8 * BOTH, 2, 128), PLANE).reshape(16 * BOTH, 128)
    lines = call(
        line_kernel,
        shape(16 * LINE_ROWS, 128),
        scratch=(
            vmem((16 * BOTH + 8, 128), F32),
            vmem((ROWS + 16, 128), F32),
            vmem((16 * LINE_ROWS + 8, 128), F32),
        ),
    )(plane)
    back = exchange(lines.reshape(8 * LINE_ROWS, 2, 128), LINE).reshape(16 * LINE_ROWS, 128)
    mine = call(sum_kernel, shape(4, 48, 128), scratch=(vmem((16 * LINE_ROWS + 16, 128), F32),))(back)
    line = exchange(mine, "zl")
    spread = call(
        spread_kernel, shape(16, 8, WIDE), scratch=(vmem((3 * PIECE + 61, 128), F32),)
    )(line)
    gathered = exchange(spread, PLANE)
    partner = lax.ppermute(gathered, "core", swap)
    output, input_grad = call(
        tile_kernel,
        (shape(16, 16 * C), shape(16, 16 * C)),
        scratch=(vmem((16 * LINE_ROWS, 128), F32),),
        cost_estimate=short,
    )(back)
    weight = shape(9, C * C)
    anywhere = pl.BlockSpec(memory_space=pl.ANY)
    scratch = (vmem((9, C * C), BF16), pltpu.SemaphoreType.DMA((4,)))
    one, two = call(
        functools.partial(final_kernel, True),
        (weight, weight),
        scratch=scratch,
        out_specs=(anywhere, anywhere),
        cost_estimate=short,
    )(gathered)
    one, two = call(
        functools.partial(final_kernel, False),
        (weight, weight),
        scratch=scratch,
        spaces={1: pl.ANY, 2: pl.ANY},
        out_specs=(anywhere, anywhere),
        input_output_aliases={1: 0, 2: 1},
    )(partner, one, two)
    return output, input_grad, one, two


def solution(mesh):
    grid = Mesh(mesh.devices.reshape(SIZES), AXES)
    tile = P(("zl", "yh", "yl"), ("x", "zh", "core"))
    return jax.shard_map(
        per_device,
        mesh=grid,
        in_specs=(tile, P(), P(), tile),
        out_specs=(tile, tile, P(), P()),
        check_vma=False,
    )
```

```python
import functools

import jax
import jax.numpy as jnp
from jax import lax
from jax.experimental import pallas as pl
from jax.experimental.pallas import tpu as pltpu
from jax.sharding import Mesh, PartitionSpec as P

C = 192
AXES = ("zl", "yh", "yl", "x", "zh", "core")
SIZES = (4, 2, 2, 4, 4, 2)
PEERS = ("zh", "zl", "x", "yh")
PLANE = ("x", "yh", "yl")
LINE = ("zh", "zl")
BF16 = jnp.bfloat16
F32 = jnp.float32
ROWS = 168
TERMS = 162
FIELD = 96
BOTH = TERMS + FIELD
PIECE = 41
WIDE = 21 * 128
LINE_ROWS = 48 + PIECE + 1
ZH = 64
PAD = 2 * ZH
CELLS = 256
OFFSETS = [(a, b) for a in (-1, 0, 1) for b in (-1, 0, 1)]


def call(kernel, out_shape, scratch=(), spaces={}, out_specs=None, limit=40 * 1024 * 1024, **extra):
    if out_specs is None:
        out_specs = jax.tree.map(lambda _: pl.BlockSpec(memory_space=pltpu.VMEM), out_shape)

    def run(*args):
        return pl.pallas_call(
            kernel,
            out_shape=out_shape,
            in_specs=[
                pl.BlockSpec(memory_space=spaces.get(n, pltpu.VMEM)) for n in range(len(args))
            ],
            out_specs=out_specs,
            scratch_shapes=list(scratch),
            compiler_params=pltpu.CompilerParams(vmem_limit_bytes=limit),
            **extra,
        )(*args)

    return run


def gelu_parts(value):
    normal_cdf = 0.5 * (1.0 + lax.erf(value * 0.7071067811865476))
    density = jnp.exp(-0.5 * value * value) * 0.3989422804014327
    return value * normal_cdf, normal_cdf + value * density


def pack_kernel(x_hbm, g_hbm, o_ref, in_ref, row_ref, sems):
    copies = [pltpu.make_async_copy(h, in_ref.at[n], sems.at[n]) for n, h in enumerate((x_hbm, g_hbm))]
    for copy in copies:
        copy.start()
    for copy in copies:
        copy.wait()
    fields = [in_ref[n].astype(F32) for n in (0, 1)]
    for j in range(16):
        pieces = [f[k * 8 : k * 8 + 8, j * C : (j + 1) * C] for f in fields for k in (0, 1)]
        wide = jnp.concatenate(pieces, axis=1)
        for t in range(6):
            row_ref[pl.ds(j * 48 + t, 8, stride=6), :] = wide[:, t * 128 : t * 128 + 128]
    for j in range(16):
        o_ref[j * 48 : j * 48 + 48, :] = row_ref[j * 48 : j * 48 + 48, :].astype(BF16)


def put_taps(tap_ref, slot, field, step):
    row = lax.broadcasted_iota(jnp.int32, (CELLS, C), 0)
    zl_of, x_of, yh_of = (row // 16) % 4, (row % 8) // 2, row % 2

    def ahead(value, rows):
        return pltpu.roll(value, (-rows) % CELLS, 0)

    more = step * ZH
    for a in (-1, 0, 1):
        moved = field
        if a != 0:
            inside = (zl_of + a >= 0) & (zl_of + a < 4)
            if step == 2:
                moved = jnp.where(inside, ahead(field, 16 * a), 0.0)
            else:
                crossed = jnp.where(inside, ahead(field, 15 * a), 0.0)
                moved = jnp.where(yh_of == (0 if a == 1 else 1), ahead(field, a), crossed)
        before = jnp.where(x_of > 0, ahead(moved, -2), 0.0)[CELLS - more :]
        after = jnp.where(x_of < 3, ahead(moved, 2), 0.0)[:more]
        tap_ref[slot, a + 1, PAD - more : PAD, :] = before.astype(BF16)
        tap_ref[slot, a + 1, PAD : PAD + CELLS, :] = moved.astype(BF16)
        tap_ref[slot, a + 1, PAD + CELLS : PAD + CELLS + more, :] = after.astype(BF16)


def get_tap(tap_ref, slot, a, b, step):
    start = PAD + ZH * b * step
    return tap_ref[slot, a + 1, start : start + CELLS, :]


def forward(tap_ref, slot, w_ref, step):
    total = None
    for t, (a, b) in enumerate(OFFSETS):
        term = jnp.dot(
            get_tap(tap_ref, slot, a, b, step), w_ref[t * C : (t + 1) * C, :], preferred_element_type=F32
        )
        total = term if total is None else total + term
    return total


def backward(tap_ref, slot, w_ref, step):
    total = None
    for t, (a, b) in enumerate(OFFSETS):
        term = lax.dot_general(
            get_tap(tap_ref, slot, -a, -b, step),
            w_ref[t * C : (t + 1) * C, :],
            (((1,), (1,)), ((), ())),
            preferred_element_type=F32,
        )
        total = term if total is None else total + term
    return total


def unpack(row_ref, f):
    tiles = [row_ref[pl.ds(3 * f + t, 128, stride=6), :] for t in range(3)]
    part = jnp.concatenate(tiles, axis=1)
    both = [part[:, k * C : (k + 1) * C].reshape(16, 1, 8, C) for k in (0, 1)]
    return jnp.concatenate(both, axis=1).reshape(CELLS, C)


def main_kernel(r_ref, w1_ref, w2_ref, keep_ref, send_ref, mid_ref, row_ref, tap_ref, pair_ref):
    row_ref[...] = r_ref[...].astype(F32)
    x = unpack(row_ref, 0)
    g = unpack(row_ref, 1)
    act_one = gelu_parts(x)[0].astype(BF16).astype(F32)
    put_taps(tap_ref, 0, act_one, 1)
    put_taps(tap_ref, 1, g, 2)
    hidden = (x + forward(tap_ref, 0, w1_ref, 1)).astype(BF16)
    gelu_two, slope_two = gelu_parts(hidden.astype(F32))
    act_two = gelu_two.astype(BF16).astype(F32)
    hidden_grad = (g + backward(tap_ref, 1, w2_ref, 2) * slope_two).astype(BF16)
    mid_ref[0] = hidden
    mid_ref[1] = hidden_grad
    hidden_grad = hidden_grad.astype(F32)
    for index, (act, grad) in enumerate(((act_two, g), (act_one, hidden_grad))):
        pair_ref[index, 0] = act[:, 0:128].astype(BF16)
        pair_ref[index, 1] = jnp.concatenate([act[:, 128:C], grad[:, 128:C]], axis=1).astype(BF16)
        pair_ref[index, 2] = grad[:, 0:128].astype(BF16)
    core = lax.axis_index("core")
    keep_ref[...] = pair_ref[core]
    send_ref[...] = pair_ref[1 - core]


def field_kernel(r_ref, w1_ref, w2_ref, mid_ref, o_ref, row_ref, tap_ref):
    def pack(value):
        split = value.reshape(16, 2, 8, C)
        return jnp.concatenate([split[:, k].reshape(128, C) for k in (0, 1)], axis=1)

    row_ref[...] = r_ref[...].astype(F32)
    slope_one = gelu_parts(unpack(row_ref, 0))[1]
    hidden, hidden_grad = mid_ref[0].astype(F32), mid_ref[1].astype(F32)
    act_two = gelu_parts(hidden)[0].astype(BF16).astype(F32)
    put_taps(tap_ref, 0, act_two, 2)
    put_taps(tap_ref, 1, hidden_grad, 1)
    output = hidden + forward(tap_ref, 0, w2_ref, 2)
    input_grad = hidden_grad + backward(tap_ref, 1, w1_ref, 1) * slope_one
    wide = jnp.concatenate([pack(output), pack(input_grad)], axis=1)
    for t in range(6):
        row_ref[t * 128 : t * 128 + 128, :] = wide[:, t * 128 : t * 128 + 128]
    for e in range(8):
        tiles = [row_ref[pl.ds(t * 128 + e, 16, stride=8), :] for t in range(6)]
        o_ref[e * FIELD : (e + 1) * FIELD, :] = jnp.concatenate(tiles, axis=0).astype(BF16)


def half_kernel(own, pair_ref, *refs):
    o_ref, tap_ref, ft_ref = refs[-4:-1] if not own else refs[-3:]
    if not own:
        for c in range(16):
            piece = refs[1][(c // 2) * FIELD : (c // 2 + 1) * FIELD, :].astype(F32)
            refs[-1][c * BOTH + TERMS : (c + 1) * BOTH, :] = piece
    first, mixed, last = [pair_ref[n].astype(F32) for n in range(3)]
    turned = jnp.concatenate([first, mixed[:, 0:64]], axis=1).T
    grad = jnp.concatenate([last, mixed[:, 64:128]], axis=1)
    for n in (0, 1):
        ft_ref[n] = turned[:, n * 128 : n * 128 + 128]
    left = jnp.concatenate(
        [
            jnp.concatenate([ft_ref[n, pl.ds(2 * u + odd, 16, stride=12), :] for n in (0, 1)], axis=1)
            for odd in (0, 1)
            for u in range(6)
        ],
        axis=0,
    ).astype(BF16)

    def weight_grad(step):
        put_taps(tap_ref, 0, grad, step)
        for t, (a, b) in enumerate(OFFSETS):
            full = jnp.dot(left, get_tap(tap_ref, 0, -a, -b, step), preferred_element_type=F32)
            if own:
                o_ref[t] = full
                continue
            full = full + refs[0][t]
            even, odd = full[0:96], full[96:192]
            lanes = (
                even[:, 0:128],
                jnp.concatenate([even[:, 128:192], odd[:, 0:64]], axis=1),
                odd[:, 64:192],
            )
            wg_ref = refs[-1]
            for q in range(3):
                for u in range(6):
                    wg_ref[pl.ds(t * 18 + u * 3 + q, 16, stride=BOTH), :] = lanes[q][
                        u * 16 : u * 16 + 16
                    ]

    for core, step in ((0, 2), (1, 1)):
        pl.when(lax.axis_index("core") == core)(lambda step=step: weight_grad(step))
    if not own:
        o_ref[...] = refs[-1][0 : 16 * BOTH, :].astype(BF16)


def line_kernel(s_ref, out_ref, part_ref, sum_ref, row_ref):
    part_ref[0 : 16 * BOTH, :] = s_ref[...].astype(F32)
    total = part_ref[0:ROWS, :]
    for c in range(1, 16):
        total = total + part_ref[c * BOTH : c * BOTH + ROWS, :]
    sum_ref[0:ROWS, :] = total
    sum_ref[ROWS : ROWS + 16, :] = jnp.zeros((16, 128), F32)
    for zl in range(4):
        piece = sum_ref[zl * PIECE : zl * PIECE + PIECE + 1, :]
        for zh in range(4):
            start = (zh * 4 + zl) * LINE_ROWS + 48
            row_ref[start : start + PIECE + 1, :] = piece
    for half in (0, 1):

        @pl.when(lax.axis_index("yl") == half)
        def _():
            for z in range(16):
                for t in range(6):
                    first = half * BOTH + TERMS + t * 16 + z
                    row_ref[z * LINE_ROWS + t * 8 : z * LINE_ROWS + t * 8 + 8, :] = part_ref[
                        pl.ds(first, 8, stride=2 * BOTH), :
                    ]

    out_ref[...] = row_ref[0 : 16 * LINE_ROWS, :].astype(BF16)


def sum_kernel(r_ref, z_ref, row_ref):
    row_ref[0 : 16 * LINE_ROWS, :] = r_ref[...].astype(F32)
    row_ref[16 * LINE_ROWS :, :] = jnp.zeros((16, 128), F32)
    total = row_ref[48:96, :]
    for z in range(1, 16):
        total = total + row_ref[z * LINE_ROWS + 48 : z * LINE_ROWS + 96, :]
    mine = (total * (1.0 / 256.0)).astype(BF16)
    for z in range(4):
        z_ref[z] = mine


def tile_kernel(r_ref, out_ref, ig_ref, row_ref):
    row_ref[...] = r_ref[...].astype(F32)
    for f, ref in enumerate((out_ref, ig_ref)):
        halves = []
        for k in (0, 1):
            parts = []
            for z in range(16):
                tiles = [
                    row_ref[z * LINE_ROWS + (3 * f + t) * 8 : z * LINE_ROWS + (3 * f + t) * 8 + 8, :]
                    for t in (k, k + 1)
                ]
                both = jnp.concatenate(tiles, axis=1)
                parts.append(both[:, k * 64 : k * 64 + C])
            halves.append(jnp.concatenate(parts, axis=1))
        ref[...] = jnp.concatenate(halves, axis=0).astype(BF16)


def spread_kernel(z_ref, out_ref, row_ref):
    for z in range(4):
        row_ref[z * PIECE : z * PIECE + 48, :] = z_ref[z].astype(F32)
    tiles = [row_ref[pl.ds(v, 8, stride=18), :] for v in range(18)]
    tiles += [row_ref[v : v + 8, :] for v in (144, 152, 160)]
    mine = jnp.concatenate(tiles, axis=1).astype(BF16)
    for c in range(16):
        out_ref[c] = mine


def final_kernel(own, r_ref, *refs):
    one_ref, two_ref, out_ref, sems = refs[-4:]

    def each_copy(part, act):
        lanes = pl.ds(part * 9216, 9216)
        for core in (0, 1):
            target = two_ref if (core == 0) == own else one_ref

            @pl.when(lax.axis_index("core") == core)
            def _(target=target):
                act(
                    pltpu.make_async_copy(
                        out_ref.at[:, lanes], target.at[:, lanes], sems.at[part]
                    )
                )

    for c in range(16):
        lanes = c * 2304
        out_ref[0:8, lanes : lanes + 2304] = r_ref[c, :, 0:2304]
        last = r_ref[c, :, 2304:WIDE].astype(F32)
        for v in range(18):
            row = last[v % 8 : v % 8 + 1, v // 8 * 128 : v // 8 * 128 + 128]
            out_ref[8:9, lanes + v * 128 : lanes + v * 128 + 128] = row.astype(BF16)
        if c % 4 == 3:
            each_copy(c // 4, lambda copy: copy.start())
    for part in range(4):
        each_copy(part, lambda copy: copy.wait())


def exchange(value, axes):
    return lax.all_to_all(value, axes, split_axis=0, concat_axis=0, tiled=True)


def shape(*dims, dtype=BF16):
    return jax.ShapeDtypeStruct(dims, dtype)


def per_device(inputs, first_weight, second_weight, cotangent):
    hbm, vmem = pltpu.HBM, pltpu.VMEM
    swap = [(0, 1), (1, 0)]
    short = pl.CostEstimate(flops=10**9, bytes_accessed=3 * 10**6, transcendentals=0)
    kernel_one = first_weight.reshape(9 * C, C)
    kernel_two = second_weight.reshape(9 * C, C)
    packed = call(
        pack_kernel,
        shape(768, 128),
        scratch=(
            vmem((2, 16, 16 * C), BF16),
            vmem((768, 128), F32),
            pltpu.SemaphoreType.DMA((2,)),
        ),
        spaces={0: hbm, 1: hbm},
        limit=63400000,
    )(inputs, cotangent)
    received = exchange(packed.reshape(384, 2, 128), PEERS).reshape(768, 128)
    taps = vmem((2, 3, CELLS + 2 * PAD, C), BF16)
    keep, send, middle = call(
        main_kernel,
        (shape(3, CELLS, 128), shape(3, CELLS, 128), shape(2, CELLS, C)),
        scratch=(vmem((768, 128), F32), taps, vmem((2, 3, CELLS, 128), BF16)),
    )(received, kernel_one, kernel_two)
    other = lax.ppermute(send, "core", swap)
    scratch = (vmem((1, 3, CELLS + 2 * PAD, C), BF16), vmem((2, C, 128), F32))
    begun = call(
        functools.partial(half_kernel, True),
        shape(9, C, C, dtype=F32),
        scratch=scratch,
        cost_estimate=short,
    )(keep)
    fields = call(
        field_kernel,
        shape(8 * FIELD, 128),
        scratch=(vmem((768, 128), F32), taps),
        cost_estimate=short,
    )(received, kernel_one, kernel_two, middle)
    terms = call(
        functools.partial(half_kernel, False),
        shape(16 * BOTH, 128),
        scratch=(*scratch, vmem((16 * BOTH + 8, 128), F32)),
    )(other, begun, fields)
    plane = exchange(terms.reshape(8 * BOTH, 2, 128), PLANE).reshape(16 * BOTH, 128)
    lines = call(
        line_kernel,
        shape(16 * LINE_ROWS, 128),
        scratch=(
            vmem((16 * BOTH + 8, 128), F32),
            vmem((ROWS + 16, 128), F32),
            vmem((16 * LINE_ROWS + 8, 128), F32),
        ),
    )(plane)
    back = exchange(lines.reshape(8 * LINE_ROWS, 2, 128), LINE).reshape(16 * LINE_ROWS, 128)
    mine = call(sum_kernel, shape(4, 48, 128), scratch=(vmem((16 * LINE_ROWS + 16, 128), F32),))(back)
    line = exchange(mine, "zl")
    spread = call(
        spread_kernel, shape(16, 8, WIDE), scratch=(vmem((3 * PIECE + 61, 128), F32),)
    )(line)
    gathered = exchange(spread, PLANE)
    partner = lax.ppermute(gathered, "core", swap)
    output, input_grad = call(
        tile_kernel,
        (shape(16, 16 * C), shape(16, 16 * C)),
        scratch=(vmem((16 * LINE_ROWS, 128), F32),),
        cost_estimate=short,
    )(back)
    weight = shape(9, C * C)
    anywhere = pl.BlockSpec(memory_space=pl.ANY)
    scratch = (vmem((9, C * C), BF16), pltpu.SemaphoreType.DMA((4,)))
    one, two = call(
        functools.partial(final_kernel, True),
        (weight, weight),
        scratch=scratch,
        out_specs=(anywhere, anywhere),
        cost_estimate=short,
    )(gathered)
    one, two = call(
        functools.partial(final_kernel, False),
        (weight, weight),
        scratch=scratch,
        spaces={1: pl.ANY, 2: pl.ANY},
        out_specs=(anywhere, anywhere),
        input_output_aliases={1: 0, 2: 1},
    )(partner, one, two)
    return output, input_grad, one, two


def solution(mesh):
    grid = Mesh(mesh.devices.reshape(SIZES), AXES)
    tile = P(("zl", "yh", "yl"), ("x", "zh", "core"))
    return jax.shard_map(
        per_device,
        mesh=grid,
        in_specs=(tile, P(), P(), tile),
        out_specs=(tile, tile, P(), P()),
        check_vma=False,
    )
```

```python
import functools

import jax
import jax.numpy as jnp
from jax import lax
from jax.experimental import pallas as pl
from jax.experimental.pallas import tpu as pltpu
from jax.sharding import Mesh, PartitionSpec as P

C = 192
AXES = ("zl", "yh", "yl", "x", "zh", "core")
SIZES = (4, 2, 2, 4, 4, 2)
PEERS = ("zh", "zl", "x", "yh")
PLANE = ("x", "yh", "yl")
LINE = ("zh", "zl")
BF16 = jnp.bfloat16
F32 = jnp.float32
ROWS = 168
TERMS = 162
FIELD = 96
BOTH = TERMS + FIELD
PIECE = 41
WIDE = 21 * 128
LINE_ROWS = 48 + PIECE + 1
ZH = 64
PAD = 2 * ZH
CELLS = 256
OFFSETS = [(a, b) for a in (-1, 0, 1) for b in (-1, 0, 1)]


def call(kernel, out_shape, scratch=(), spaces={}, out_specs=None, limit=40 * 1024 * 1024, **extra):
    if out_specs is None:
        out_specs = jax.tree.map(lambda _: pl.BlockSpec(memory_space=pltpu.VMEM), out_shape)

    def run(*args):
        return pl.pallas_call(
            kernel,
            out_shape=out_shape,
            in_specs=[
                pl.BlockSpec(memory_space=spaces.get(n, pltpu.VMEM)) for n in range(len(args))
            ],
            out_specs=out_specs,
            scratch_shapes=list(scratch),
            compiler_params=pltpu.CompilerParams(vmem_limit_bytes=limit),
            **extra,
        )(*args)

    return run


def gelu_parts(value):
    normal_cdf = 0.5 * (1.0 + lax.erf(value * 0.7071067811865476))
    density = jnp.exp(-0.5 * value * value) * 0.3989422804014327
    return value * normal_cdf, normal_cdf + value * density


def pack_kernel(x_hbm, g_hbm, o_ref, in_ref, row_ref, sems):
    copies = [pltpu.make_async_copy(h, in_ref.at[n], sems.at[n]) for n, h in enumerate((x_hbm, g_hbm))]
    for copy in copies:
        copy.start()
    for copy in copies:
        copy.wait()
    fields = [in_ref[n].astype(F32) for n in (0, 1)]
    for j in range(16):
        pieces = [f[k * 8 : k * 8 + 8, j * C : (j + 1) * C] for f in fields for k in (0, 1)]
        wide = jnp.concatenate(pieces, axis=1)
        for t in range(6):
            row_ref[pl.ds(j * 48 + t, 8, stride=6), :] = wide[:, t * 128 : t * 128 + 128]
    for j in range(16):
        o_ref[j * 48 : j * 48 + 48, :] = row_ref[j * 48 : j * 48 + 48, :].astype(BF16)


def put_taps(tap_ref, slot, field, step):
    row = lax.broadcasted_iota(jnp.int32, (CELLS, C), 0)
    zl_of, x_of, yh_of = (row // 16) % 4, (row % 8) // 2, row % 2

    def ahead(value, rows):
        return pltpu.roll(value, (-rows) % CELLS, 0)

    more = step * ZH
    for a in (-1, 0, 1):
        moved = field
        if a != 0:
            inside = (zl_of + a >= 0) & (zl_of + a < 4)
            if step == 2:
                moved = jnp.where(inside, ahead(field, 16 * a), 0.0)
            else:
                crossed = jnp.where(inside, ahead(field, 15 * a), 0.0)
                moved = jnp.where(yh_of == (0 if a == 1 else 1), ahead(field, a), crossed)
        before = jnp.where(x_of > 0, ahead(moved, -2), 0.0)[CELLS - more :]
        after = jnp.where(x_of < 3, ahead(moved, 2), 0.0)[:more]
        tap_ref[slot, a + 1, PAD - more : PAD, :] = before.astype(BF16)
        tap_ref[slot, a + 1, PAD : PAD + CELLS, :] = moved.astype(BF16)
        tap_ref[slot, a + 1, PAD + CELLS : PAD + CELLS + more, :] = after.astype(BF16)


def get_tap(tap_ref, slot, a, b, step):
    start = PAD + ZH * b * step
    return tap_ref[slot, a + 1, start : start + CELLS, :]


def forward(tap_ref, slot, w_ref, step):
    total = None
    for t, (a, b) in enumerate(OFFSETS):
        term = jnp.dot(
            get_tap(tap_ref, slot, a, b, step), w_ref[t * C : (t + 1) * C, :], preferred_element_type=F32
        )
        total = term if total is None else total + term
    return total


def backward(tap_ref, slot, w_ref, step):
    total = None
    for t, (a, b) in enumerate(OFFSETS):
        term = lax.dot_general(
            get_tap(tap_ref, slot, -a, -b, step),
            w_ref[t * C : (t + 1) * C, :],
            (((1,), (1,)), ((), ())),
            preferred_element_type=F32,
        )
        total = term if total is None else total + term
    return total


def unpack(row_ref, f):
    tiles = [row_ref[pl.ds(3 * f + t, 128, stride=6), :] for t in range(3)]
    part = jnp.concatenate(tiles, axis=1)
    both = [part[:, k * C : (k + 1) * C].reshape(16, 1, 8, C) for k in (0, 1)]
    return jnp.concatenate(both, axis=1).reshape(CELLS, C)


def main_kernel(r_ref, w1_ref, w2_ref, keep_ref, send_ref, mid_ref, row_ref, tap_ref, pair_ref):
    row_ref[...] = r_ref[...].astype(F32)
    g = unpack(row_ref, 1)
    put_taps(tap_ref, 1, g, 2)
    back_two = backward(tap_ref, 1, w2_ref, 2)
    x = unpack(row_ref, 0)
    act_one = gelu_parts(x)[0].astype(BF16).astype(F32)
    put_taps(tap_ref, 0, act_one, 1)
    hidden = (x + forward(tap_ref, 0, w1_ref, 1)).astype(BF16)
    gelu_two, slope_two = gelu_parts(hidden.astype(F32))
    act_two = gelu_two.astype(BF16).astype(F32)
    hidden_grad = (g + back_two * slope_two).astype(BF16)
    mid_ref[0] = hidden
    mid_ref[1] = hidden_grad
    hidden_grad = hidden_grad.astype(F32)
    for index, (act, grad) in enumerate(((act_two, g), (act_one, hidden_grad))):
        pair_ref[index, 0] = act[:, 0:128].astype(BF16)
        pair_ref[index, 1] = jnp.concatenate([act[:, 128:C], grad[:, 128:C]], axis=1).astype(BF16)
        pair_ref[index, 2] = grad[:, 0:128].astype(BF16)
    core = lax.axis_index("core")
    keep_ref[...] = pair_ref[core]
    send_ref[...] = pair_ref[1 - core]


def field_kernel(r_ref, w1_ref, w2_ref, mid_ref, o_ref, row_ref, tap_ref):
    def pack(value):
        split = value.reshape(16, 2, 8, C)
        return jnp.concatenate([split[:, k].reshape(128, C) for k in (0, 1)], axis=1)

    row_ref[...] = r_ref[...].astype(F32)
    hidden, hidden_grad = mid_ref[0].astype(F32), mid_ref[1].astype(F32)
    put_taps(tap_ref, 1, hidden_grad, 1)
    back_one = backward(tap_ref, 1, w1_ref, 1)
    slope_one = gelu_parts(unpack(row_ref, 0))[1]
    act_two = gelu_parts(hidden)[0].astype(BF16).astype(F32)
    put_taps(tap_ref, 0, act_two, 2)
    output = hidden + forward(tap_ref, 0, w2_ref, 2)
    input_grad = hidden_grad + back_one * slope_one
    wide = jnp.concatenate([pack(output), pack(input_grad)], axis=1)
    for t in range(6):
        row_ref[t * 128 : t * 128 + 128, :] = wide[:, t * 128 : t * 128 + 128]
    for e in range(8):
        tiles = [row_ref[pl.ds(t * 128 + e, 16, stride=8), :] for t in range(6)]
        o_ref[e * FIELD : (e + 1) * FIELD, :] = jnp.concatenate(tiles, axis=0).astype(BF16)


def half_kernel(own, pair_ref, *refs):
    o_ref, tap_ref, ft_ref = refs[-4:-1] if not own else refs[-3:]
    if not own:
        for c in range(16):
            piece = refs[1][(c // 2) * FIELD : (c // 2 + 1) * FIELD, :].astype(F32)
            refs[-1][c * BOTH + TERMS : (c + 1) * BOTH, :] = piece
    first, mixed, last = [pair_ref[n].astype(F32) for n in range(3)]
    turned = jnp.concatenate([first, mixed[:, 0:64]], axis=1).T
    grad = jnp.concatenate([last, mixed[:, 64:128]], axis=1)
    for n in (0, 1):
        ft_ref[n] = turned[:, n * 128 : n * 128 + 128]
    left = jnp.concatenate(
        [
            jnp.concatenate([ft_ref[n, pl.ds(2 * u + odd, 16, stride=12), :] for n in (0, 1)], axis=1)
            for odd in (0, 1)
            for u in range(6)
        ],
        axis=0,
    ).astype(BF16)

    def weight_grad(step):
        put_taps(tap_ref, 0, grad, step)
        for t, (a, b) in enumerate(OFFSETS):
            full = jnp.dot(left, get_tap(tap_ref, 0, -a, -b, step), preferred_element_type=F32)
            if own:
                o_ref[t] = full
                continue
            full = full + refs[0][t]
            even, odd = full[0:96], full[96:192]
            lanes = (
                even[:, 0:128],
                jnp.concatenate([even[:, 128:192], odd[:, 0:64]], axis=1),
                odd[:, 64:192],
            )
            wg_ref = refs[-1]
            for q in range(3):
                for u in range(6):
                    wg_ref[pl.ds(t * 18 + u * 3 + q, 16, stride=BOTH), :] = lanes[q][
                        u * 16 : u * 16 + 16
                    ]

    for core, step in ((0, 2), (1, 1)):
        pl.when(lax.axis_index("core") == core)(lambda step=step: weight_grad(step))
    if not own:
        o_ref[...] = refs[-1][0 : 16 * BOTH, :].astype(BF16)


def line_kernel(s_ref, out_ref, part_ref, sum_ref, row_ref):
    part_ref[0 : 16 * BOTH, :] = s_ref[...].astype(F32)
    total = part_ref[0:ROWS, :]
    for c in range(1, 16):
        total = total + part_ref[c * BOTH : c * BOTH + ROWS, :]
    sum_ref[0:ROWS, :] = total
    sum_ref[ROWS : ROWS + 16, :] = jnp.zeros((16, 128), F32)
    for zl in range(4):
        piece = sum_ref[zl * PIECE : zl * PIECE + PIECE + 1, :]
        for zh in range(4):
            start = (zh * 4 + zl) * LINE_ROWS + 48
            row_ref[start : start + PIECE + 1, :] = piece
    for half in (0, 1):

        @pl.when(lax.axis_index("yl") == half)
        def _():
            for z in range(16):
                for t in range(6):
                    first = half * BOTH + TERMS + t * 16 + z
                    row_ref[z * LINE_ROWS + t * 8 : z * LINE_ROWS + t * 8 + 8, :] = part_ref[
                        pl.ds(first, 8, stride=2 * BOTH), :
                    ]

    out_ref[...] = row_ref[0 : 16 * LINE_ROWS, :].astype(BF16)


def sum_kernel(r_ref, z_ref, row_ref):
    row_ref[0 : 16 * LINE_ROWS, :] = r_ref[...].astype(F32)
    row_ref[16 * LINE_ROWS :, :] = jnp.zeros((16, 128), F32)
    total = row_ref[48:96, :]
    for z in range(1, 16):
        total = total + row_ref[z * LINE_ROWS + 48 : z * LINE_ROWS + 96, :]
    mine = (total * (1.0 / 256.0)).astype(BF16)
    for z in range(4):
        z_ref[z] = mine


def tile_kernel(r_ref, out_ref, ig_ref, row_ref):
    row_ref[...] = r_ref[...].astype(F32)
    for f, ref in enumerate((out_ref, ig_ref)):
        halves = []
        for k in (0, 1):
            parts = []
            for z in range(16):
                tiles = [
                    row_ref[z * LINE_ROWS + (3 * f + t) * 8 : z * LINE_ROWS + (3 * f + t) * 8 + 8, :]
                    for t in (k, k + 1)
                ]
                both = jnp.concatenate(tiles, axis=1)
                parts.append(both[:, k * 64 : k * 64 + C])
            halves.append(jnp.concatenate(parts, axis=1))
        ref[...] = jnp.concatenate(halves, axis=0).astype(BF16)


def spread_kernel(z_ref, out_ref, row_ref):
    for z in range(4):
        row_ref[z * PIECE : z * PIECE + 48, :] = z_ref[z].astype(F32)
    tiles = [row_ref[pl.ds(v, 8, stride=18), :] for v in range(18)]
    tiles += [row_ref[v : v + 8, :] for v in (144, 152, 160)]
    mine = jnp.concatenate(tiles, axis=1).astype(BF16)
    for c in range(16):
        out_ref[c] = mine


def final_kernel(own, r_ref, *refs):
    one_ref, two_ref, out_ref, sems = refs[-4:]

    def each_copy(part, act):
        lanes = pl.ds(part * 9216, 9216)
        for core in (0, 1):
            target = two_ref if (core == 0) == own else one_ref

            @pl.when(lax.axis_index("core") == core)
            def _(target=target):
                act(
                    pltpu.make_async_copy(
                        out_ref.at[:, lanes], target.at[:, lanes], sems.at[part]
                    )
                )

    for c in range(16):
        lanes = c * 2304
        out_ref[0:8, lanes : lanes + 2304] = r_ref[c, :, 0:2304]
        last = r_ref[c, :, 2304:WIDE].astype(F32)
        for v in range(18):
            row = last[v % 8 : v % 8 + 1, v // 8 * 128 : v // 8 * 128 + 128]
            out_ref[8:9, lanes + v * 128 : lanes + v * 128 + 128] = row.astype(BF16)
        if c % 4 == 3:
            each_copy(c // 4, lambda copy: copy.start())
    for part in range(4):
        each_copy(part, lambda copy: copy.wait())


def exchange(value, axes):
    return lax.all_to_all(value, axes, split_axis=0, concat_axis=0, tiled=True)


def shape(*dims, dtype=BF16):
    return jax.ShapeDtypeStruct(dims, dtype)


def per_device(inputs, first_weight, second_weight, cotangent):
    hbm, vmem = pltpu.HBM, pltpu.VMEM
    swap = [(0, 1), (1, 0)]
    short = pl.CostEstimate(flops=10**9, bytes_accessed=3 * 10**6, transcendentals=0)
    kernel_one = first_weight.reshape(9 * C, C)
    kernel_two = second_weight.reshape(9 * C, C)
    packed = call(
        pack_kernel,
        shape(768, 128),
        scratch=(
            vmem((2, 16, 16 * C), BF16),
            vmem((768, 128), F32),
            pltpu.SemaphoreType.DMA((2,)),
        ),
        spaces={0: hbm, 1: hbm},
        limit=63400000,
    )(inputs, cotangent)
    received = exchange(packed.reshape(384, 2, 128), PEERS).reshape(768, 128)
    taps = vmem((2, 3, CELLS + 2 * PAD, C), BF16)
    keep, send, middle = call(
        main_kernel,
        (shape(3, CELLS, 128), shape(3, CELLS, 128), shape(2, CELLS, C)),
        scratch=(vmem((768, 128), F32), taps, vmem((2, 3, CELLS, 128), BF16)),
    )(received, kernel_one, kernel_two)
    other = lax.ppermute(send, "core", swap)
    scratch = (vmem((1, 3, CELLS + 2 * PAD, C), BF16), vmem((2, C, 128), F32))
    begun = call(
        functools.partial(half_kernel, True),
        shape(9, C, C, dtype=F32),
        scratch=scratch,
        cost_estimate=short,
    )(keep)
    fields = call(
        field_kernel,
        shape(8 * FIELD, 128),
        scratch=(vmem((768, 128), F32), taps),
        cost_estimate=short,
    )(received, kernel_one, kernel_two, middle)
    terms = call(
        functools.partial(half_kernel, False),
        shape(16 * BOTH, 128),
        scratch=(*scratch, vmem((16 * BOTH + 8, 128), F32)),
    )(other, begun, fields)
    plane = exchange(terms.reshape(8 * BOTH, 2, 128), PLANE).reshape(16 * BOTH, 128)
    lines = call(
        line_kernel,
        shape(16 * LINE_ROWS, 128),
        scratch=(
            vmem((16 * BOTH + 8, 128), F32),
            vmem((ROWS + 16, 128), F32),
            vmem((16 * LINE_ROWS + 8, 128), F32),
        ),
    )(plane)
    back = exchange(lines.reshape(8 * LINE_ROWS, 2, 128), LINE).reshape(16 * LINE_ROWS, 128)
    mine = call(sum_kernel, shape(4, 48, 128), scratch=(vmem((16 * LINE_ROWS + 16, 128), F32),))(back)
    line = exchange(mine, "zl")
    spread = call(
        spread_kernel, shape(16, 8, WIDE), scratch=(vmem((3 * PIECE + 61, 128), F32),)
    )(line)
    gathered = exchange(spread, PLANE)
    partner = lax.ppermute(gathered, "core", swap)
    output, input_grad = call(
        tile_kernel,
        (shape(16, 16 * C), shape(16, 16 * C)),
        scratch=(vmem((16 * LINE_ROWS, 128), F32),),
        cost_estimate=short,
    )(back)
    weight = shape(9, C * C)
    anywhere = pl.BlockSpec(memory_space=pl.ANY)
    scratch = (vmem((9, C * C), BF16), pltpu.SemaphoreType.DMA((4,)))
    one, two = call(
        functools.partial(final_kernel, True),
        (weight, weight),
        scratch=scratch,
        out_specs=(anywhere, anywhere),
        cost_estimate=short,
    )(gathered)
    one, two = call(
        functools.partial(final_kernel, False),
        (weight, weight),
        scratch=scratch,
        spaces={1: pl.ANY, 2: pl.ANY},
        out_specs=(anywhere, anywhere),
        input_output_aliases={1: 0, 2: 1},
    )(partner, one, two)
    return output, input_grad, one, two


def solution(mesh):
    grid = Mesh(mesh.devices.reshape(SIZES), AXES)
    tile = P(("zl", "yh", "yl"), ("x", "zh", "core"))
    return jax.shard_map(
        per_device,
        mesh=grid,
        in_specs=(tile, P(), P(), tile),
        out_specs=(tile, tile, P(), P()),
        check_vma=False,
    )
```

```python
import functools

import jax
import jax.numpy as jnp
from jax import lax
from jax.experimental import pallas as pl
from jax.experimental.pallas import tpu as pltpu
from jax.sharding import Mesh, PartitionSpec as P

C = 192
AXES = ("zl", "yh", "yl", "x", "zh", "core")
SIZES = (4, 2, 2, 4, 4, 2)
PEERS = ("zh", "zl", "x", "yh")
PLANE = ("x", "yh", "yl")
LINE = ("zh", "zl")
BF16 = jnp.bfloat16
F32 = jnp.float32
ROWS = 168
TERMS = 162
FIELD = 96
BOTH = TERMS + FIELD
PIECE = 41
WIDE = 21 * 128
LINE_ROWS = 48 + PIECE + 1
ZH = 64
PAD = 2 * ZH
CELLS = 256
OFFSETS = [(a, b) for a in (-1, 0, 1) for b in (-1, 0, 1)]


def call(kernel, out_shape, scratch=(), spaces={}, out_specs=None, limit=40 * 1024 * 1024, **extra):
    if out_specs is None:
        out_specs = jax.tree.map(lambda _: pl.BlockSpec(memory_space=pltpu.VMEM), out_shape)

    def run(*args):
        return pl.pallas_call(
            kernel,
            out_shape=out_shape,
            in_specs=[
                pl.BlockSpec(memory_space=spaces.get(n, pltpu.VMEM)) for n in range(len(args))
            ],
            out_specs=out_specs,
            scratch_shapes=list(scratch),
            compiler_params=pltpu.CompilerParams(vmem_limit_bytes=limit),
            **extra,
        )(*args)

    return run


def gelu_parts(value):
    normal_cdf = 0.5 * (1.0 + lax.erf(value * 0.7071067811865476))
    density = jnp.exp(-0.5 * value * value) * 0.3989422804014327
    return value * normal_cdf, normal_cdf + value * density


def pack_kernel(x_hbm, g_hbm, o_ref, in_ref, row_ref, sems):
    copies = [pltpu.make_async_copy(h, in_ref.at[n], sems.at[n]) for n, h in enumerate((x_hbm, g_hbm))]
    for copy in copies:
        copy.start()
    for copy in copies:
        copy.wait()
    fields = [in_ref[n].astype(F32) for n in (0, 1)]
    for j in range(16):
        pieces = [f[k * 8 : k * 8 + 8, j * C : (j + 1) * C] for f in fields for k in (0, 1)]
        wide = jnp.concatenate(pieces, axis=1)
        for t in range(6):
            row_ref[pl.ds(j * 48 + t, 8, stride=6), :] = wide[:, t * 128 : t * 128 + 128]
    for j in range(16):
        o_ref[j * 48 : j * 48 + 48, :] = row_ref[j * 48 : j * 48 + 48, :].astype(BF16)


def put_taps(tap_ref, slot, field, step):
    row = lax.broadcasted_iota(jnp.int32, (CELLS, C), 0)
    zl_of, x_of, yh_of = (row // 16) % 4, (row % 8) // 2, row % 2

    def ahead(value, rows):
        return pltpu.roll(value, (-rows) % CELLS, 0)

    more = step * ZH
    for a in (-1, 0, 1):
        moved = field
        if a != 0:
            inside = (zl_of + a >= 0) & (zl_of + a < 4)
            if step == 2:
                moved = jnp.where(inside, ahead(field, 16 * a), 0.0)
            else:
                crossed = jnp.where(inside, ahead(field, 15 * a), 0.0)
                moved = jnp.where(yh_of == (0 if a == 1 else 1), ahead(field, a), crossed)
        before = jnp.where(x_of > 0, ahead(moved, -2), 0.0)[CELLS - more :]
        after = jnp.where(x_of < 3, ahead(moved, 2), 0.0)[:more]
        tap_ref[slot, a + 1, PAD - more : PAD, :] = before.astype(BF16)
        tap_ref[slot, a + 1, PAD : PAD + CELLS, :] = moved.astype(BF16)
        tap_ref[slot, a + 1, PAD + CELLS : PAD + CELLS + more, :] = after.astype(BF16)


def get_tap(tap_ref, slot, a, b, step):
    start = PAD + ZH * b * step
    return tap_ref[slot, a + 1, start : start + CELLS, :]


def forward(tap_ref, slot, w_ref, step):
    total = None
    for t, (a, b) in enumerate(OFFSETS):
        term = jnp.dot(
            get_tap(tap_ref, slot, a, b, step), w_ref[t * C : (t + 1) * C, :], preferred_element_type=F32
        )
        total = term if total is None else total + term
    return total


def backward(tap_ref, slot, w_ref, step):
    total = None
    for t, (a, b) in enumerate(OFFSETS):
        term = lax.dot_general(
            get_tap(tap_ref, slot, -a, -b, step),
            w_ref[t * C : (t + 1) * C, :],
            (((1,), (1,)), ((), ())),
            preferred_element_type=F32,
        )
        total = term if total is None else total + term
    return total


def unpack(row_ref, f):
    tiles = [row_ref[pl.ds(3 * f + t, 128, stride=6), :] for t in range(3)]
    part = jnp.concatenate(tiles, axis=1)
    both = [part[:, k * C : (k + 1) * C].reshape(16, 1, 8, C) for k in (0, 1)]
    return jnp.concatenate(both, axis=1).reshape(CELLS, C)


def main_kernel(r_ref, w1_ref, w2_ref, keep_ref, send_ref, mid_ref, row_ref, tap_ref, pair_ref):
    row_ref[...] = r_ref[...].astype(F32)
    x = unpack(row_ref, 0)
    g = unpack(row_ref, 1)
    act_one = gelu_parts(x)[0].astype(BF16).astype(F32)
    put_taps(tap_ref, 0, act_one, 1)
    put_taps(tap_ref, 1, g, 2)
    hidden = (x + forward(tap_ref, 0, w1_ref, 1)).astype(BF16)
    gelu_two, slope_two = gelu_parts(hidden.astype(F32))
    act_two = gelu_two.astype(BF16).astype(F32)
    hidden_grad = (g + backward(tap_ref, 1, w2_ref, 2) * slope_two).astype(BF16)
    mid_ref[0] = hidden
    mid_ref[1] = hidden_grad
    hidden_grad = hidden_grad.astype(F32)
    for index, (act, grad) in enumerate(((act_two, g), (act_one, hidden_grad))):
        pair_ref[index, 0] = act[:, 0:128].astype(BF16)
        pair_ref[index, 1] = jnp.concatenate([act[:, 128:C], grad[:, 128:C]], axis=1).astype(BF16)
        pair_ref[index, 2] = grad[:, 0:128].astype(BF16)
    core = lax.axis_index("core")
    keep_ref[...] = pair_ref[core]
    send_ref[...] = pair_ref[1 - core]


def field_kernel(r_ref, w1_ref, w2_ref, mid_ref, o_ref, row_ref, tap_ref):
    def pack(value):
        split = value.reshape(16, 2, 8, C)
        return jnp.concatenate([split[:, k].reshape(128, C) for k in (0, 1)], axis=1)

    row_ref[...] = r_ref[...].astype(F32)
    hidden, hidden_grad = mid_ref[0].astype(F32), mid_ref[1].astype(F32)
    put_taps(tap_ref, 1, hidden_grad, 1)
    back_one = backward(tap_ref, 1, w1_ref, 1)
    slope_one = gelu_parts(unpack(row_ref, 0))[1]
    act_two = gelu_parts(hidden)[0].astype(BF16).astype(F32)
    put_taps(tap_ref, 0, act_two, 2)
    output = hidden + forward(tap_ref, 0, w2_ref, 2)
    input_grad = hidden_grad + back_one * slope_one
    wide = jnp.concatenate([pack(output), pack(input_grad)], axis=1)
    for t in range(6):
        row_ref[t * 128 : t * 128 + 128, :] = wide[:, t * 128 : t * 128 + 128]
    for e in range(8):
        tiles = [row_ref[pl.ds(t * 128 + e, 16, stride=8), :] for t in range(6)]
        o_ref[e * FIELD : (e + 1) * FIELD, :] = jnp.concatenate(tiles, axis=0).astype(BF16)


def half_kernel(own, pair_ref, *refs):
    o_ref, tap_ref, ft_ref = refs[-4:-1] if not own else refs[-3:]
    if not own:
        for c in range(16):
            piece = refs[1][(c // 2) * FIELD : (c // 2 + 1) * FIELD, :].astype(F32)
            refs[-1][c * BOTH + TERMS : (c + 1) * BOTH, :] = piece
    first, mixed, last = [pair_ref[n].astype(F32) for n in range(3)]
    turned = jnp.concatenate([first, mixed[:, 0:64]], axis=1).T
    grad = jnp.concatenate([last, mixed[:, 64:128]], axis=1)
    for n in (0, 1):
        ft_ref[n] = turned[:, n * 128 : n * 128 + 128]
    left = jnp.concatenate(
        [
            jnp.concatenate([ft_ref[n, pl.ds(2 * u + odd, 16, stride=12), :] for n in (0, 1)], axis=1)
            for odd in (0, 1)
            for u in range(6)
        ],
        axis=0,
    ).astype(BF16)

    def weight_grad(step):
        put_taps(tap_ref, 0, grad, step)
        for t, (a, b) in enumerate(OFFSETS):
            full = jnp.dot(left, get_tap(tap_ref, 0, -a, -b, step), preferred_element_type=F32)
            if own:
                o_ref[t] = full
                continue
            full = full + refs[0][t]
            even, odd = full[0:96], full[96:192]
            lanes = (
                even[:, 0:128],
                jnp.concatenate([even[:, 128:192], odd[:, 0:64]], axis=1),
                odd[:, 64:192],
            )
            wg_ref = refs[-1]
            for q in range(3):
                for u in range(6):
                    wg_ref[pl.ds(t * 18 + u * 3 + q, 16, stride=BOTH), :] = lanes[q][
                        u * 16 : u * 16 + 16
                    ]

    for core, step in ((0, 2), (1, 1)):
        pl.when(lax.axis_index("core") == core)(lambda step=step: weight_grad(step))
    if not own:
        o_ref[...] = refs[-1][0 : 16 * BOTH, :].astype(BF16)


def line_kernel(s_ref, out_ref, part_ref, sum_ref, row_ref):
    part_ref[0 : 16 * BOTH, :] = s_ref[...].astype(F32)
    total = part_ref[0:ROWS, :]
    for c in range(1, 16):
        total = total + part_ref[c * BOTH : c * BOTH + ROWS, :]
    sum_ref[0:ROWS, :] = total
    sum_ref[ROWS : ROWS + 16, :] = jnp.zeros((16, 128), F32)
    for zl in range(4):
        piece = sum_ref[zl * PIECE : zl * PIECE + PIECE + 1, :]
        for zh in range(4):
            start = (zh * 4 + zl) * LINE_ROWS + 48
            row_ref[start : start + PIECE + 1, :] = piece
    for half in (0, 1):

        @pl.when(lax.axis_index("yl") == half)
        def _():
            for z in range(16):
                for t in range(6):
                    first = half * BOTH + TERMS + t * 16 + z
                    row_ref[z * LINE_ROWS + t * 8 : z * LINE_ROWS + t * 8 + 8, :] = part_ref[
                        pl.ds(first, 8, stride=2 * BOTH), :
                    ]

    out_ref[...] = row_ref[0 : 16 * LINE_ROWS, :].astype(BF16)


def sum_kernel(r_ref, z_ref, row_ref):
    row_ref[0 : 16 * LINE_ROWS, :] = r_ref[...].astype(F32)
    row_ref[16 * LINE_ROWS :, :] = jnp.zeros((16, 128), F32)
    total = row_ref[48:96, :]
    for z in range(1, 16):
        total = total + row_ref[z * LINE_ROWS + 48 : z * LINE_ROWS + 96, :]
    mine = (total * (1.0 / 256.0)).astype(BF16)
    for z in range(4):
        z_ref[z] = mine


def tile_kernel(r_ref, out_ref, ig_ref, row_ref):
    row_ref[...] = r_ref[...].astype(F32)
    for f, ref in enumerate((out_ref, ig_ref)):
        halves = []
        for k in (0, 1):
            parts = []
            for z in range(16):
                tiles = [
                    row_ref[z * LINE_ROWS + (3 * f + t) * 8 : z * LINE_ROWS + (3 * f + t) * 8 + 8, :]
                    for t in (k, k + 1)
                ]
                both = jnp.concatenate(tiles, axis=1)
                parts.append(both[:, k * 64 : k * 64 + C])
            halves.append(jnp.concatenate(parts, axis=1))
        ref[...] = jnp.concatenate(halves, axis=0).astype(BF16)


def spread_kernel(z_ref, out_ref, row_ref):
    for z in range(4):
        row_ref[z * PIECE : z * PIECE + 48, :] = z_ref[z].astype(F32)
    tiles = [row_ref[pl.ds(v, 8, stride=18), :] for v in range(18)]
    tiles += [row_ref[v : v + 8, :] for v in (144, 152, 160)]
    mine = jnp.concatenate(tiles, axis=1).astype(BF16)
    for c in range(16):
        out_ref[c] = mine


def final_kernel(own, r_ref, *refs):
    one_ref, two_ref, out_ref, sems = refs[-4:]

    def each_copy(part, act):
        lanes = pl.ds(part * 9216, 9216)
        for core in (0, 1):
            target = two_ref if (core == 0) == own else one_ref

            @pl.when(lax.axis_index("core") == core)
            def _(target=target):
                act(
                    pltpu.make_async_copy(
                        out_ref.at[:, lanes], target.at[:, lanes], sems.at[part]
                    )
                )

    for c in range(16):
        lanes = c * 2304
        out_ref[0:8, lanes : lanes + 2304] = r_ref[c, :, 0:2304]
        last = r_ref[c, :, 2304:WIDE].astype(F32)
        for v in range(18):
            row = last[v % 8 : v % 8 + 1, v // 8 * 128 : v // 8 * 128 + 128]
            out_ref[8:9, lanes + v * 128 : lanes + v * 128 + 128] = row.astype(BF16)
        if c % 4 == 3:
            each_copy(c // 4, lambda copy: copy.start())
    for part in range(4):
        each_copy(part, lambda copy: copy.wait())


def exchange(value, axes):
    return lax.all_to_all(value, axes, split_axis=0, concat_axis=0, tiled=True)


def shape(*dims, dtype=BF16):
    return jax.ShapeDtypeStruct(dims, dtype)


def per_device(inputs, first_weight, second_weight, cotangent):
    hbm, vmem = pltpu.HBM, pltpu.VMEM
    swap = [(0, 1), (1, 0)]
    short = pl.CostEstimate(flops=10**9, bytes_accessed=3 * 10**6, transcendentals=0)
    kernel_one = first_weight.reshape(9 * C, C)
    kernel_two = second_weight.reshape(9 * C, C)
    packed = call(
        pack_kernel,
        shape(768, 128),
        scratch=(
            vmem((2, 16, 16 * C), BF16),
            vmem((768, 128), F32),
            pltpu.SemaphoreType.DMA((2,)),
        ),
        spaces={0: hbm, 1: hbm},
        limit=63400000,
    )(inputs, cotangent)
    received = exchange(packed.reshape(384, 2, 128), PEERS).reshape(768, 128)
    taps = vmem((2, 3, CELLS + 2 * PAD, C), BF16)
    keep, send, middle = call(
        main_kernel,
        (shape(3, CELLS, 128), shape(3, CELLS, 128), shape(2, CELLS, C)),
        scratch=(vmem((768, 128), F32), taps, vmem((2, 3, CELLS, 128), BF16)),
    )(received, kernel_one, kernel_two)
    other = lax.ppermute(send, "core", swap)
    scratch = (vmem((1, 3, CELLS + 2 * PAD, C), BF16), vmem((2, C, 128), F32))
    begun = call(
        functools.partial(half_kernel, True),
        shape(9, C, C, dtype=F32),
        scratch=scratch,
        cost_estimate=short,
    )(keep)
    fields = call(
        field_kernel,
        shape(8 * FIELD, 128),
        scratch=(vmem((768, 128), F32), taps),
        cost_estimate=short,
    )(received, kernel_one, kernel_two, middle)
    terms = call(
        functools.partial(half_kernel, False),
        shape(16 * BOTH, 128),
        scratch=(*scratch, vmem((16 * BOTH + 8, 128), F32)),
    )(other, begun, fields)
    plane = exchange(terms.reshape(8 * BOTH, 2, 128), PLANE).reshape(16 * BOTH, 128)
    lines = call(
        line_kernel,
        shape(16 * LINE_ROWS, 128),
        scratch=(
            vmem((16 * BOTH + 8, 128), F32),
            vmem((ROWS + 16, 128), F32),
            vmem((16 * LINE_ROWS + 8, 128), F32),
        ),
    )(plane)
    back = exchange(lines.reshape(8 * LINE_ROWS, 2, 128), LINE).reshape(16 * LINE_ROWS, 128)
    mine = call(sum_kernel, shape(4, 48, 128), scratch=(vmem((16 * LINE_ROWS + 16, 128), F32),))(back)
    line = exchange(mine, "zl")
    spread = call(
        spread_kernel, shape(16, 8, WIDE), scratch=(vmem((3 * PIECE + 61, 128), F32),)
    )(line)
    gathered = exchange(spread, PLANE)
    partner = lax.ppermute(gathered, "core", swap)
    output, input_grad = call(
        tile_kernel,
        (shape(16, 16 * C), shape(16, 16 * C)),
        scratch=(vmem((16 * LINE_ROWS, 128), F32),),
        cost_estimate=short,
    )(back)
    weight = shape(9, C * C)
    anywhere = pl.BlockSpec(memory_space=pl.ANY)
    scratch = (vmem((9, C * C), BF16), pltpu.SemaphoreType.DMA((4,)))
    one, two = call(
        functools.partial(final_kernel, True),
        (weight, weight),
        scratch=scratch,
        out_specs=(anywhere, anywhere),
        cost_estimate=short,
    )(gathered)
    one, two = call(
        functools.partial(final_kernel, False),
        (weight, weight),
        scratch=scratch,
        spaces={1: pl.ANY, 2: pl.ANY},
        out_specs=(anywhere, anywhere),
        input_output_aliases={1: 0, 2: 1},
    )(partner, one, two)
    return output, input_grad, one, two


def solution(mesh):
    grid = Mesh(mesh.devices.reshape(SIZES), AXES)
    tile = P(("zl", "yh", "yl"), ("x", "zh", "core"))
    return jax.shard_map(
        per_device,
        mesh=grid,
        in_specs=(tile, P(), P(), tile),
        out_specs=(tile, tile, P(), P()),
        check_vma=False,
    )
```
